128 devices in a mesh: grp: 32 (over x, y_lo, z), sp: 4 (over y_hi, core).
Axes of the slice: x: 4, y: 4 (y_hi: 2, y_lo: 2; y = y_hi * 2 + y_lo), z: 4, core: 2. Of those that a mesh axis runs over, the one named last changes fastest.
Arguments:
- tokens: bfloat16 [65536, 1280], P(('grp', 'sp')), may hold values from -6 to 6
- w_query: bfloat16 [1280, 640], replicated, may hold values from -4 to 4
- w_key: bfloat16 [1280, 640], replicated, may hold values from -4 to 4
- w_value: bfloat16 [1280, 640], replicated, may hold values from -0.15625 to 0.15625
- w_out: bfloat16 [640, 1280], replicated, may hold values from -0.25 to 0.25
- w_neck: bfloat16 [1280, 256], replicated, may hold values from -0.15625 to 0.15625
- owner_table: int32 [128, 128], P(('grp', 'sp')), may hold values from 0 to 127, each once within a row
- student_in: bfloat16 [65536, 512], P(('grp', 'sp')), may hold values from -24 to 24
- w_expand: bfloat16 [512, 2048], replicated, may hold values from -0.25 to 0.25
- w_project: bfloat16 [2048, 256], replicated, may hold values from -0.125 to 0.125
Outputs:
- student_error: bfloat16 [65536, 256], P(('grp', 'sp'))
- grad_expand: float32 [512, 2048], P(('grp', 'sp'))
- grad_project: float32 [2048, 256], P(('grp', 'sp'))
The draws below stay inside these ranges and needn't reach their ends.
Inputs may be any that keep to these rules, and one draw needn't show every extreme that they name: `owner_table`: each row is a permutation.
All inputs are finite; a program needn't handle non-finite values.
Results may differ from the reference program's by a relative error of at most 0.008.
The reference program's roundings to bfloat16 on the way count: a program that leaves them out, or rounds other values in their place, can miss the bound.
Values may be sent and summed in bfloat16 or wider, within the bound.
No kernel may reach another device: no remote copies, remote signals or barrier semaphores. Data moves between devices by JAX's collectives and lax.ppermute only.
A program may use at most 128 MiB of HBM per device.

```python
import jax
import jax.numpy as jnp
from jax import lax

D = 1280
HEADS_W = 8
HEAD = 80
TGT = 256
C_S = 512
HID = 2048
IMG_TOK = 2048
TOK_DEV = 512
TOKENS = 65536
PIECE = 4
N_GRP = 32
DEVICES = 128


def shared_base(key):
    return jnp.clip(jax.random.normal(key, (D, HEADS_W * HEAD), jnp.float32), -6.0, 6.0) * (2.5 / D ** 0.5)


def draw_w_query(key, part):
    base = shared_base(key)
    return jnp.clip(base, -4.0, 4.0).astype(jnp.bfloat16)


def draw_w_key(key, part):
    key = jax.random.fold_in(key, 7)
    noise_key = jax.random.fold_in(key, 0)
    noise = jnp.clip(jax.random.normal(noise_key, (D, HEADS_W * HEAD), jnp.float32), -6.0, 6.0) * (2.5 / D ** 0.5)
    value = noise
    return jnp.clip(value, -4.0, 4.0).astype(jnp.bfloat16)


def spiked(values, stream_key, source, target, blocks, factor):
    owner, partner = [(jnp.arange(values.shape[dim]) // (values.shape[dim] // blocks)).reshape([-1 if axis == dim else 1 for axis in range(values.ndim)]) for dim in (source, target)]
    chosen = jax.random.permutation(stream_key, blocks)[partner]
    strong = (owner == chosen) | (owner == (partner + blocks // 2) % blocks)
    return jnp.where(strong, factor * values, values)


def block_levels(own_key, extent, cuts, low, top_value):
    def one(dim, parts):
        steps = jax.random.uniform(jax.random.fold_in(jax.random.fold_in(own_key, 6), dim), (parts,), jnp.float32, low / len(cuts), top_value / len(cuts))
        return jnp.repeat(jnp.exp(steps), extent[dim] // parts).reshape((-1,) + (1,) * (len(extent) - dim - 1))

    loudness = one(*cuts[0])
    for cut in cuts[1:]:
        loudness = loudness * one(*cut)
    return loudness


def normal_values(key, extent, width, most, cuts=(), dtype=jnp.bfloat16):
    values = width * jax.random.normal(key, extent, jnp.float32)
    if cuts:
        values = values * block_levels(key, extent, cuts, -0.22, 0.18)
    return jnp.clip(values, -most, most).astype(dtype)


def noise_with(stream_key, shape, scale, most, pieces, heavy, dtype=jnp.bfloat16):
    entries = scale * jax.random.normal(stream_key, shape, jnp.float32)
    if pieces:
        entries = entries * block_levels(stream_key, shape, pieces, -0.22, 0.18)
    return jnp.clip(spiked(entries, jax.random.fold_in(stream_key, 3), *heavy), -most, most).astype(dtype)


def setup_inputs(seed: int = 0) -> dict:
    arg_keys = jax.random.split(jax.random.key(seed), 11)
    return {
        "tokens": normal_values(arg_keys[0], (TOKENS, D), 1.0, 6.0, ((0, 128),)),
        "w_query": draw_w_query(jax.random.fold_in(arg_keys[10], 71), 0),
        "w_key": draw_w_key(jax.random.fold_in(arg_keys[10], 71), 0),
        "w_value": normal_values(arg_keys[3], (D, HEADS_W * HEAD), D ** -0.5, 0.15625),
        "w_out": normal_values(arg_keys[4], (HEADS_W * HEAD, D), (HEADS_W * HEAD) ** -0.5, 0.25),
        "w_neck": normal_values(arg_keys[5], (D, TGT), D ** -0.5, 0.15625),
        "owner_table": jax.vmap(lambda own: jax.random.permutation(own, DEVICES))(jax.random.split(arg_keys[6], DEVICES)).reshape((DEVICES, DEVICES)).astype(jnp.int32),
        "student_in": noise_with(arg_keys[7], (TOKENS, C_S), 1.0, 24.0, ((0, 128),), (0, 1, 128, 5.5)),
        "w_expand": normal_values(arg_keys[8], (C_S, HID), C_S ** -0.5, 0.25),
        "w_project": normal_values(arg_keys[9], (HID, TGT), HID ** -0.5, 0.125),
    }


def layer_norm(value):
    centred = value - lax.optimization_barrier(jnp.mean(value, axis=-1, keepdims=True))
    spread = lax.optimization_barrier(jnp.mean(centred * centred, axis=-1, keepdims=True))
    return centred * lax.rsqrt(spread + 1e-06)

def attend(query, keys, values):
    count = query.shape[1] // HEAD

    def split(array):
        return array.reshape(array.shape[0], count, HEAD).transpose(1, 0, 2)

    def one_head(operands):
        q_head, k_head, v_head = operands
        scores = jnp.dot(q_head, k_head.T, preferred_element_type=jnp.float32) * HEAD ** (-0.5)
        top = lax.optimization_barrier(jnp.max(scores, axis=1, keepdims=True))
        weights = jnp.exp(scores - top)
        total = lax.optimization_barrier(jnp.sum(weights, axis=1, keepdims=True))
        mixed = jnp.dot(weights.astype(jnp.bfloat16), v_head, preferred_element_type=jnp.float32)
        return mixed / total
    result = lax.map(one_head, (split(query), split(keys), split(values)))
    return result.transpose(1, 0, 2).reshape(query.shape[0], count * HEAD).astype(jnp.bfloat16)

def reference(tokens, w_query, w_key, w_value, w_out, w_neck, owner_table, student_in, w_expand, w_project):

    def teacher(image):
        normed = layer_norm(image.astype(jnp.float32)).astype(jnp.bfloat16)
        query = jnp.dot(normed, w_query, preferred_element_type=jnp.float32).astype(jnp.bfloat16)
        keys = jnp.dot(normed, w_key, preferred_element_type=jnp.float32).astype(jnp.bfloat16)
        values = jnp.dot(normed, w_value, preferred_element_type=jnp.float32).astype(jnp.bfloat16)
        attended = attend(query, keys, values)
        block_out = (image.astype(jnp.float32) + jnp.dot(attended, w_out, preferred_element_type=jnp.float32)).astype(jnp.bfloat16)
        return layer_norm(jnp.dot(block_out, w_neck, preferred_element_type=jnp.float32)).astype(jnp.bfloat16)
    target = lax.map(teacher, tokens.reshape(N_GRP, IMG_TOK, D))
    blocks = target.reshape(DEVICES, DEVICES, PIECE, TGT)
    inverse = jnp.argsort(owner_table, axis=1).astype(jnp.int32)
    sent = jnp.take_along_axis(blocks, inverse[:, :, None, None], axis=1)
    moved = sent.transpose(1, 0, 2, 3).reshape(DEVICES, TOK_DEV, TGT)

    def student(carry, operands):
        grad_e, grad_p = carry
        rows_in, rows_target = operands
        pre = jnp.dot(rows_in, w_expand, preferred_element_type=jnp.float32)
        act_float, pull = jax.vjp(lambda v: jax.nn.gelu(v, approximate=True), pre)
        act = act_float.astype(jnp.bfloat16)
        error = jnp.dot(act, w_project, preferred_element_type=jnp.float32) - rows_target.astype(jnp.float32)
        d_pred = (error / TOK_DEV).astype(jnp.bfloat16)
        d_act = jnp.dot(d_pred, w_project.T, preferred_element_type=jnp.float32)
        d_pre = pull(d_act)[0].astype(jnp.bfloat16)
        grad_p = grad_p + jnp.dot(act.T, d_pred, preferred_element_type=jnp.float32)
        grad_e = grad_e + jnp.dot(rows_in.T, d_pre, preferred_element_type=jnp.float32)
        return ((grad_e, grad_p), error.astype(jnp.bfloat16))
    start = (jnp.zeros((C_S, HID), jnp.float32), jnp.zeros((HID, TGT), jnp.float32))
    (grad_expand, grad_project), errors = lax.scan(student, start, (student_in.reshape(DEVICES, TOK_DEV, C_S), moved))
    return (errors.reshape(TOKENS, TGT), grad_expand, grad_project)
```

```python
import jax
import jax.numpy as jnp
import numpy as np
from jax import lax
from jax.sharding import Mesh
from jax.sharding import PartitionSpec as P

HEADS_W = 8
HEAD = 80
AXES = ("x", "yl", "z", "yh", "c")
Y = ("yl", "yh")
Y_INDEX = (0, 2, 1, 3)


def layer_norm(value):
    centred = value - jnp.mean(value, axis=-1, keepdims=True)
    spread = jnp.mean(centred * centred, axis=-1, keepdims=True)
    return centred * lax.rsqrt(spread + 1e-06)


def split_heads(array):
    count = array.shape[1] // HEAD
    return array.reshape(array.shape[0], count, HEAD).transpose(1, 0, 2)


def hop(value, axis, shift, size):
    name = Y_INDEX if axis == Y else range(size)
    return lax.ppermute(value, axis, [(name[i], name[(i + shift) % size]) for i in range(size)])


def gather_rows(value):
    far = hop(value, "yh", 1, 2)
    near = hop(value, "c", 1, 2)
    far_near = hop(far, "c", 1, 2)
    return jnp.concatenate([value, near, far, far_near], axis=0)


def axis_step(part, axis, place):
    rows = part.shape[0] // 4
    total = lax.dynamic_slice_in_dim(part, place * rows, rows, 0)
    for shift in (2, 1, 3):
        chunk = lax.dynamic_slice_in_dim(part, ((place + shift) % 4) * rows, rows, 0)
        got = hop(chunk.astype(jnp.bfloat16), axis, shift, 4)
        total = total + got.astype(jnp.float32)
    return total


def core_step(part, place):
    rows = part.shape[0] // 2
    keep = lax.dynamic_slice_in_dim(part, place * rows, rows, 0)
    send = lax.dynamic_slice_in_dim(part, (1 - place) * rows, rows, 0)
    return keep + hop(send.astype(jnp.bfloat16), "c", 1, 2).astype(jnp.float32)


def row_order(order, unit):
    index = np.arange(128 * unit).reshape(4, 2, 4, 2, 2, unit)
    place = {"x": (0,), "y": (3, 1), "z": (2,)}
    axes = (4,) + sum((place[a] for a in order), ()) + (5,)
    return index.transpose(axes).reshape(-1)


def one_hot(order):
    eye = np.zeros((512, 512), np.float32)
    eye[order, np.arange(512)] = 1
    return jnp.asarray(eye, jnp.bfloat16)


def per_device(
    tokens, w_query, w_key, w_value, w_out, w_neck, owner_table, student_in, w_expand, w_project
):
    rows = tokens.shape[0]
    place = {"x": lax.axis_index("x"), "y": lax.axis_index("yh") * 2 + lax.axis_index("yl"), "z": lax.axis_index("z")}
    axis = {"x": "x", "y": Y, "z": "z"}
    normed = layer_norm(tokens.astype(jnp.float32)).astype(jnp.bfloat16)
    keys = jnp.dot(normed, w_key, preferred_element_type=jnp.float32).astype(jnp.bfloat16)
    values = jnp.dot(normed, w_value, preferred_element_type=jnp.float32).astype(jnp.bfloat16)
    query = jnp.dot(normed, w_query, preferred_element_type=jnp.float32).astype(jnp.bfloat16)
    query_heads = split_heads(query)
    key_heads = split_heads(gather_rows(keys))
    value_heads = split_heads(gather_rows(values))

    def one_head(operands):
        q_head, k_head, v_head = operands
        scores = jnp.dot(q_head, k_head.T, preferred_element_type=jnp.float32) * HEAD ** (-0.5)
        top = jnp.max(scores, axis=1, keepdims=True)
        weights = jnp.exp(scores - top)
        total = jnp.sum(weights, axis=1, keepdims=True)
        mixed = jnp.dot(
            weights.astype(jnp.bfloat16), v_head, preferred_element_type=jnp.float32
        )
        return (mixed / total).astype(jnp.bfloat16)

    attended = lax.map(one_head, (query_heads, key_heads, value_heads))
    attended = attended.transpose(1, 0, 2).reshape(rows, HEADS_W * HEAD)
    block_out = (
        tokens.astype(jnp.float32) + jnp.dot(attended, w_out, preferred_element_type=jnp.float32)
    ).astype(jnp.bfloat16)
    target = layer_norm(jnp.dot(block_out, w_neck, preferred_element_type=jnp.float32)).astype(
        jnp.bfloat16
    )
    peers = 128
    blocks = target.reshape(peers, rows // peers, target.shape[1])
    order = jnp.argsort(owner_table[0])
    outgoing = jnp.take(blocks, order, axis=0)
    arrived = lax.all_to_all(outgoing, AXES, split_axis=0, concat_axis=0, tiled=True)
    moved = arrived.reshape(rows, target.shape[1])
    pre = jnp.dot(student_in, w_expand, preferred_element_type=jnp.float32)
    act_float, pull = jax.vjp(lambda v: jax.nn.gelu(v, approximate=True), pre)
    act = act_float.astype(jnp.bfloat16)
    error = jnp.dot(act, w_project, preferred_element_type=jnp.float32) - moved.astype(jnp.float32)
    d_pred = (error / rows).astype(jnp.bfloat16)
    d_act = jnp.dot(d_pred, w_project.T, preferred_element_type=jnp.float32)
    d_pre = pull(d_act)[0].astype(jnp.bfloat16)

    def permuted(order):
        return jnp.dot(
            student_in, one_hot(row_order(order, 4)), preferred_element_type=jnp.float32
        ).astype(jnp.bfloat16)

    half = d_pre.shape[1] // 2
    left = jnp.dot(permuted("xyz").T, d_pre[:, :half], preferred_element_type=jnp.float32)
    right = jnp.dot(permuted("yzx").T, d_pre[:, half:], preferred_element_type=jnp.float32)
    project = jnp.dot(act.T, d_pred, preferred_element_type=jnp.float32)
    project = (
        project.reshape(4, 2, 4, 2, 2, 16, 256).transpose(4, 2, 0, 3, 1, 5, 6).reshape(2048, 256)
    )
    core = lax.axis_index("c")
    parts = {"xyz": left, "yzx": right, "zxy": project}
    parts = {order: core_step(part, core) for order, part in parts.items()}
    for step in range(3):
        parts = {
            order: axis_step(part, axis[order[step]], place[order[step]])
            for order, part in parts.items()
        }
    grad_expand = jnp.concatenate([parts["xyz"], parts["yzx"]], axis=1)
    return (error.astype(jnp.bfloat16), grad_expand, parts["zxy"])


def solution(mesh):
    fine = Mesh(mesh.devices.reshape(4, 2, 4, 2, 2), AXES)
    rows = P(AXES, None)
    return jax.shard_map(
        per_device,
        mesh=fine,
        in_specs=(rows, P(), P(), P(), P(), P(), rows, rows, P(), P()),
        out_specs=(rows, rows, rows),
        check_vma=False,
    )
```

```python
import functools

import jax
import jax.numpy as jnp
from jax import lax
from jax.experimental import pallas as pl
from jax.experimental.pallas import tpu as pltpu
from jax.sharding import Mesh
from jax.sharding import PartitionSpec as P

HEAD = 80
HALF = 320
SCALE = HEAD**-0.5 * 1.4426950408889634
AXES = ("x", "yl", "z", "yh", "c")
CHIPS = ("x", "yl", "z", "yh")
GELU_A = 0.7978845608028654
GELU_B = 0.044715
F32 = jnp.float32
BF16 = jnp.bfloat16
MIB = 2**20


def dot(a, b):
    return jnp.dot(a, b, preferred_element_type=F32)


def dot_t(a, b):
    return lax.dot_general(a, b, (((1,), (1,)), ((), ())), preferred_element_type=F32)


def layer_norm(value):
    centred = value - jnp.mean(value, axis=-1, keepdims=True)
    spread = jnp.mean(centred * centred, axis=-1, keepdims=True)
    return centred * lax.rsqrt(spread + 1e-06)


def lanes(width, low, high):
    index = lax.broadcasted_iota(jnp.int32, (1, width), 1)
    return (index >= low) & (index < high)


def shape(*dims, dtype=BF16):
    return jax.ShapeDtypeStruct(dims, dtype)


def params(mib):
    return pltpu.CompilerParams(vmem_limit_bytes=mib * MIB)


def cost(flops, moved, exps=0):
    return pl.CostEstimate(flops=flops, bytes_accessed=moved, transcendentals=exps)


def first_kernel(tokens_ref, w_key_ref, w_value_ref, normed_ref, kv_ref):
    normed = layer_norm(tokens_ref[...].astype(F32)).astype(BF16)
    normed_ref[...] = normed
    keys = dot(normed, w_key_ref[:, :384])
    values = dot(normed, w_value_ref[:, :384])
    kv_ref[...] = jnp.concatenate([keys[:, :HALF], values[:, :HALF]], axis=1).astype(BF16)


def first_project(tokens, w_key, w_value):
    return pl.pallas_call(
        first_kernel,
        out_shape=(shape(512, 1280), shape(512, 640)),
        compiler_params=params(24),
        cost_estimate=cost(2 * 512 * 1280 * 768, 6 * MIB),
        name="norm_kv_first",
    )(tokens, w_key, w_value)


def second_kernel(normed_ref, w_key_ref, w_value_ref, w_query_ref, kv_ref, q0_ref, q1_ref):
    normed = normed_ref[...]
    keys = dot(normed, w_key_ref[:, 256:])
    values = dot(normed, w_value_ref[:, 256:])
    kv_ref[...] = jnp.concatenate([keys[:, 64:], values[:, 64:]], axis=1).astype(BF16)
    query = dot(normed, w_query_ref[...])
    blank = jnp.zeros((512, 64), F32)
    q0_ref[...] = jnp.concatenate([query[:, :HALF], blank], axis=1).astype(BF16)
    q1_ref[...] = jnp.concatenate([query[:, HALF:], blank], axis=1).astype(BF16)


def second_project(normed, w_key, w_value, w_query):
    return pl.pallas_call(
        second_kernel,
        out_shape=(shape(512, 640), shape(512, 384), shape(512, 384)),
        compiler_params=params(24),
        cost_estimate=cost(2 * 512 * 1280 * 1408, 8 * MIB),
        name="kv_second_query",
    )(normed, w_key, w_value, w_query)


def attention_kernel(q_ref, kv0_ref, kv1_ref, kv2_ref, kv3_ref, out_ref):
    sources = (kv0_ref, kv1_ref, kv2_ref, kv3_ref)
    mixed = []
    for head in range(4):
        key_at = 0 if head < 3 else 128
        value_at = 256 if head < 2 else 384
        own = lanes(256, HEAD * head - key_at, HEAD * head - key_at + HEAD)
        query = q_ref[:, key_at : key_at + 256] * own.astype(F32).astype(BF16)
        scores = [dot_t(query, kv[:, key_at : key_at + 256]) for kv in sources]
        top = functools.reduce(
            jnp.maximum, [jnp.max(part, axis=1, keepdims=True) for part in scores]
        )
        probs = [jnp.exp2((part - top) * SCALE) for part in scores]
        total = sum(jnp.sum(part, axis=1, keepdims=True) for part in probs)
        weighed = sum(
            dot(part.astype(BF16), kv[:, value_at : value_at + 256])
            for part, kv in zip(probs, sources)
        )
        mixed.append(weighed / total)
    low = jnp.where(
        lanes(256, 144, 256), mixed[1], jnp.where(lanes(256, 64, 144), mixed[0], 0.0)
    )
    high = jnp.where(lanes(256, 176, 256), mixed[3], mixed[2])
    middle = jnp.where(lanes(128, 0, 96), low[:, 128:], high[:, :128])
    out_ref[...] = jnp.concatenate([low[:, :128], middle, high[:, 128:]], axis=1).astype(BF16)


def attention(query, sources):
    return pl.pallas_call(
        attention_kernel,
        out_shape=shape(512, 384),
        compiler_params=params(40),
        cost_estimate=cost(2 * 512 * 2048 * 512 * 4, 4 * MIB, 4 * 512 * 2048),
        name="attention_four_heads",
    )(query, *sources)


def target_kernel(place_ref, tokens_ref, att0_ref, att1_ref, w_out_ref, w_neck_ref, out_ref):
    first = jnp.concatenate([jnp.zeros((64, 1280), BF16), w_out_ref[:HALF, :]], axis=0)
    added = dot(att0_ref[...], first) + dot(att1_ref[...], w_out_ref[256:, :])
    block_out = (tokens_ref[...].astype(F32) + added).astype(BF16)
    target = layer_norm(dot(block_out, w_neck_ref[...])).astype(BF16)
    rows = lax.broadcasted_iota(jnp.int32, (512, 512), 0)
    pick = (rows == place_ref[...]).astype(F32).astype(BF16)
    out_ref[...] = dot(pick, target).astype(BF16)


def make_target(place, tokens, att0, att1, w_out, w_neck):
    return pl.pallas_call(
        target_kernel,
        out_shape=shape(512, 256),
        compiler_params=params(32),
        cost_estimate=cost(2 * 512 * 1280 * 1024, 6 * MIB),
        name="out_neck_target",
    )(place, tokens, att0, att1, w_out, w_neck)


def forward_kernel(
    core_ref, rows_ref, w_expand_ref, w_project_ref, pred_ref, slope_ref, act_t_ref, rows_t_ref
):
    step = pl.program_id(0)
    core = core_ref[0]
    rows = rows_ref[...]

    @pl.when(step == 0)
    def _():
        out_row = lax.broadcasted_iota(jnp.int32, (512, 512), 0)
        column = lax.broadcasted_iota(jnp.int32, (512, 512), 1)
        member = jnp.where(out_row < 256, core, 1 - core)
        wanted = (out_row % 256) // 4 * 8 + member * 4 + out_row % 4
        pick = (column == wanted).astype(F32).astype(BF16)
        rows_t_ref[...] = dot_t(pick, rows).astype(BF16)

    pre = dot(rows, w_expand_ref[...])
    square = pre * pre
    bend = jnp.tanh(GELU_A * pre * (1.0 + GELU_B * square))
    gate = 0.5 * (1.0 + bend)
    act = (pre * gate).astype(BF16)
    slope_ref[...] = gate + (0.5 * GELU_A) * pre * (1.0 - bend * bend) * (
        1.0 + (3.0 * GELU_B) * square
    )
    act_t = act.T
    for group in range(32):
        half = jnp.where(core == group % 2, 0, 1024)
        start = pl.multiple_of(half + (step * 16 + group // 2) * 16, 16)
        act_t_ref[pl.ds(start, 16), :] = act_t[group * 16 : group * 16 + 16, :]
    part = dot(act, w_project_ref[...])

    @pl.when(step == 0)
    def _():
        pred_ref[...] = part

    @pl.when(step > 0)
    def _():
        pred_ref[...] += part


def student_forward(core, rows, w_expand, w_project):
    whole = lambda i: (0, 0)
    return pl.pallas_call(
        forward_kernel,
        grid=(4,),
        in_specs=[
            pl.BlockSpec(memory_space=pltpu.SMEM),
            pl.BlockSpec((512, 512), whole),
            pl.BlockSpec((512, 512), lambda i: (0, i)),
            pl.BlockSpec((512, 256), lambda i: (i, 0)),
        ],
        out_specs=[
            pl.BlockSpec((512, 256), whole),
            pl.BlockSpec((512, 512), lambda i: (0, i)),
            pl.BlockSpec((2048, 512), whole),
            pl.BlockSpec((512, 512), whole),
        ],
        out_shape=(
            shape(512, 256, dtype=F32),
            shape(512, 2048, dtype=F32),
            shape(2048, 512),
            shape(512, 512),
        ),
        compiler_params=params(24),
        cost_estimate=cost(2 * 512 * 2048 * 768, 12 * MIB, 512 * 2048),
        name="student_forward",
    )(core, rows, w_expand, w_project)


def backward_kernel(
    pred_ref,
    moved_ref,
    slope_ref,
    w_project_ref,
    act_t_ref,
    rows_t_ref,
    error_ref,
    d_pred_ref,
    d_pre_ref,
    project_ref,
    expand_ref,
):
    @pl.when(pl.program_id(0) == 0)
    def _():
        error = pred_ref[...] - moved_ref[...].astype(F32)
        error_ref[...] = error.astype(BF16)
        d_pred_ref[...] = (error * (1.0 / 512.0)).astype(BF16)

    d_pred = d_pred_ref[...]
    d_pre = (slope_ref[...] * dot_t(d_pred, w_project_ref[...])).astype(BF16)
    d_pre_ref[...] = d_pre
    project_ref[...] = dot(act_t_ref[...], d_pred).astype(BF16)
    expand_ref[...] = dot(rows_t_ref[...], d_pre).astype(BF16)


def student_backward(pred, moved, slope, w_project, act_t, rows_t):
    whole = lambda i: (0, 0)
    return pl.pallas_call(
        backward_kernel,
        grid=(4,),
        in_specs=[
            pl.BlockSpec((512, 256), whole),
            pl.BlockSpec((512, 256), whole),
            pl.BlockSpec((512, 512), lambda i: (0, i)),
            pl.BlockSpec((512, 256), lambda i: (i, 0)),
            pl.BlockSpec((256, 512), lambda i: (4 + i, 0)),
            pl.BlockSpec((256, 512), lambda i: (1, 0)),
        ],
        out_specs=[
            pl.BlockSpec((512, 256), whole),
            pl.BlockSpec((512, 256), whole),
            pl.BlockSpec((512, 512), lambda i: (0, i)),
            pl.BlockSpec((256, 256), lambda i: (i, 0)),
            pl.BlockSpec((256, 512), lambda i: (0, i)),
        ],
        out_shape=(
            shape(512, 256),
            shape(512, 256),
            shape(512, 2048),
            shape(1024, 256),
            shape(256, 2048),
        ),
        compiler_params=params(24),
        cost_estimate=cost(2 * 512 * 2048 * 640, 10 * MIB),
        name="student_backward",
    )(pred, moved, slope, w_project, act_t, rows_t)


def own_kernel(d_pred_ref, d_pre_ref, act_t_ref, rows_t_ref, project_ref, expand_ref):
    project_ref[...] = dot(act_t_ref[...], d_pred_ref[...])
    expand_ref[...] = dot(rows_t_ref[...], d_pre_ref[...])


def own_half(d_pred, d_pre, act_t, rows_t):
    whole = lambda i: (0, 0)
    return pl.pallas_call(
        own_kernel,
        grid=(4,),
        in_specs=[
            pl.BlockSpec((512, 256), whole),
            pl.BlockSpec((512, 512), lambda i: (0, i)),
            pl.BlockSpec((256, 512), lambda i: (i, 0)),
            pl.BlockSpec((256, 512), whole),
        ],
        out_specs=[
            pl.BlockSpec((256, 256), lambda i: (i, 0)),
            pl.BlockSpec((256, 512), lambda i: (0, i)),
        ],
        out_shape=(shape(1024, 256, dtype=F32), shape(256, 2048, dtype=F32)),
        compiler_params=params(16),
        cost_estimate=cost(2 * 512 * 2048 * 384, 6 * MIB),
        name="own_half_gradients",
    )(d_pred, d_pre, act_t, rows_t)


def pack_kernel(project_ref, project_in_ref, expand_ref, expand_in_ref, out_ref):
    project = (project_ref[...] + project_in_ref[...].astype(F32)).astype(BF16)
    expand = (expand_ref[...] + expand_in_ref[...].astype(F32)).astype(BF16)
    stacked = jnp.concatenate([expand[:, 256 * j : 256 * j + 256] for j in range(8)], axis=0)
    row = lax.broadcasted_iota(jnp.int32, (256, 256), 0)
    column = lax.broadcasted_iota(jnp.int32, (256, 256), 1)
    wanted = row % 32 // 4 * 32 + row // 32 * 4 + row % 4
    sorted_rows = dot((column == wanted).astype(F32).astype(BF16), stacked).astype(BF16)
    for chip in range(8):
        out_ref[chip, :16, :] = project[16 * chip : 16 * chip + 16, :]
        out_ref[chip, 16:, :] = sorted_rows[32 * chip : 32 * chip + 32, :]


def pack(project, project_in, expand, expand_in):
    return pl.pallas_call(
        pack_kernel,
        grid=(8,),
        in_specs=[
            pl.BlockSpec((128, 256), lambda i: (i, 0)),
            pl.BlockSpec((128, 256), lambda i: (i, 0)),
            pl.BlockSpec((32, 2048), lambda i: (i, 0)),
            pl.BlockSpec((32, 2048), lambda i: (i, 0)),
        ],
        out_specs=pl.BlockSpec((8, 48, 256), lambda i: (i, 0, 0)),
        out_shape=shape(64, 48, 256),
        compiler_params=params(16),
        cost_estimate=cost(2 * 256 * 256 * 256 * 8, 6 * MIB),
        name="pack_gradients",
    )(project, project_in, expand, expand_in)


def finish_kernel(parts_ref, expand_ref, project_ref):
    total = jnp.sum(parts_ref[...].astype(F32), axis=0)
    project_ref[...] = total[:16, :]
    for j in range(8):
        expand_ref[:, 256 * j : 256 * j + 256] = total[16 + 4 * j : 20 + 4 * j, :]


def finish(parts):
    return pl.pallas_call(
        finish_kernel,
        out_shape=(shape(4, 2048, dtype=F32), shape(16, 256, dtype=F32)),
        compiler_params=params(16),
        cost_estimate=cost(64 * 48 * 256, 2 * MIB),
        name="sum_gradients",
    )(parts)


def swap(value, axis):
    return lax.ppermute(value, axis, [(0, 1), (1, 0)])


def per_device(
    tokens, w_query, w_key, w_value, w_out, w_neck, owner_table, student_in, w_expand, w_project
):
    core = lax.axis_index("c").astype(jnp.int32).reshape(1)
    normed, kv_first = first_project(tokens, w_key, w_value)
    far_first = swap(kv_first, "yh")
    near_first = swap(kv_first, "c")
    kv_second, query_first, query_second = second_project(normed, w_key, w_value, w_query)
    far_second = swap(kv_second, "yh")
    near_second = swap(kv_second, "c")
    pred, slope, act_t, rows_t = student_forward(core, student_in, w_expand, w_project)
    att_first = attention(
        query_first, (kv_first, near_first, far_first, swap(far_first, "c"))
    )
    att_second = attention(
        query_second, (kv_second, near_second, far_second, swap(far_second, "c"))
    )
    place = (owner_table.reshape(128, 1) * 4 + jnp.arange(4, dtype=jnp.int32)).reshape(1, 512)
    target = make_target(place, tokens, att_first, att_second, w_out, w_neck)
    moved = lax.all_to_all(
        target.reshape(128, 4, 256), AXES, split_axis=0, concat_axis=0, tiled=True
    ).reshape(512, 256)
    error, d_pred, d_pre, project_out, expand_out = student_backward(
        pred, moved, slope, w_project, act_t, rows_t
    )
    project_in = swap(project_out, "c")
    expand_in = swap(expand_out, "c")
    project, expand = own_half(d_pred, d_pre, act_t, rows_t)
    packed = pack(project, project_in, expand, expand_in)
    parts = lax.all_to_all(packed, CHIPS, split_axis=0, concat_axis=0, tiled=True)
    grad_expand, grad_project = finish(parts)
    return (error, grad_expand, grad_project)


def solution(mesh):
    fine = Mesh(mesh.devices.reshape(4, 2, 4, 2, 2), AXES)
    rows = P(AXES, None)
    return jax.shard_map(
        per_device,
        mesh=fine,
        in_specs=(rows, P(), P(), P(), P(), P(), rows, rows, P(), P()),
        out_specs=(rows, rows, rows),
        check_vma=False,
    )
```

```python
import functools

import jax
import jax.numpy as jnp
from jax import lax
from jax.experimental import pallas as pl
from jax.experimental.pallas import tpu as pltpu
from jax.sharding import Mesh
from jax.sharding import PartitionSpec as P

HEAD = 80
HALF = 320
SCALE = HEAD**-0.5 * 1.4426950408889634
AXES = ("x", "yl", "z", "yh", "c")
CHIPS = ("x", "yl", "z", "yh")
GELU_A = 0.7978845608028654
GELU_B = 0.044715
F32 = jnp.float32
TOKEN = jax.ShapeDtypeStruct((8, 128), jnp.float32)
BF16 = jnp.bfloat16
MIB = 2**20


def dot(a, b):
    return jnp.dot(a, b, preferred_element_type=F32)


def dot_t(a, b):
    return lax.dot_general(a, b, (((1,), (1,)), ((), ())), preferred_element_type=F32)


def layer_norm(value):
    centred = value - jnp.mean(value, axis=-1, keepdims=True)
    spread = jnp.mean(centred * centred, axis=-1, keepdims=True)
    return centred * lax.rsqrt(spread + 1e-06)


def lanes(width, low, high):
    index = lax.broadcasted_iota(jnp.int32, (1, width), 1)
    return (index >= low) & (index < high)


def shape(*dims, dtype=BF16):
    return jax.ShapeDtypeStruct(dims, dtype)


def kept(*dims, dtype=BF16):
    return pltpu.VMEM(dims, dtype)


def in_hbm(value):
    return pltpu.with_memory_space_constraint(value, pltpu.HBM)


def params(mib=16):
    return pltpu.CompilerParams(vmem_limit_bytes=mib * MIB)


def cost(flops, moved, exps=0):
    return pl.CostEstimate(flops=flops, bytes_accessed=moved, transcendentals=exps)


def first_kernel(
    tokens_hbm, w_key_hbm, w_value_hbm, normed_ref, kv_ref, tokens_ref, w_key_ref, w_value_ref, sems
):
    copies = []
    for i in range(4):
        rows = pl.ds(128 * i, 128)
        copies.append((tokens_hbm.at[rows], tokens_ref.at[rows]))
    for source, target in ((w_key_hbm, w_key_ref), (w_value_hbm, w_value_ref)):
        for i in range(2):
            rows = pl.ds(640 * i, 640)
            copies.append((source.at[rows, pl.ds(0, 384)], target.at[rows]))
    copies = [
        pltpu.make_async_copy(source, target, sems.at[i])
        for i, (source, target) in enumerate(copies)
    ]
    for copy in copies:
        copy.start()
    for i in range(4):
        copies[i].wait()
        rows = pl.ds(128 * i, 128)
        normed_ref[rows, :] = layer_norm(tokens_ref[rows, :].astype(F32)).astype(BF16)
    for copy in copies[4:]:
        copy.wait()
    normed = normed_ref[...]
    keys = dot(normed, w_key_ref[...])
    values = dot(normed, w_value_ref[...])
    kv_ref[...] = jnp.concatenate([keys[:, :HALF], values[:, :HALF]], axis=1).astype(BF16)


def first_project(tokens, w_key, w_value):
    return pl.pallas_call(
        first_kernel,
        in_specs=[pl.BlockSpec(memory_space=pltpu.HBM)] * 3,
        out_shape=(kept(512, 1280), shape(512, 640)),
        scratch_shapes=[
            pltpu.VMEM((512, 1280), BF16),
            pltpu.VMEM((1280, 384), BF16),
            pltpu.VMEM((1280, 384), BF16),
            pltpu.SemaphoreType.DMA((8,)),
        ],
        compiler_params=params(),
        cost_estimate=cost(2 * 512 * 1280 * 768, 6 * MIB),
        name="norm_kv_first",
    )(tokens, w_key, w_value)


def second_kernel(
    normed_ref, w_key_ref, w_value_ref, w_query_ref, after_ref, kv_ref, q0_ref, q1_ref, token_ref
):
    token_ref[...] = after_ref[...]
    normed = normed_ref[...]
    keys = dot(normed, w_key_ref[:, 256:])
    values = dot(normed, w_value_ref[:, 256:])
    kv_ref[...] = jnp.concatenate([keys[:, 64:], values[:, 64:]], axis=1).astype(BF16)
    query = dot(normed, w_query_ref[...])
    blank = jnp.zeros((512, 64), F32)
    q0_ref[...] = jnp.concatenate([query[:, :HALF], blank], axis=1).astype(BF16)
    q1_ref[...] = jnp.concatenate([query[:, HALF:], blank], axis=1).astype(BF16)


def second_project(normed, w_key, w_value, w_query, after):
    return pl.pallas_call(
        second_kernel,
        in_specs=[pl.BlockSpec(memory_space=pltpu.VMEM)] * 5,
        out_shape=(shape(512, 640), kept(512, 384), kept(512, 384), TOKEN),
        compiler_params=params(),
        cost_estimate=cost(1000, 1000),
        name="kv_second_query",
    )(normed, w_key, w_value, w_query, after)


def masked_query(q_ref, head):
    key_at = 0 if head < 3 else 128
    low = HEAD * head - key_at
    return q_ref[:, key_at : key_at + 256] * lanes(256, low, low + HEAD).astype(F32).astype(BF16)


def wide(value, times):
    return jnp.concatenate([value] * times, axis=1)


def attend(q_ref, sources, head, floor=None):
    key_at = 0 if head < 3 else 128
    value_at = 256 if head < 2 else 384
    query = masked_query(q_ref, head)
    scores = [dot_t(query, kv[:, key_at : key_at + 256]) for kv in sources]
    top = jnp.max(functools.reduce(jnp.maximum, scores), axis=1, keepdims=True)
    if floor is not None:
        top = jnp.maximum(jnp.broadcast_to(top, floor.shape), floor)
    shift = top if floor is None else wide(top, 4)
    probs = [jnp.exp2((part - shift) * SCALE) for part in scores]
    total = jnp.sum(functools.reduce(jnp.add, probs), axis=1, keepdims=True)
    weighed = sum(
        dot(part.astype(BF16), kv[:, value_at : value_at + 256])
        for part, kv in zip(probs, sources)
    )
    return top, total, weighed


def side_by_side(mixed):
    low = jnp.where(
        lanes(256, 144, 256), mixed[1], jnp.where(lanes(256, 64, 144), mixed[0], 0.0)
    )
    high = jnp.where(lanes(256, 176, 256), mixed[3], mixed[2])
    middle = jnp.where(lanes(128, 0, 96), low[:, 128:], high[:, :128])
    return jnp.concatenate([low[:, :128], middle, high[:, 128:]], axis=1)


def attention_kernel(q_ref, kv0_ref, kv1_ref, kv2_ref, kv3_ref, after_ref, out_ref, token_ref):
    token_ref[...] = after_ref[...]
    sources = (kv0_ref, kv1_ref, kv2_ref, kv3_ref)
    mixed = []
    for head in range(4):
        _, total, weighed = attend(q_ref, sources, head)
        mixed.append(weighed / total)
    out_ref[...] = side_by_side(mixed).astype(BF16)


def attention(query, sources, after):
    return pl.pallas_call(
        attention_kernel,
        in_specs=[pl.BlockSpec(memory_space=pltpu.VMEM)] * 6,
        out_shape=(kept(512, 384), TOKEN),
        compiler_params=params(),
        cost_estimate=cost(2 * 512 * 2048 * 512 * 4, 4 * MIB, 4 * 512 * 2048),
        name="attention_four_heads",
    )(query, *sources, after)


def near_kernel(q_ref, kv0_ref, kv1_ref, after_ref, mixed_ref, stats_ref, token_ref):
    token_ref[...] = after_ref[...]
    mixed = []
    for head in range(4):
        top, total, weighed = attend(q_ref, (kv0_ref, kv1_ref), head)
        mixed.append(weighed)
        stats_ref[head] = jnp.broadcast_to(top, (512, 128))
        stats_ref[4 + head] = jnp.broadcast_to(total, (512, 128))
    mixed_ref[...] = side_by_side(mixed)


def near_attention(query, sources, after):
    return pl.pallas_call(
        near_kernel,
        in_specs=[pl.BlockSpec(memory_space=pltpu.VMEM)] * 4,
        out_shape=(kept(512, 384, dtype=F32), kept(8, 512, 128, dtype=F32), TOKEN),
        compiler_params=params(),
        cost_estimate=cost(512 * 2048 * 512 * 4, 4 * MIB, 2 * 512 * 2048),
        name="attention_near_keys",
    )(query, *sources, after)


def far_kernel(q_ref, kv0_ref, kv1_ref, near_ref, stats_ref, out_ref):
    mixed = []
    for head in range(4):
        at = 0 if head < 2 else 128
        near_top = stats_ref[head]
        top, total, weighed = attend(q_ref, (kv0_ref, kv1_ref), head, near_top)
        factor = jnp.exp2((near_top - top) * SCALE)
        share = 1.0 / (total + factor * stats_ref[4 + head])
        near = wide(factor * share, 2) * near_ref[:, at : at + 256]
        mixed.append(wide(share, 2) * weighed + near)
    out_ref[...] = side_by_side(mixed).astype(BF16)


def far_attention(query, sources, near, stats):
    return pl.pallas_call(
        far_kernel,
        in_specs=[pl.BlockSpec(memory_space=pltpu.VMEM)] * 5,
        out_shape=kept(512, 384),
        compiler_params=params(),
        cost_estimate=cost(512 * 2048 * 512 * 4, 4 * MIB, 2 * 512 * 2048),
        name="attention_far_keys",
    )(query, *sources, near, stats)


def target_kernel(owner_ref, tokens_ref, att0_ref, att1_ref, w_out_ref, w_neck_ref, out_ref):
    first = jnp.concatenate([jnp.zeros((64, 1280), BF16), w_out_ref[:HALF, :]], axis=0)
    added = dot(att0_ref[...], first) + dot(att1_ref[...], w_out_ref[256:, :])
    block_out = (tokens_ref[...].astype(F32) + added).astype(BF16)
    target = layer_norm(dot(block_out, w_neck_ref[...])).astype(BF16)
    block = lax.broadcasted_iota(jnp.int32, (128, 512), 0)
    source = lax.broadcasted_iota(jnp.int32, (128, 512), 1)
    spread = (source // 4 == block).astype(F32).astype(BF16)
    owner = jnp.broadcast_to(owner_ref[...].astype(F32), (8, 128)).astype(BF16)
    owner = dot(owner, spread)[:1, :].astype(jnp.int32)
    row = lax.broadcasted_iota(jnp.int32, (512, 512), 0)
    place = owner * 4 + lax.broadcasted_iota(jnp.int32, (1, 512), 1) % 4
    pick = (row == place).astype(F32).astype(BF16)
    out_ref[...] = dot(pick, target).reshape(128, 4, 256).astype(BF16)


def make_target(owner_table, tokens, att0, att1, w_out, w_neck):
    return pl.pallas_call(
        target_kernel,
        out_shape=shape(128, 4, 256),
        compiler_params=params(),
        cost_estimate=cost(2 * 512 * 1280 * 1024, 6 * MIB),
        name="out_neck_target",
    )(owner_table, tokens, att0, att1, w_out, w_neck)


def forward_kernel(
    core_ref, rows_ref, w_expand_ref, w_project_ref, pred_ref, slope_ref, act_t_ref, rows_t_ref, token_ref
):
    token_ref[...] = jnp.zeros((8, 128), F32)
    step = pl.program_id(0)
    core = core_ref[0]
    rows = rows_ref[...]

    @pl.when(step == 0)
    def _():
        out_row = lax.broadcasted_iota(jnp.int32, (512, 512), 0)
        column = lax.broadcasted_iota(jnp.int32, (512, 512), 1)
        member = jnp.where(out_row < 256, core, 1 - core)
        wanted = (out_row % 256) // 4 * 8 + member * 4 + out_row % 4
        pick = (column == wanted).astype(F32).astype(BF16)
        rows_t_ref[...] = dot_t(pick, rows).astype(BF16)

    pre = dot(rows, w_expand_ref[...])
    square = pre * pre
    bend = jnp.tanh(GELU_A * pre * (1.0 + GELU_B * square))
    gate = 0.5 * (1.0 + bend)
    act = (pre * gate).astype(BF16)
    slope_ref[...] = gate + (0.5 * GELU_A) * pre * (1.0 - bend * bend) * (
        1.0 + (3.0 * GELU_B) * square
    )
    act_t = act.T
    for group in range(32):
        half = jnp.where(core == group % 2, 0, 1024)
        start = pl.multiple_of(half + (step * 16 + group // 2) * 16, 16)
        act_t_ref[pl.ds(start, 16), :] = act_t[group * 16 : group * 16 + 16, :]
    part = dot(act, w_project_ref[...])

    @pl.when(step == 0)
    def _():
        pred_ref[...] = part

    @pl.when(step > 0)
    def _():
        pred_ref[...] += part


def student_forward(core, rows, w_expand, w_project):
    whole = lambda i: (0, 0)
    return pl.pallas_call(
        forward_kernel,
        grid=(4,),
        in_specs=[
            pl.BlockSpec(memory_space=pltpu.SMEM),
            pl.BlockSpec((512, 512), whole),
            pl.BlockSpec((512, 512), lambda i: (0, i)),
            pl.BlockSpec((512, 256), lambda i: (i, 0)),
        ],
        out_specs=[
            pl.BlockSpec((512, 256), whole),
            pl.BlockSpec((512, 512), lambda i: (0, i)),
            pl.BlockSpec((2048, 512), whole),
            pl.BlockSpec((512, 512), whole),
            pl.BlockSpec((8, 128), whole),
        ],
        out_shape=(
            kept(512, 256, dtype=F32),
            kept(512, 2048, dtype=F32),
            kept(2048, 512),
            kept(512, 512),
            TOKEN,
        ),
        compiler_params=params(),
        cost_estimate=cost(1000, 1000),
        name="student_forward",
    )(core, rows, w_expand, w_project)


def backward_kernel(
    pred_ref,
    moved_ref,
    slope_ref,
    w_project_ref,
    act_t_ref,
    rows_t_ref,
    error_ref,
    d_pred_ref,
    d_pre_ref,
    project_ref,
    expand_ref,
):
    @pl.when(pl.program_id(0) == 0)
    def _():
        error = pred_ref[...] - moved_ref[...].astype(F32).reshape(512, 256)
        error_ref[...] = error.astype(BF16)
        d_pred_ref[...] = (error * (1.0 / 512.0)).astype(BF16)

    d_pred = d_pred_ref[...]
    d_pre = (slope_ref[...] * dot_t(d_pred, w_project_ref[...])).astype(BF16)
    d_pre_ref[...] = d_pre
    project_ref[...] = dot(act_t_ref[...], d_pred).astype(BF16)
    expand_ref[...] = dot(rows_t_ref[...], d_pre).astype(BF16)


def student_backward(pred, moved, slope, w_project, act_t, rows_t):
    whole = lambda i: (0, 0)
    return pl.pallas_call(
        backward_kernel,
        grid=(4,),
        in_specs=[
            pl.BlockSpec((512, 256), whole),
            pl.BlockSpec((128, 4, 256), lambda i: (0, 0, 0)),
            pl.BlockSpec((512, 512), lambda i: (0, i)),
            pl.BlockSpec((512, 256), lambda i: (i, 0)),
            pl.BlockSpec((256, 512), lambda i: (4 + i, 0)),
            pl.BlockSpec((256, 512), lambda i: (1, 0)),
        ],
        out_specs=[
            pl.BlockSpec((512, 256), whole),
            pl.BlockSpec((512, 256), whole),
            pl.BlockSpec((512, 512), lambda i: (0, i)),
            pl.BlockSpec((256, 256), lambda i: (i, 0)),
            pl.BlockSpec((256, 512), lambda i: (0, i)),
        ],
        out_shape=(
            shape(512, 256),
            kept(512, 256),
            kept(512, 2048),
            shape(1024, 256),
            shape(256, 2048),
        ),
        compiler_params=params(),
        cost_estimate=cost(2 * 512 * 2048 * 640, 10 * MIB),
        name="student_backward",
    )(pred, moved, slope, w_project, act_t, rows_t)


def own_kernel(d_pred_ref, d_pre_ref, act_t_ref, rows_t_ref, project_ref, expand_ref):
    project_ref[...] = dot(act_t_ref[...], d_pred_ref[...])
    expand_ref[...] = dot(rows_t_ref[...], d_pre_ref[...])


def own_half(d_pred, d_pre, act_t, rows_t):
    whole = lambda i: (0, 0)
    return pl.pallas_call(
        own_kernel,
        grid=(4,),
        in_specs=[
            pl.BlockSpec((512, 256), whole),
            pl.BlockSpec((512, 512), lambda i: (0, i)),
            pl.BlockSpec((256, 512), lambda i: (i, 0)),
            pl.BlockSpec((256, 512), whole),
        ],
        out_specs=[
            pl.BlockSpec((256, 256), lambda i: (i, 0)),
            pl.BlockSpec((256, 512), lambda i: (0, i)),
        ],
        out_shape=(kept(1024, 256, dtype=F32), kept(256, 2048, dtype=F32)),
        compiler_params=params(),
        cost_estimate=cost(2 * 512 * 2048 * 384, 6 * MIB),
        name="own_half_gradients",
    )(d_pred, d_pre, act_t, rows_t)


def pack_kernel(project_ref, project_in_ref, expand_ref, expand_in_ref, out_ref):
    project = (project_ref[...] + project_in_ref[...].astype(F32)).astype(BF16)
    expand = (expand_ref[...] + expand_in_ref[...].astype(F32)).astype(BF16)
    stacked = jnp.concatenate([expand[:, 256 * j : 256 * j + 256] for j in range(8)], axis=0)
    row = lax.broadcasted_iota(jnp.int32, (256, 256), 0)
    column = lax.broadcasted_iota(jnp.int32, (256, 256), 1)
    wanted = row % 32 // 4 * 32 + row // 32 * 4 + row % 4
    sorted_rows = dot((column == wanted).astype(F32).astype(BF16), stacked).astype(BF16)
    for chip in range(8):
        out_ref[chip, :16, :] = project[16 * chip : 16 * chip + 16, :]
        out_ref[chip, 16:, :] = sorted_rows[32 * chip : 32 * chip + 32, :]


def pack(project, project_in, expand, expand_in):
    return pl.pallas_call(
        pack_kernel,
        grid=(8,),
        in_specs=[
            pl.BlockSpec((128, 256), lambda i: (i, 0)),
            pl.BlockSpec((128, 256), lambda i: (i, 0)),
            pl.BlockSpec((32, 2048), lambda i: (i, 0)),
            pl.BlockSpec((32, 2048), lambda i: (i, 0)),
        ],
        out_specs=pl.BlockSpec((8, 48, 256), lambda i: (i, 0, 0)),
        out_shape=shape(64, 48, 256),
        compiler_params=params(),
        cost_estimate=cost(2 * 256 * 256 * 256 * 8, 6 * MIB),
        name="pack_gradients",
    )(project, project_in, expand, expand_in)


def finish_kernel(parts_ref, expand_ref, project_ref):
    total = jnp.sum(parts_ref[...].astype(F32), axis=0)
    project_ref[...] = total[:16, :]
    for j in range(8):
        expand_ref[:, 256 * j : 256 * j + 256] = total[16 + 4 * j : 20 + 4 * j, :]


def finish(parts):
    return pl.pallas_call(
        finish_kernel,
        out_shape=(shape(4, 2048, dtype=F32), shape(16, 256, dtype=F32)),
        compiler_params=params(),
        cost_estimate=cost(64 * 48 * 256, 2 * MIB),
        name="sum_gradients",
    )(parts)


def gate_kernel(value_ref, after_ref, out_ref):
    del value_ref, after_ref, out_ref


def gate(value, after):
    return pl.pallas_call(
        gate_kernel,
        in_specs=[pl.BlockSpec(memory_space=pl.ANY)] * 2,
        out_specs=pl.BlockSpec(memory_space=pl.ANY),
        out_shape=jax.ShapeDtypeStruct(value.shape, value.dtype),
        input_output_aliases={0: 0},
        compiler_params=params(1),
        cost_estimate=cost(10, 10),
        name="gate",
    )(value, after)


def swap(value, axis):
    return lax.ppermute(value, axis, [(0, 1), (1, 0)])


def per_device(
    tokens, w_query, w_key, w_value, w_out, w_neck, owner_table, student_in, w_expand, w_project
):
    core = lax.axis_index("c").astype(jnp.int32).reshape(1)
    normed, kv_first = first_project(in_hbm(tokens), in_hbm(w_key), in_hbm(w_value))
    far_first = swap(kv_first, "yh")
    near_first = swap(kv_first, "c")
    pred, slope, act_t, rows_t, token = student_forward(
        core, in_hbm(student_in), in_hbm(w_expand), in_hbm(w_project)
    )
    kv_second, query_first, query_second, token = second_project(
        normed, in_hbm(w_key), in_hbm(w_value), in_hbm(w_query), token
    )
    far_second = swap(kv_second, "yh")
    near_second = swap(kv_second, "c")
    far_first = gate(far_first, token)
    near, stats, token = near_attention(query_second, (kv_second, near_second), token)
    att_first, token = attention(
        query_first, (kv_first, near_first, far_first, swap(far_first, "c")), token
    )
    far_second = gate(far_second, token)
    att_second = far_attention(query_second, (far_second, swap(far_second, "c")), near, stats)
    target = make_target(owner_table, tokens, att_first, att_second, w_out, w_neck)
    moved = lax.all_to_all(target, AXES, split_axis=0, concat_axis=0, tiled=True)
    error, d_pred, d_pre, project_out, expand_out = student_backward(
        pred, moved, slope, w_project, act_t, rows_t
    )
    project_in = swap(project_out, "c")
    expand_in = swap(expand_out, "c")
    project, expand = own_half(d_pred, d_pre, act_t, rows_t)
    packed = pack(project, project_in, expand, expand_in)
    parts = lax.all_to_all(packed, CHIPS, split_axis=0, concat_axis=0, tiled=True)
    grad_expand, grad_project = finish(parts)
    return (error, grad_expand, grad_project)


def solution(mesh):
    fine = Mesh(mesh.devices.reshape(4, 2, 4, 2, 2), AXES)
    rows = P(AXES, None)
    return jax.shard_map(
        per_device,
        mesh=fine,
        in_specs=(rows, P(), P(), P(), P(), P(), rows, rows, P(), P()),
        out_specs=(rows, rows, rows),
        check_vma=False,
    )
```

```python
import functools

import jax
import jax.numpy as jnp
from jax import lax
from jax.experimental import pallas as pl
from jax.experimental.pallas import tpu as pltpu
from jax.sharding import Mesh
from jax.sharding import PartitionSpec as P

HEAD = 80
HALF = 320
SCALE = HEAD**-0.5 * 1.4426950408889634
AXES = ("x", "yl", "z", "yh", "c")
CHIPS = ("x", "yl", "z", "yh")
GELU_A = 0.7978845608028654
GELU_B = 0.044715
F32 = jnp.float32
TOKEN = jax.ShapeDtypeStruct((8, 128), jnp.float32)
BF16 = jnp.bfloat16
MIB = 2**20


def dot(a, b):
    return jnp.dot(a, b, preferred_element_type=F32)


def dot_t(a, b):
    return lax.dot_general(a, b, (((1,), (1,)), ((), ())), preferred_element_type=F32)


def layer_norm(value):
    centred = value - jnp.mean(value, axis=-1, keepdims=True)
    spread = jnp.mean(centred * centred, axis=-1, keepdims=True)
    return centred * lax.rsqrt(spread + 1e-06)


def lanes(width, low, high):
    index = lax.broadcasted_iota(jnp.int32, (1, width), 1)
    return (index >= low) & (index < high)


def shape(*dims, dtype=BF16):
    return jax.ShapeDtypeStruct(dims, dtype)


def kept(*dims, dtype=BF16):
    return pltpu.VMEM(dims, dtype)


def in_hbm(value):
    return pltpu.with_memory_space_constraint(value, pltpu.HBM)


def params(mib=16):
    return pltpu.CompilerParams(vmem_limit_bytes=mib * MIB)


def cost(flops, moved, exps=0):
    return pl.CostEstimate(flops=flops, bytes_accessed=moved, transcendentals=exps)


def first_kernel(
    tokens_hbm, w_key_hbm, w_value_hbm, normed_ref, kv_ref, tokens_ref, w_key_ref, w_value_ref, sems
):
    copies = []
    for i in range(4):
        rows = pl.ds(128 * i, 128)
        copies.append((tokens_hbm.at[rows], tokens_ref.at[rows]))
    for source, target in ((w_key_hbm, w_key_ref), (w_value_hbm, w_value_ref)):
        for i in range(2):
            rows = pl.ds(640 * i, 640)
            copies.append((source.at[rows, pl.ds(0, 384)], target.at[rows]))
    copies = [
        pltpu.make_async_copy(source, target, sems.at[i])
        for i, (source, target) in enumerate(copies)
    ]
    for copy in copies:
        copy.start()
    for i in range(4):
        copies[i].wait()
        rows = pl.ds(128 * i, 128)
        normed_ref[rows, :] = layer_norm(tokens_ref[rows, :].astype(F32)).astype(BF16)
    for copy in copies[4:]:
        copy.wait()
    normed = normed_ref[...]
    keys = dot(normed, w_key_ref[...])
    values = dot(normed, w_value_ref[...])
    kv_ref[...] = jnp.concatenate([keys[:, :HALF], values[:, :HALF]], axis=1).astype(BF16)


def first_project(tokens, w_key, w_value):
    return pl.pallas_call(
        first_kernel,
        in_specs=[pl.BlockSpec(memory_space=pltpu.HBM)] * 3,
        out_shape=(kept(512, 1280), shape(512, 640)),
        scratch_shapes=[
            pltpu.VMEM((512, 1280), BF16),
            pltpu.VMEM((1280, 384), BF16),
            pltpu.VMEM((1280, 384), BF16),
            pltpu.SemaphoreType.DMA((8,)),
        ],
        compiler_params=params(),
        cost_estimate=cost(2 * 512 * 1280 * 768, 6 * MIB),
        name="norm_kv_first",
    )(tokens, w_key, w_value)


def second_kernel(
    normed_ref, w_key_ref, w_value_ref, w_query_ref, kv_ref, send_ref, q0_ref, q1_ref
):
    normed = normed_ref[...]
    keys = dot(normed, w_key_ref[:, 256:])
    values = dot(normed, w_value_ref[:, 256:])
    kv = jnp.concatenate([keys[:, 64:], values[:, 64:]], axis=1).astype(BF16)
    kv_ref[...] = kv
    send_ref[:512, :] = kv
    send_ref[512:, :] = jnp.zeros((16, 640), BF16)
    query = dot(normed, w_query_ref[...])
    blank = jnp.zeros((512, 64), F32)
    q0_ref[...] = jnp.concatenate([query[:, :HALF], blank], axis=1).astype(BF16)
    q1_ref[...] = jnp.concatenate([query[:, HALF:], blank], axis=1).astype(BF16)


def second_project(normed, w_key, w_value, w_query):
    return pl.pallas_call(
        second_kernel,
        in_specs=[pl.BlockSpec(memory_space=pltpu.VMEM)] * 4,
        out_shape=(shape(512, 640), shape(528, 640), kept(512, 384), kept(512, 384)),
        compiler_params=params(),
        cost_estimate=cost(1000, 1000),
        name="kv_second_query",
    )(normed, w_key, w_value, w_query)


def masked_query(q_ref, head):
    key_at = 0 if head < 3 else 128
    low = HEAD * head - key_at
    return q_ref[:, key_at : key_at + 256] * lanes(256, low, low + HEAD).astype(F32).astype(BF16)


def wide(value, times):
    return jnp.concatenate([value] * times, axis=1)


def attend(q_ref, sources, head, floor=None):
    key_at = 0 if head < 3 else 128
    value_at = 256 if head < 2 else 384
    query = masked_query(q_ref, head)
    scores = [dot_t(query, kv[:512, key_at : key_at + 256]) for kv in sources]
    top = jnp.max(functools.reduce(jnp.maximum, scores), axis=1, keepdims=True)
    if floor is not None:
        top = jnp.maximum(jnp.broadcast_to(top, floor.shape), floor)
    shift = top if floor is None else wide(top, 4)
    probs = [jnp.exp2((part - shift) * SCALE) for part in scores]
    total = jnp.sum(functools.reduce(jnp.add, probs), axis=1, keepdims=True)
    weighed = sum(
        dot(part.astype(BF16), kv[:512, value_at : value_at + 256])
        for part, kv in zip(probs, sources)
    )
    return top, total, weighed


def side_by_side(mixed):
    low = jnp.where(
        lanes(256, 144, 256), mixed[1], jnp.where(lanes(256, 64, 144), mixed[0], 0.0)
    )
    high = jnp.where(lanes(256, 176, 256), mixed[3], mixed[2])
    middle = jnp.where(lanes(128, 0, 96), low[:, 128:], high[:, :128])
    return jnp.concatenate([low[:, :128], middle, high[:, 128:]], axis=1)


def attention_kernel(q_ref, kv0_ref, kv1_ref, kv2_ref, kv3_ref, after_ref, out_ref, token_ref):
    token_ref[...] = after_ref[...]
    sources = (kv0_ref, kv1_ref, kv2_ref, kv3_ref)
    mixed = []
    for head in range(4):
        _, total, weighed = attend(q_ref, sources, head)
        mixed.append(weighed / total)
    out_ref[...] = side_by_side(mixed).astype(BF16)


def attention(query, sources, after):
    return pl.pallas_call(
        attention_kernel,
        in_specs=[pl.BlockSpec(memory_space=pltpu.VMEM)] * 6,
        out_shape=(kept(512, 384), TOKEN),
        compiler_params=params(17),
        cost_estimate=cost(1000, 1000),
        name="attention_four_heads",
    )(query, *sources, after)


def near_kernel(q_ref, kv0_ref, kv1_ref, mixed_ref, stats_ref, token_ref):
    token_ref[...] = jnp.zeros((8, 128), F32)
    mixed = []
    for head in range(4):
        top, total, weighed = attend(q_ref, (kv0_ref, kv1_ref), head)
        mixed.append(weighed)
        stats_ref[head] = jnp.broadcast_to(top, (512, 128))
        stats_ref[4 + head] = jnp.broadcast_to(total, (512, 128))
    mixed_ref[...] = side_by_side(mixed)


def near_attention(query, sources):
    return pl.pallas_call(
        near_kernel,
        out_shape=(kept(512, 384, dtype=F32), kept(8, 512, 128, dtype=F32), TOKEN),
        compiler_params=params(),
        cost_estimate=cost(1000, 1000),
        name="attention_near_keys",
    )(query, *sources)


def far_kernel(q_ref, kv0_ref, kv1_ref, near_ref, stats_ref, out_ref):
    mixed = []
    for head in range(4):
        at = 0 if head < 2 else 128
        near_top = stats_ref[head]
        top, total, weighed = attend(q_ref, (kv0_ref, kv1_ref), head, near_top)
        factor = jnp.exp2((near_top - top) * SCALE)
        share = 1.0 / (total + factor * stats_ref[4 + head])
        near = wide(factor * share, 2) * near_ref[:, at : at + 256]
        mixed.append(wide(share, 2) * weighed + near)
    out_ref[...] = side_by_side(mixed).astype(BF16)


def far_attention(query, sources, near, stats):
    return pl.pallas_call(
        far_kernel,
        in_specs=[pl.BlockSpec(memory_space=pltpu.VMEM)] * 5,
        out_shape=kept(512, 384),
        compiler_params=params(),
        cost_estimate=cost(512 * 2048 * 512 * 4, 4 * MIB, 2 * 512 * 2048),
        name="attention_far_keys",
    )(query, *sources, near, stats)


def target_kernel(owner_ref, tokens_ref, att0_ref, att1_ref, w_out_ref, w_neck_ref, out_ref):
    first = jnp.concatenate([jnp.zeros((64, 1280), BF16), w_out_ref[:HALF, :]], axis=0)
    added = dot(att0_ref[...], first) + dot(att1_ref[...], w_out_ref[256:, :])
    block_out = (tokens_ref[...].astype(F32) + added).astype(BF16)
    target = layer_norm(dot(block_out, w_neck_ref[...])).astype(BF16)
    block = lax.broadcasted_iota(jnp.int32, (128, 512), 0)
    source = lax.broadcasted_iota(jnp.int32, (128, 512), 1)
    spread = (source // 4 == block).astype(F32).astype(BF16)
    owner = jnp.broadcast_to(owner_ref[...].astype(F32), (8, 128)).astype(BF16)
    owner = dot(owner, spread)[:1, :].astype(jnp.int32)
    row = lax.broadcasted_iota(jnp.int32, (512, 512), 0)
    place = owner * 4 + lax.broadcasted_iota(jnp.int32, (1, 512), 1) % 4
    pick = (row == place).astype(F32).astype(BF16)
    out_ref[...] = dot(pick, target).reshape(128, 4, 256).astype(BF16)


def make_target(owner_table, tokens, att0, att1, w_out, w_neck):
    return pl.pallas_call(
        target_kernel,
        out_shape=shape(128, 4, 256),
        compiler_params=params(),
        cost_estimate=cost(2 * 512 * 1280 * 1024, 6 * MIB),
        name="out_neck_target",
    )(owner_table, tokens, att0, att1, w_out, w_neck)


def forward_kernel(
    core_ref, rows_ref, w_expand_ref, w_project_ref, pred_ref, slope_ref, act_t_ref, rows_t_ref, token_ref
):
    token_ref[...] = jnp.zeros((8, 128), F32)
    step = pl.program_id(0)
    core = core_ref[0]
    rows = rows_ref[...]

    @pl.when(step == 0)
    def _():
        out_row = lax.broadcasted_iota(jnp.int32, (512, 512), 0)
        column = lax.broadcasted_iota(jnp.int32, (512, 512), 1)
        member = jnp.where(out_row < 256, core, 1 - core)
        wanted = (out_row % 256) // 4 * 8 + member * 4 + out_row % 4
        pick = (column == wanted).astype(F32).astype(BF16)
        rows_t_ref[...] = dot_t(pick, rows).astype(BF16)

    pre = dot(rows, w_expand_ref[...])
    square = pre * pre
    bend = jnp.tanh(GELU_A * pre * (1.0 + GELU_B * square))
    gate = 0.5 * (1.0 + bend)
    act = (pre * gate).astype(BF16)
    slope_ref[...] = gate + (0.5 * GELU_A) * pre * (1.0 - bend * bend) * (
        1.0 + (3.0 * GELU_B) * square
    )
    act_t = act.T
    for group in range(32):
        half = jnp.where(core == group % 2, 0, 1024)
        start = pl.multiple_of(half + (step * 16 + group // 2) * 16, 16)
        act_t_ref[pl.ds(start, 16), :] = act_t[group * 16 : group * 16 + 16, :]
    part = dot(act, w_project_ref[...])

    @pl.when(step == 0)
    def _():
        pred_ref[...] = part

    @pl.when(step > 0)
    def _():
        pred_ref[...] += part


def student_forward(core, rows, w_expand, w_project):
    whole = lambda i: (0, 0)
    return pl.pallas_call(
        forward_kernel,
        grid=(4,),
        in_specs=[
            pl.BlockSpec(memory_space=pltpu.SMEM),
            pl.BlockSpec((512, 512), whole),
            pl.BlockSpec((512, 512), lambda i: (0, i)),
            pl.BlockSpec((512, 256), lambda i: (i, 0)),
        ],
        out_specs=[
            pl.BlockSpec((512, 256), whole),
            pl.BlockSpec((512, 512), lambda i: (0, i)),
            pl.BlockSpec((2048, 512), whole),
            pl.BlockSpec((512, 512), whole),
            pl.BlockSpec((8, 128), whole),
        ],
        out_shape=(
            kept(512, 256, dtype=F32),
            kept(512, 2048, dtype=F32),
            kept(2048, 512),
            kept(512, 512),
            TOKEN,
        ),
        compiler_params=params(),
        cost_estimate=cost(1000, 1000),
        name="student_forward",
    )(core, rows, w_expand, w_project)


def backward_kernel(
    pred_ref,
    moved_ref,
    slope_ref,
    w_project_ref,
    act_t_ref,
    rows_t_ref,
    error_ref,
    d_pred_ref,
    d_pre_ref,
    project_ref,
    expand_ref,
):
    error = pred_ref[...] - moved_ref[...].astype(F32).reshape(512, 256)
    error_ref[...] = error.astype(BF16)
    d_pred = (error * (1.0 / 512.0)).astype(BF16)
    d_pred_ref[...] = d_pred
    for i in range(4):
        part = slice(512 * i, 512 * i + 512)
        d_pre = (slope_ref[:, part] * dot_t(d_pred, w_project_ref[part, :])).astype(BF16)
        d_pre_ref[:, part] = d_pre
        expand_ref[:, part] = dot(rows_t_ref[256:, :], d_pre).astype(BF16)
    project_ref[...] = dot(act_t_ref[1024:, :], d_pred).astype(BF16)


def student_backward(pred, moved, slope, w_project, act_t, rows_t):
    return pl.pallas_call(
        backward_kernel,
        out_shape=(
            shape(512, 256),
            kept(512, 256),
            kept(512, 2048),
            shape(1024, 256),
            shape(256, 2048),
        ),
        compiler_params=params(),
        cost_estimate=cost(2 * 512 * 2048 * 640, 10 * MIB),
        name="student_backward",
    )(pred, moved, slope, w_project, act_t, rows_t)


def own_kernel(d_pred_ref, d_pre_ref, act_t_ref, rows_t_ref, project_ref, expand_ref):
    project_ref[...] = dot(act_t_ref[:1024, :], d_pred_ref[...])
    for i in range(4):
        part = slice(512 * i, 512 * i + 512)
        expand_ref[:, part] = dot(rows_t_ref[:256, :], d_pre_ref[:, part])


def own_half(d_pred, d_pre, act_t, rows_t):
    return pl.pallas_call(
        own_kernel,
        out_shape=(kept(1024, 256, dtype=F32), kept(256, 2048, dtype=F32)),
        compiler_params=params(),
        cost_estimate=cost(2 * 512 * 2048 * 384, 6 * MIB),
        name="own_half_gradients",
    )(d_pred, d_pre, act_t, rows_t)


def pack_kernel(project_ref, project_in_ref, expand_ref, expand_in_ref, out_ref):
    row = lax.broadcasted_iota(jnp.int32, (256, 256), 0)
    column = lax.broadcasted_iota(jnp.int32, (256, 256), 1)
    wanted = row % 32 // 4 * 32 + row // 32 * 4 + row % 4
    order = (column == wanted).astype(F32).astype(BF16)
    project = (project_ref[...] + project_in_ref[...].astype(F32)).astype(BF16)
    for block in range(8):
        part = slice(32 * block, 32 * block + 32)
        expand = (expand_ref[part, :] + expand_in_ref[part, :].astype(F32)).astype(BF16)
        stacked = jnp.concatenate([expand[:, 256 * j : 256 * j + 256] for j in range(8)], axis=0)
        sorted_rows = dot(order, stacked).astype(BF16)
        for i in range(8):
            chip = 8 * block + i
            out_ref[chip, :16, :] = project[16 * chip : 16 * chip + 16, :]
            out_ref[chip, 16:, :] = sorted_rows[32 * i : 32 * i + 32, :]


def pack(project, project_in, expand, expand_in):
    return pl.pallas_call(
        pack_kernel,
        out_shape=shape(64, 48, 256),
        compiler_params=params(),
        cost_estimate=cost(2 * 256 * 256 * 256 * 8, 6 * MIB),
        name="pack_gradients",
    )(project, project_in, expand, expand_in)


def finish_kernel(parts_ref, expand_ref, project_ref):
    total = jnp.sum(parts_ref[...].astype(F32), axis=0)
    project_ref[...] = total[:16, :]
    for j in range(8):
        expand_ref[:, 256 * j : 256 * j + 256] = total[16 + 4 * j : 20 + 4 * j, :]


def finish(parts):
    return pl.pallas_call(
        finish_kernel,
        out_shape=(shape(4, 2048, dtype=F32), shape(16, 256, dtype=F32)),
        compiler_params=params(),
        cost_estimate=cost(64 * 48 * 256, 2 * MIB),
        name="sum_gradients",
    )(parts)


def gate_kernel(*refs):
    refs[-1][...] = jnp.zeros((8, 128), F32)


def gate(value, *after, flops=10):
    return pl.pallas_call(
        gate_kernel,
        in_specs=[pl.BlockSpec(memory_space=pl.ANY)] * (1 + len(after)),
        out_specs=[
            pl.BlockSpec(memory_space=pl.ANY),
            pl.BlockSpec(memory_space=pltpu.VMEM),
        ],
        out_shape=(jax.ShapeDtypeStruct(value.shape, value.dtype), TOKEN),
        input_output_aliases={0: 0},
        compiler_params=params(1),
        cost_estimate=cost(flops, 10),
        name="gate",
    )(value, *after)


def swap(value, axis):
    return lax.ppermute(value, axis, [(0, 1), (1, 0)])


def per_device(
    tokens, w_query, w_key, w_value, w_out, w_neck, owner_table, student_in, w_expand, w_project
):
    core = lax.axis_index("c").astype(jnp.int32).reshape(1)
    normed, kv_first = first_project(in_hbm(tokens), in_hbm(w_key), in_hbm(w_value))
    far_first = swap(kv_first, "yh")
    near_first = swap(kv_first, "c")
    kv_second, kv_send, query_first, query_second = second_project(
        normed, in_hbm(w_key), in_hbm(w_value), in_hbm(w_query)
    )
    far_second = swap(kv_send, "yh")
    near_second = swap(kv_second, "c")
    pred, slope, act_t, rows_t, token = student_forward(
        core, in_hbm(student_in), in_hbm(w_expand), in_hbm(w_project)
    )
    far_first, _ = gate(far_first, token)
    near, stats, token = near_attention(query_second, (kv_second, near_second))
    att_first, token = attention(
        query_first, (kv_first, near_first, far_first, swap(far_first, "c")), token
    )
    far_second, token = gate(far_second, token)
    att_second = far_attention(query_second, (far_second, swap(far_second, "c")), near, stats)
    target = make_target(owner_table, tokens, att_first, att_second, w_out, w_neck)
    moved = lax.all_to_all(target, AXES, split_axis=0, concat_axis=0, tiled=True)
    error, d_pred, d_pre, project_out, expand_out = student_backward(
        pred, moved, slope, w_project, act_t, rows_t
    )
    project_in = swap(project_out, "c")
    expand_in = swap(expand_out, "c")
    project, expand = own_half(d_pred, d_pre, act_t, rows_t)
    packed = pack(project, project_in, expand, expand_in)
    parts = lax.all_to_all(packed, CHIPS, split_axis=0, concat_axis=0, tiled=True)
    grad_expand, grad_project = finish(parts)
    return (error, grad_expand, grad_project)


def solution(mesh):
    fine = Mesh(mesh.devices.reshape(4, 2, 4, 2, 2), AXES)
    rows = P(AXES, None)
    return jax.shard_map(
        per_device,
        mesh=fine,
        in_specs=(rows, P(), P(), P(), P(), P(), rows, rows, P(), P()),
        out_specs=(rows, rows, rows),
        check_vma=False,
    )
```

```python
import functools

import jax
import jax.numpy as jnp
from jax import lax
from jax.experimental import pallas as pl
from jax.experimental.pallas import tpu as pltpu
from jax.sharding import Mesh
from jax.sharding import PartitionSpec as P

HEAD = 80
HALF = 320
SCALE = HEAD**-0.5 * 1.4426950408889634
AXES = ("x", "yl", "z", "yh", "c")
CHIPS = ("x", "yl", "z", "yh")
GELU_A = 0.7978845608028654
GELU_B = 0.044715
F32 = jnp.float32
TOKEN = jax.ShapeDtypeStruct((8, 128), jnp.float32)
BF16 = jnp.bfloat16
MIB = 2**20


def dot(a, b):
    return jnp.dot(a, b, preferred_element_type=F32)


def dot_t(a, b):
    return lax.dot_general(a, b, (((1,), (1,)), ((), ())), preferred_element_type=F32)


def layer_norm(value):
    centred = value - jnp.mean(value, axis=-1, keepdims=True)
    spread = jnp.mean(centred * centred, axis=-1, keepdims=True)
    return centred * lax.rsqrt(spread + 1e-06)


def lanes(width, low, high):
    index = lax.broadcasted_iota(jnp.int32, (1, width), 1)
    return (index >= low) & (index < high)


def shape(*dims, dtype=BF16):
    return jax.ShapeDtypeStruct(dims, dtype)


def kept(*dims, dtype=BF16):
    return pltpu.VMEM(dims, dtype)


def in_hbm(value):
    return pltpu.with_memory_space_constraint(value, pltpu.HBM)


def params(mib=16):
    return pltpu.CompilerParams(vmem_limit_bytes=mib * MIB)


def cost(flops, moved, exps=0):
    return pl.CostEstimate(flops=flops, bytes_accessed=moved, transcendentals=exps)


def first_kernel(
    tokens_hbm,
    w_key_hbm,
    w_value_hbm,
    normed_ref,
    send_ref,
    tokens_ref,
    w_key_ref,
    w_value_ref,
    kv_ref,
    sems,
):
    copies = []
    for i in range(4):
        rows = pl.ds(128 * i, 128)
        copies.append((tokens_hbm.at[rows], tokens_ref.at[rows]))
    for source, target in ((w_key_hbm, w_key_ref), (w_value_hbm, w_value_ref)):
        for i in range(2):
            rows = pl.ds(640 * i, 640)
            copies.append((source.at[rows, pl.ds(0, 384)], target.at[rows]))
    copies = [
        pltpu.make_async_copy(source, target, sems.at[i])
        for i, (source, target) in enumerate(copies)
    ]
    for copy in copies:
        copy.start()
    for i in range(4):
        copies[i].wait()
        rows = pl.ds(128 * i, 128)
        normed_ref[rows, :] = layer_norm(tokens_ref[rows, :].astype(F32)).astype(BF16)
    for copy in copies[4:]:
        copy.wait()
    sends = []
    for i in range(2):
        rows = pl.ds(256 * i, 256)
        normed = normed_ref[rows, :]
        keys = dot(normed, w_key_ref[...])
        values = dot(normed, w_value_ref[...])
        kv = jnp.concatenate([keys[:, :HALF], values[:, :HALF]], axis=1).astype(BF16)
        kv_ref[rows, :] = kv
        sends.append(pltpu.make_async_copy(kv_ref.at[rows], send_ref.at[rows], sems.at[8 + i]))
        sends[-1].start()
    for send in sends:
        send.wait()


def first_project(tokens, w_key, w_value):
    return pl.pallas_call(
        first_kernel,
        in_specs=[pl.BlockSpec(memory_space=pltpu.HBM)] * 3,
        out_specs=[pl.BlockSpec(memory_space=pltpu.VMEM), pl.BlockSpec(memory_space=pl.ANY)],
        out_shape=(kept(512, 1280), shape(512, 640)),
        scratch_shapes=[
            pltpu.VMEM((512, 1280), BF16),
            pltpu.VMEM((1280, 384), BF16),
            pltpu.VMEM((1280, 384), BF16),
            pltpu.VMEM((512, 640), BF16),
            pltpu.SemaphoreType.DMA((10,)),
        ],
        compiler_params=params(),
        cost_estimate=cost(2 * 512 * 1280 * 768, 6 * MIB),
        name="norm_kv_first",
    )(tokens, w_key, w_value)


def second_kernel(
    normed_ref, w_key_ref, w_value_ref, w_query_ref, kv_ref, q0_ref, q1_ref, send_ref, sems
):
    normed = normed_ref[...]
    keys = dot(normed, w_key_ref[:, 256:])
    values = dot(normed, w_value_ref[:, 256:])
    kv_ref[...] = jnp.concatenate([keys[:, 64:], values[:, 64:]], axis=1).astype(BF16)
    sends = (
        pltpu.make_async_copy(kv_ref, send_ref.at[pl.ds(0, 512)], sems.at[0]),
        pltpu.make_async_copy(kv_ref.at[pl.ds(0, 16)], send_ref.at[pl.ds(512, 16)], sems.at[1]),
    )
    for send in sends:
        send.start()
    query = dot(normed, w_query_ref[...])
    blank = jnp.zeros((512, 64), F32)
    q0_ref[...] = jnp.concatenate([query[:, :HALF], blank], axis=1).astype(BF16)
    q1_ref[...] = jnp.concatenate([query[:, HALF:], blank], axis=1).astype(BF16)
    for send in sends:
        send.wait()


def second_project(normed, w_key, w_value, w_query):
    return pl.pallas_call(
        second_kernel,
        out_specs=[pl.BlockSpec(memory_space=pltpu.VMEM)] * 3 + [pl.BlockSpec(memory_space=pl.ANY)],
        out_shape=(kept(512, 640), kept(512, 384), kept(512, 384), shape(528, 640)),
        scratch_shapes=[pltpu.SemaphoreType.DMA((2,))],
        compiler_params=params(),
        cost_estimate=cost(1000, 1000),
        name="kv_second_query",
    )(normed, w_key, w_value, w_query)


def masked_query(q_ref, head):
    key_at = 0 if head < 3 else 128
    low = HEAD * head - key_at
    return q_ref[:, key_at : key_at + 256] * lanes(256, low, low + HEAD).astype(F32).astype(BF16)


def wide(value, times):
    return jnp.concatenate([value] * times, axis=1)


def attend(q_ref, sources, head, floor=None):
    key_at = 0 if head < 3 else 128
    value_at = 256 if head < 2 else 384
    query = masked_query(q_ref, head)
    scores = [dot_t(query, kv[:512, key_at : key_at + 256]) for kv in sources]
    top = jnp.max(functools.reduce(jnp.maximum, scores), axis=1, keepdims=True)
    if floor is not None:
        top = jnp.maximum(jnp.broadcast_to(top, floor.shape), floor)
    shift = top if floor is None else wide(top, 4)
    probs = [jnp.exp2((part - shift) * SCALE) for part in scores]
    total = jnp.sum(functools.reduce(jnp.add, probs), axis=1, keepdims=True)
    weighed = sum(
        dot(part.astype(BF16), kv[:512, value_at : value_at + 256])
        for part, kv in zip(probs, sources)
    )
    return top, total, weighed


def side_by_side(mixed):
    low = jnp.where(
        lanes(256, 144, 256), mixed[1], jnp.where(lanes(256, 64, 144), mixed[0], 0.0)
    )
    high = jnp.where(lanes(256, 176, 256), mixed[3], mixed[2])
    middle = jnp.where(lanes(128, 0, 96), low[:, 128:], high[:, :128])
    return jnp.concatenate([low[:, :128], middle, high[:, 128:]], axis=1)


def attention_kernel(q_ref, kv0_ref, kv1_ref, kv2_ref, kv3_ref, after_ref, out_ref, token_ref):
    token_ref[...] = after_ref[...]
    sources = (kv0_ref, kv1_ref, kv2_ref, kv3_ref)
    mixed = []
    for head in range(4):
        _, total, weighed = attend(q_ref, sources, head)
        mixed.append(weighed / total)
    out_ref[...] = side_by_side(mixed).astype(BF16)


def attention(query, sources, after):
    return pl.pallas_call(
        attention_kernel,
        in_specs=[pl.BlockSpec(memory_space=pltpu.VMEM)] * 6,
        out_shape=(kept(512, 384), TOKEN),
        compiler_params=params(),
        cost_estimate=cost(1000, 1000),
        name="attention_four_heads",
    )(query, *sources, after)


def near_kernel(q_ref, kv0_ref, kv1_ref, owner_ref, mixed_ref, stats_ref, pick_ref, token_ref):
    token_ref[...] = jnp.zeros((8, 128), F32)
    block = lax.broadcasted_iota(jnp.int32, (128, 512), 0)
    source = lax.broadcasted_iota(jnp.int32, (128, 512), 1)
    spread = (source // 4 == block).astype(F32).astype(BF16)
    owner = jnp.broadcast_to(owner_ref[...].astype(F32), (8, 128)).astype(BF16)
    owner = dot(owner, spread)[:1, :].astype(jnp.int32)
    row = lax.broadcasted_iota(jnp.int32, (512, 512), 0)
    place = owner * 4 + lax.broadcasted_iota(jnp.int32, (1, 512), 1) % 4
    pick_ref[...] = (row == place).astype(F32).astype(BF16)
    mixed = []
    for head in range(4):
        top, total, weighed = attend(q_ref, (kv0_ref, kv1_ref), head)
        mixed.append(weighed)
        stats_ref[head] = jnp.broadcast_to(top, (512, 128))
        stats_ref[4 + head] = jnp.broadcast_to(total, (512, 128))
    mixed_ref[...] = side_by_side(mixed)


def near_attention(query, sources, owner_table):
    return pl.pallas_call(
        near_kernel,
        out_shape=(
            kept(512, 384, dtype=F32),
            kept(8, 512, 128, dtype=F32),
            kept(512, 512),
            TOKEN,
        ),
        compiler_params=params(),
        cost_estimate=cost(1000, 1000),
        name="attention_near_keys",
    )(query, *sources, owner_table)


def far_kernel(last, q_ref, kv_ref, near_ref, stats_ref, out_ref, *rest):
    mixed = []
    for head in range(4):
        at = 0 if head < 2 else 128
        before = stats_ref[head]
        top, total, weighed = attend(q_ref, (kv_ref,), head, before)
        factor = jnp.exp2((before - top) * SCALE)
        total = total + factor * stats_ref[4 + head]
        if last:
            share = 1.0 / total
            weighed = wide(share, 2) * weighed
            factor = factor * share
        else:
            rest[0][head] = top
            rest[0][4 + head] = total
        mixed.append(weighed + wide(factor, 2) * near_ref[:, at : at + 256])
    out_ref[...] = side_by_side(mixed).astype(out_ref.dtype)


def far_attention(query, source, near, stats, last):
    mixed = (kept(512, 384, dtype=F32), kept(8, 512, 128, dtype=F32))
    return pl.pallas_call(
        functools.partial(far_kernel, last),
        out_shape=kept(512, 384) if last else mixed,
        compiler_params=params(),
        cost_estimate=cost(2 * 512 * 512 * 512 * 4, 2 * MIB, 4 * 512 * 512),
        name="attention_last_keys" if last else "attention_far_keys",
    )(query, source, near, stats)


def target_kernel(pick_ref, tokens_ref, att0_ref, att1_ref, w_out_ref, w_neck_ref, out_ref):
    first = jnp.concatenate([jnp.zeros((64, 1280), BF16), w_out_ref[:64, :]], axis=0)
    added = dot(att0_ref[:, 128:], w_out_ref[64:HALF, :]) + dot(att1_ref[...], w_out_ref[256:, :])
    added = added + dot(att0_ref[:, :128], first)
    block_out = (tokens_ref[...].astype(F32) + added).astype(BF16)
    target = layer_norm(dot(block_out, w_neck_ref[...])).astype(BF16)
    out_ref[...] = dot(pick_ref[...], target).reshape(128, 4, 256).astype(BF16)


def make_target(pick, tokens, att0, att1, w_out, w_neck):
    return pl.pallas_call(
        target_kernel,
        out_shape=shape(128, 4, 256),
        compiler_params=params(),
        cost_estimate=cost(2 * 512 * 1280 * 1024, 6 * MIB),
        name="out_neck_target",
    )(pick, tokens, att0, att1, w_out, w_neck)


def forward_kernel(
    core_ref, rows_ref, w_expand_ref, w_project_ref, pred_ref, slope_ref, act_t_ref, rows_t_ref, token_ref
):
    token_ref[...] = jnp.zeros((8, 128), F32)
    step = pl.program_id(0)
    core = core_ref[0]
    rows = rows_ref[...]

    @pl.when(step == 0)
    def _():
        out_row = lax.broadcasted_iota(jnp.int32, (512, 512), 0)
        column = lax.broadcasted_iota(jnp.int32, (512, 512), 1)
        member = jnp.where(out_row < 256, core, 1 - core)
        wanted = (out_row % 256) // 4 * 8 + member * 4 + out_row % 4
        pick = (column == wanted).astype(F32).astype(BF16)
        rows_t_ref[...] = dot_t(pick, rows).astype(BF16)

    pre = dot(rows, w_expand_ref[...])
    square = pre * pre
    bend = jnp.tanh(GELU_A * pre * (1.0 + GELU_B * square))
    gate = 0.5 * (1.0 + bend)
    act = (pre * gate).astype(BF16)
    slope_ref[...] = gate + (0.5 * GELU_A) * pre * (1.0 - bend * bend) * (
        1.0 + (3.0 * GELU_B) * square
    )
    act_t = act.T
    for group in range(32):
        half = jnp.where(core == group % 2, 0, 1024)
        start = pl.multiple_of(half + (step * 16 + group // 2) * 16, 16)
        act_t_ref[pl.ds(start, 16), :] = act_t[group * 16 : group * 16 + 16, :]
    part = dot(act, w_project_ref[...])

    @pl.when(step == 0)
    def _():
        pred_ref[...] = part

    @pl.when(step > 0)
    def _():
        pred_ref[...] += part


def student_forward(core, rows, w_expand, w_project):
    whole = lambda i: (0, 0)
    return pl.pallas_call(
        forward_kernel,
        grid=(4,),
        in_specs=[
            pl.BlockSpec(memory_space=pltpu.SMEM),
            pl.BlockSpec((512, 512), whole),
            pl.BlockSpec((512, 512), lambda i: (0, i)),
            pl.BlockSpec((512, 256), lambda i: (i, 0)),
        ],
        out_specs=[
            pl.BlockSpec((512, 256), whole),
            pl.BlockSpec((512, 512), lambda i: (0, i)),
            pl.BlockSpec((2048, 512), whole),
            pl.BlockSpec((512, 512), whole),
            pl.BlockSpec((8, 128), whole),
        ],
        out_shape=(
            kept(512, 256, dtype=F32),
            kept(512, 2048, dtype=F32),
            kept(2048, 512),
            kept(512, 512),
            TOKEN,
        ),
        compiler_params=params(),
        cost_estimate=cost(1000, 1000),
        name="student_forward",
    )(core, rows, w_expand, w_project)


def backward_kernel(
    pred_ref,
    moved_ref,
    slope_ref,
    w_project_ref,
    act_t_ref,
    rows_t_ref,
    error_ref,
    d_pred_ref,
    d_pre_ref,
    project_ref,
    expand_ref,
):
    error = pred_ref[...] - moved_ref[...].astype(F32).reshape(512, 256)
    error_ref[...] = error.astype(BF16)
    d_pred = (error * (1.0 / 512.0)).astype(BF16)
    d_pred_ref[...] = d_pred
    for i in range(4):
        part = slice(512 * i, 512 * i + 512)
        d_pre = (slope_ref[:, part] * dot_t(d_pred, w_project_ref[part, :])).astype(BF16)
        d_pre_ref[:, part] = d_pre
        expand_ref[:, part] = dot(rows_t_ref[256:, :], d_pre).astype(BF16)
    project_ref[...] = dot(act_t_ref[1024:, :], d_pred).astype(BF16)


def student_backward(pred, moved, slope, w_project, act_t, rows_t):
    return pl.pallas_call(
        backward_kernel,
        out_shape=(
            shape(512, 256),
            kept(512, 256),
            kept(512, 2048),
            shape(1024, 256),
            shape(256, 2048),
        ),
        compiler_params=params(),
        cost_estimate=cost(2 * 512 * 2048 * 640, 10 * MIB),
        name="student_backward",
    )(pred, moved, slope, w_project, act_t, rows_t)


def own_kernel(d_pred_ref, d_pre_ref, act_t_ref, rows_t_ref, project_ref, expand_ref):
    project_ref[...] = dot(act_t_ref[:1024, :], d_pred_ref[...])
    for i in range(4):
        part = slice(512 * i, 512 * i + 512)
        expand_ref[:, part] = dot(rows_t_ref[:256, :], d_pre_ref[:, part])


def own_half(d_pred, d_pre, act_t, rows_t):
    return pl.pallas_call(
        own_kernel,
        out_shape=(kept(1024, 256, dtype=F32), kept(256, 2048, dtype=F32)),
        compiler_params=params(),
        cost_estimate=cost(2 * 512 * 2048 * 384, 6 * MIB),
        name="own_half_gradients",
    )(d_pred, d_pre, act_t, rows_t)


def pack_kernel(project_ref, project_in_ref, expand_ref, expand_in_ref, out_ref):
    row = lax.broadcasted_iota(jnp.int32, (256, 256), 0)
    column = lax.broadcasted_iota(jnp.int32, (256, 256), 1)
    wanted = row % 32 // 4 * 32 + row // 32 * 4 + row % 4
    order = (column == wanted).astype(F32).astype(BF16)
    project = (project_ref[...] + project_in_ref[...].astype(F32)).astype(BF16)
    for block in range(8):
        part = slice(32 * block, 32 * block + 32)
        expand = (expand_ref[part, :] + expand_in_ref[part, :].astype(F32)).astype(BF16)
        stacked = jnp.concatenate([expand[:, 256 * j : 256 * j + 256] for j in range(8)], axis=0)
        sorted_rows = dot(order, stacked).astype(BF16)
        for i in range(8):
            chip = 8 * block + i
            out_ref[chip, :16, :] = project[16 * chip : 16 * chip + 16, :]
            out_ref[chip, 16:, :] = sorted_rows[32 * i : 32 * i + 32, :]


def pack(project, project_in, expand, expand_in):
    return pl.pallas_call(
        pack_kernel,
        out_shape=shape(64, 48, 256),
        compiler_params=params(),
        cost_estimate=cost(2 * 256 * 256 * 256 * 8, 6 * MIB),
        name="pack_gradients",
    )(project, project_in, expand, expand_in)


def finish_kernel(parts_ref, expand_ref, project_ref):
    total = jnp.sum(parts_ref[...].astype(F32), axis=0)
    project_ref[...] = total[:16, :]
    for j in range(8):
        expand_ref[:, 256 * j : 256 * j + 256] = total[16 + 4 * j : 20 + 4 * j, :]


def finish(parts):
    return pl.pallas_call(
        finish_kernel,
        out_shape=(shape(4, 2048, dtype=F32), shape(16, 256, dtype=F32)),
        compiler_params=params(),
        cost_estimate=cost(64 * 48 * 256, 2 * MIB),
        name="sum_gradients",
    )(parts)


def gate_kernel(*refs):
    refs[-1][...] = jnp.zeros((8, 128), F32)


def gate(value, *after, flops=10):
    return pl.pallas_call(
        gate_kernel,
        in_specs=[pl.BlockSpec(memory_space=pl.ANY)] * (1 + len(after)),
        out_specs=[
            pl.BlockSpec(memory_space=pl.ANY),
            pl.BlockSpec(memory_space=pltpu.VMEM),
        ],
        out_shape=(jax.ShapeDtypeStruct(value.shape, value.dtype), TOKEN),
        input_output_aliases={0: 0},
        compiler_params=params(1),
        cost_estimate=cost(flops, 10),
        name="gate",
    )(value, *after)


def swap(value, axis):
    return lax.ppermute(value, axis, [(0, 1), (1, 0)])


def per_device(
    tokens, w_query, w_key, w_value, w_out, w_neck, owner_table, student_in, w_expand, w_project
):
    core = lax.axis_index("c").astype(jnp.int32).reshape(1)
    normed, kv_first = first_project(in_hbm(tokens), in_hbm(w_key), in_hbm(w_value))
    far_first = swap(kv_first, "yh")
    near_first = swap(kv_first, "c")
    kv_second, query_first, query_second, kv_send = second_project(
        normed, in_hbm(w_key), in_hbm(w_value), in_hbm(w_query)
    )
    far_second = swap(kv_send, "yh")
    near_second = swap(kv_second, "c")
    pred, slope, act_t, rows_t, token = student_forward(
        core, in_hbm(student_in), in_hbm(w_expand), in_hbm(w_project)
    )
    far_first, _ = gate(far_first, token)
    near, stats, pick, token = near_attention(
        query_second, (kv_second, near_second), owner_table
    )
    att_first, token = attention(
        query_first, (kv_first, near_first, far_first, swap(far_first, "c")), token
    )
    far_second, token = gate(far_second, token)
    last_second = swap(far_second, "c")
    near, stats = far_attention(query_second, far_second, near, stats, False)
    att_second = far_attention(query_second, last_second, near, stats, True)
    target = make_target(pick, tokens, att_first, att_second, w_out, w_neck)
    moved = lax.all_to_all(target, AXES, split_axis=0, concat_axis=0, tiled=True)
    error, d_pred, d_pre, project_out, expand_out = student_backward(
        pred, moved, slope, w_project, act_t, rows_t
    )
    project_in = swap(project_out, "c")
    expand_in = swap(expand_out, "c")
    project, expand = own_half(d_pred, d_pre, act_t, rows_t)
    packed = pack(project, project_in, expand, expand_in)
    parts = lax.all_to_all(packed, CHIPS, split_axis=0, concat_axis=0, tiled=True)
    grad_expand, grad_project = finish(parts)
    return (error, grad_expand, grad_project)


def solution(mesh):
    fine = Mesh(mesh.devices.reshape(4, 2, 4, 2, 2), AXES)
    rows = P(AXES, None)
    return jax.shard_map(
        per_device,
        mesh=fine,
        in_specs=(rows, P(), P(), P(), P(), P(), rows, rows, P(), P()),
        out_specs=(rows, rows, rows),
        check_vma=False,
    )
```

```python
import functools

import jax
import jax.numpy as jnp
from jax import lax
from jax.experimental import pallas as pl
from jax.experimental.pallas import tpu as pltpu
from jax.sharding import Mesh
from jax.sharding import PartitionSpec as P

HEAD = 80
HALF = 320
SCALE = HEAD**-0.5 * 1.4426950408889634
AXES = ("x", "yl", "z", "yh", "c")
CHIPS = ("yh", "yl", "x", "z")
BY_CORE = ("c", "x", "yl", "z", "yh")
GELU_A = 0.7978845608028654
GELU_B = 0.044715
F32 = jnp.float32
TOKEN = jax.ShapeDtypeStruct((8, 128), jnp.float32)
BF16 = jnp.bfloat16
MIB = 2**20


def dot(a, b):
    return jnp.dot(a, b, preferred_element_type=F32)


def dot_t(a, b):
    return lax.dot_general(a, b, (((1,), (1,)), ((), ())), preferred_element_type=F32)


def layer_norm(value):
    centred = value - jnp.mean(value, axis=-1, keepdims=True)
    spread = jnp.mean(centred * centred, axis=-1, keepdims=True)
    return centred * lax.rsqrt(spread + 1e-06)


def lanes(width, low, high):
    index = lax.broadcasted_iota(jnp.int32, (1, width), 1)
    return (index >= low) & (index < high)


def shape(*dims, dtype=BF16):
    return jax.ShapeDtypeStruct(dims, dtype)


def kept(*dims, dtype=BF16):
    return pltpu.VMEM(dims, dtype)


def in_hbm(value):
    return pltpu.with_memory_space_constraint(value, pltpu.HBM)


def params(mib=16):
    return pltpu.CompilerParams(vmem_limit_bytes=mib * MIB)


def cost(flops, moved, exps=0):
    return pl.CostEstimate(flops=flops, bytes_accessed=moved, transcendentals=exps)


def first_kernel(
    tokens_hbm,
    w_key_hbm,
    w_value_hbm,
    normed_ref,
    send_ref,
    tokens_ref,
    w_key_ref,
    w_value_ref,
    kv_ref,
    sems,
):
    copies = []
    for i in range(4):
        rows = pl.ds(128 * i, 128)
        copies.append((tokens_hbm.at[rows], tokens_ref.at[rows]))
    for source, target in ((w_key_hbm, w_key_ref), (w_value_hbm, w_value_ref)):
        for i in range(2):
            rows = pl.ds(640 * i, 640)
            copies.append((source.at[rows, pl.ds(0, 384)], target.at[rows]))
    copies = [
        pltpu.make_async_copy(source, target, sems.at[i])
        for i, (source, target) in enumerate(copies)
    ]
    for copy in copies:
        copy.start()
    for i in range(4):
        copies[i].wait()
        rows = pl.ds(128 * i, 128)
        normed_ref[rows, :] = layer_norm(tokens_ref[rows, :].astype(F32)).astype(BF16)
    for copy in copies[4:]:
        copy.wait()
    sends = []
    for i in range(2):
        rows = pl.ds(256 * i, 256)
        normed = normed_ref[rows, :]
        keys = dot(normed, w_key_ref[...])
        values = dot(normed, w_value_ref[...])
        kv = jnp.concatenate([keys[:, :HALF], values[:, :HALF]], axis=1).astype(BF16)
        kv_ref[rows, :] = kv
        sends.append(pltpu.make_async_copy(kv_ref.at[rows], send_ref.at[rows], sems.at[8 + i]))
        sends[-1].start()
    for send in sends:
        send.wait()


def first_project(tokens, w_key, w_value):
    return pl.pallas_call(
        first_kernel,
        in_specs=[pl.BlockSpec(memory_space=pltpu.HBM)] * 3,
        out_specs=[pl.BlockSpec(memory_space=pltpu.VMEM), pl.BlockSpec(memory_space=pl.ANY)],
        out_shape=(kept(512, 1280), shape(512, 640)),
        scratch_shapes=[
            pltpu.VMEM((512, 1280), BF16),
            pltpu.VMEM((1280, 384), BF16),
            pltpu.VMEM((1280, 384), BF16),
            pltpu.VMEM((512, 640), BF16),
            pltpu.SemaphoreType.DMA((10,)),
        ],
        compiler_params=params(),
        cost_estimate=cost(2 * 512 * 1280 * 768, 6 * MIB),
        name="norm_kv_first",
    )(tokens, w_key, w_value)


def second_kernel(
    normed_ref, w_key_ref, w_value_ref, w_query_ref, kv_ref, q0_ref, q1_ref, send_ref, sems
):
    normed = normed_ref[...]
    keys = dot(normed, w_key_ref[:, 256:])
    values = dot(normed, w_value_ref[:, 256:])
    kv_ref[...] = jnp.concatenate([keys[:, 64:], values[:, 64:]], axis=1).astype(BF16)
    sends = (
        pltpu.make_async_copy(kv_ref, send_ref.at[pl.ds(0, 512)], sems.at[0]),
        pltpu.make_async_copy(kv_ref.at[pl.ds(0, 16)], send_ref.at[pl.ds(512, 16)], sems.at[1]),
    )
    for send in sends:
        send.start()
    query = dot(normed, w_query_ref[...])
    blank = jnp.zeros((512, 64), F32)
    q0_ref[...] = jnp.concatenate([query[:, :HALF], blank], axis=1).astype(BF16)
    q1_ref[...] = jnp.concatenate([query[:, HALF:], blank], axis=1).astype(BF16)
    for send in sends:
        send.wait()


def second_project(normed, w_key, w_value, w_query):
    return pl.pallas_call(
        second_kernel,
        out_specs=[pl.BlockSpec(memory_space=pltpu.VMEM)] * 3 + [pl.BlockSpec(memory_space=pl.ANY)],
        out_shape=(kept(512, 640), kept(512, 384), kept(512, 384), shape(528, 640)),
        scratch_shapes=[pltpu.SemaphoreType.DMA((2,))],
        compiler_params=params(),
        cost_estimate=cost(1000, 1000),
        name="kv_second_query",
    )(normed, w_key, w_value, w_query)


def masked_query(q_ref, head):
    key_at = 0 if head < 3 else 128
    low = HEAD * head - key_at
    return q_ref[:, key_at : key_at + 256] * lanes(256, low, low + HEAD).astype(F32).astype(BF16)


def wide(value, times):
    return jnp.concatenate([value] * times, axis=1)


def attend(q_ref, sources, head, floor=None):
    key_at = 0 if head < 3 else 128
    value_at = 256 if head < 2 else 384
    query = masked_query(q_ref, head)
    scores = [dot_t(query, kv[:512, key_at : key_at + 256]) for kv in sources]
    top = jnp.max(functools.reduce(jnp.maximum, scores), axis=1, keepdims=True)
    if floor is not None:
        top = jnp.maximum(jnp.broadcast_to(top, floor.shape), floor)
    shift = top if floor is None else wide(top, 4)
    probs = [jnp.exp2((part - shift) * SCALE) for part in scores]
    total = jnp.sum(functools.reduce(jnp.add, probs), axis=1, keepdims=True)
    weighed = sum(
        dot(part.astype(BF16), kv[:512, value_at : value_at + 256])
        for part, kv in zip(probs, sources)
    )
    return top, total, weighed


def side_by_side(mixed):
    low = jnp.where(
        lanes(256, 144, 256), mixed[1], jnp.where(lanes(256, 64, 144), mixed[0], 0.0)
    )
    high = jnp.where(lanes(256, 176, 256), mixed[3], mixed[2])
    middle = jnp.where(lanes(128, 0, 96), low[:, 128:], high[:, :128])
    return jnp.concatenate([low[:, :128], middle, high[:, 128:]], axis=1)


def attention_kernel(q_ref, kv0_ref, kv1_ref, kv2_ref, kv3_ref, after_ref, out_ref, token_ref):
    token_ref[...] = after_ref[...]
    sources = (kv0_ref, kv1_ref, kv2_ref, kv3_ref)
    mixed = []
    for head in range(4):
        _, total, weighed = attend(q_ref, sources, head)
        mixed.append(weighed / total)
    out_ref[...] = side_by_side(mixed).astype(BF16)


def attention(query, sources, after):
    return pl.pallas_call(
        attention_kernel,
        in_specs=[pl.BlockSpec(memory_space=pltpu.VMEM)] * 6,
        out_shape=(kept(512, 384), TOKEN),
        compiler_params=params(),
        cost_estimate=cost(1000, 1000),
        name="attention_four_heads",
    )(query, *sources, after)


def near_kernel(q_ref, kv0_ref, kv1_ref, owner_ref, mixed_ref, stats_ref, pick_ref, token_ref):
    token_ref[...] = jnp.zeros((8, 128), F32)
    block = lax.broadcasted_iota(jnp.int32, (128, 512), 0)
    source = lax.broadcasted_iota(jnp.int32, (128, 512), 1)
    spread = (source // 4 == block).astype(F32).astype(BF16)
    owner = jnp.broadcast_to(owner_ref[...].astype(F32), (8, 128)).astype(BF16)
    owner = dot(owner, spread)[:1, :].astype(jnp.int32)
    row = lax.broadcasted_iota(jnp.int32, (512, 512), 0)
    place = (owner % 2 * 64 + owner // 2) * 4 + lax.broadcasted_iota(jnp.int32, (1, 512), 1) % 4
    pick_ref[...] = (row == place).astype(F32).astype(BF16)
    mixed = []
    for head in range(4):
        top, total, weighed = attend(q_ref, (kv0_ref, kv1_ref), head)
        mixed.append(weighed)
        stats_ref[head] = jnp.broadcast_to(top, (512, 128))
        stats_ref[4 + head] = jnp.broadcast_to(total, (512, 128))
    mixed_ref[...] = side_by_side(mixed)


def near_attention(query, sources, owner_table):
    return pl.pallas_call(
        near_kernel,
        out_shape=(
            kept(512, 384, dtype=F32),
            kept(8, 512, 128, dtype=F32),
            kept(512, 512),
            TOKEN,
        ),
        compiler_params=params(),
        cost_estimate=cost(1000, 1000),
        name="attention_near_keys",
    )(query, *sources, owner_table)


def far_kernel(last, q_ref, kv_ref, near_ref, stats_ref, out_ref, *rest):
    mixed = []
    for head in range(4):
        at = 0 if head < 2 else 128
        before = stats_ref[head]
        top, total, weighed = attend(q_ref, (kv_ref,), head, before)
        factor = jnp.exp2((before - top) * SCALE)
        total = total + factor * stats_ref[4 + head]
        if last:
            share = 1.0 / total
            weighed = wide(share, 2) * weighed
            factor = factor * share
        else:
            rest[0][head] = top
            rest[0][4 + head] = total
        mixed.append(weighed + wide(factor, 2) * near_ref[:, at : at + 256])
    out_ref[...] = side_by_side(mixed).astype(out_ref.dtype)


def far_attention(query, source, near, stats, last):
    mixed = (kept(512, 384, dtype=F32), kept(8, 512, 128, dtype=F32))
    return pl.pallas_call(
        functools.partial(far_kernel, last),
        out_shape=kept(512, 384) if last else mixed,
        compiler_params=params(),
        cost_estimate=cost(2 * 512 * 512 * 512 * 4, 2 * MIB, 4 * 512 * 512),
        name="attention_last_keys" if last else "attention_far_keys",
    )(query, source, near, stats)


def target_kernel(pick_ref, tokens_ref, att0_ref, att1_ref, w_out_ref, w_neck_ref, out_ref):
    first = jnp.concatenate([jnp.zeros((64, 1280), BF16), w_out_ref[:64, :]], axis=0)
    added = dot(att0_ref[:, 128:], w_out_ref[64:HALF, :]) + dot(att1_ref[...], w_out_ref[256:, :])
    added = added + dot(att0_ref[:, :128], first)
    block_out = (tokens_ref[...].astype(F32) + added).astype(BF16)
    target = layer_norm(dot(block_out, w_neck_ref[...])).astype(BF16)
    out_ref[...] = dot(pick_ref[...], target).reshape(128, 4, 256).astype(BF16)


def make_target(pick, tokens, att0, att1, w_out, w_neck):
    return pl.pallas_call(
        target_kernel,
        out_shape=shape(128, 4, 256),
        compiler_params=params(),
        cost_estimate=cost(2 * 512 * 1280 * 1024, 6 * MIB),
        name="out_neck_target",
    )(pick, tokens, att0, att1, w_out, w_neck)


def forward_kernel(
    core_ref, rows_ref, w_expand_ref, w_project_ref, pred_ref, slope_ref, act_t_ref, rows_t_ref, token_ref
):
    token_ref[...] = jnp.zeros((8, 128), F32)
    step = pl.program_id(0)
    core = core_ref[0]
    rows = rows_ref[...]

    @pl.when(step == 0)
    def _():
        out_row = lax.broadcasted_iota(jnp.int32, (512, 512), 0)
        column = lax.broadcasted_iota(jnp.int32, (512, 512), 1)
        member = jnp.where(out_row < 256, core, 1 - core)
        wanted = (out_row % 256) // 4 * 8 + member * 4 + out_row % 4
        pick = (column == wanted).astype(F32).astype(BF16)
        rows_t_ref[...] = dot_t(pick, rows).astype(BF16)

    pre = dot(rows, w_expand_ref[...])
    square = pre * pre
    bend = jnp.tanh(GELU_A * pre * (1.0 + GELU_B * square))
    gate = 0.5 * (1.0 + bend)
    act = (pre * gate).astype(BF16)
    slope_ref[...] = gate + (0.5 * GELU_A) * pre * (1.0 - bend * bend) * (
        1.0 + (3.0 * GELU_B) * square
    )
    act_t = act.T
    for group in range(32):
        half = jnp.where(core == group % 2, 0, 1024)
        start = pl.multiple_of(half + (step * 16 + group // 2) * 16, 16)
        act_t_ref[pl.ds(start, 16), :] = act_t[group * 16 : group * 16 + 16, :]
    part = dot(act, w_project_ref[...])

    @pl.when(step == 0)
    def _():
        pred_ref[...] = part

    @pl.when(step > 0)
    def _():
        pred_ref[...] += part


def student_forward(core, rows, w_expand, w_project):
    whole = lambda i: (0, 0)
    return pl.pallas_call(
        forward_kernel,
        grid=(4,),
        in_specs=[
            pl.BlockSpec(memory_space=pltpu.SMEM),
            pl.BlockSpec((512, 512), whole),
            pl.BlockSpec((512, 512), lambda i: (0, i)),
            pl.BlockSpec((512, 256), lambda i: (i, 0)),
        ],
        out_specs=[
            pl.BlockSpec((512, 256), whole),
            pl.BlockSpec((512, 512), lambda i: (0, i)),
            pl.BlockSpec((2048, 512), whole),
            pl.BlockSpec((512, 512), whole),
            pl.BlockSpec((8, 128), whole),
        ],
        out_shape=(
            kept(512, 256, dtype=F32),
            kept(512, 2048, dtype=F32),
            kept(2048, 512),
            kept(512, 512),
            TOKEN,
        ),
        compiler_params=params(),
        cost_estimate=cost(1000, 1000),
        name="student_forward",
    )(core, rows, w_expand, w_project)


def backward_kernel(
    pred_ref,
    moved_ref,
    slope_ref,
    w_project_ref,
    act_t_ref,
    rows_t_ref,
    error_ref,
    d_pred_ref,
    d_pre_ref,
    project_ref,
    expand_ref,
):
    moved = moved_ref[...].astype(F32)
    moved = jnp.concatenate([moved[:64], moved[64:]], axis=1).reshape(512, 256)
    error = pred_ref[...] - moved
    error_ref[...] = error.astype(BF16)
    d_pred = (error * (1.0 / 512.0)).astype(BF16)
    d_pred_ref[...] = d_pred
    for i in range(4):
        part = slice(512 * i, 512 * i + 512)
        d_pre = (slope_ref[:, part] * dot_t(d_pred, w_project_ref[part, :])).astype(BF16)
        d_pre_ref[:, part] = d_pre
        expand_ref[:, part] = dot(rows_t_ref[256:, :], d_pre).astype(BF16)
    project_ref[...] = dot(act_t_ref[1024:, :], d_pred).astype(BF16)


def student_backward(pred, moved, slope, w_project, act_t, rows_t):
    return pl.pallas_call(
        backward_kernel,
        out_shape=(
            shape(512, 256),
            kept(512, 256),
            kept(512, 2048),
            shape(1024, 256),
            shape(256, 2048),
        ),
        compiler_params=params(),
        cost_estimate=cost(2 * 512 * 2048 * 640, 10 * MIB),
        name="student_backward",
    )(pred, moved, slope, w_project, act_t, rows_t)


def own_kernel(d_pred_ref, d_pre_ref, act_t_ref, rows_t_ref, project_ref, expand_ref):
    project_ref[...] = dot(act_t_ref[:1024, :], d_pred_ref[...])
    for i in range(4):
        part = slice(512 * i, 512 * i + 512)
        expand_ref[:, part] = dot(rows_t_ref[:256, :], d_pre_ref[:, part])


def own_half(d_pred, d_pre, act_t, rows_t):
    return pl.pallas_call(
        own_kernel,
        out_shape=(kept(1024, 256, dtype=F32), kept(256, 2048, dtype=F32)),
        compiler_params=params(),
        cost_estimate=cost(2 * 512 * 2048 * 384, 6 * MIB),
        name="own_half_gradients",
    )(d_pred, d_pre, act_t, rows_t)


def pack_kernel(project_ref, project_in_ref, expand_ref, expand_in_ref, out_ref):
    row = lax.broadcasted_iota(jnp.int32, (256, 256), 0)
    column = lax.broadcasted_iota(jnp.int32, (256, 256), 1)
    wanted = row % 32 // 4 * 32 + row // 32 * 4 + row % 4
    order = (column == wanted).astype(F32).astype(BF16)
    project = (project_ref[...] + project_in_ref[...].astype(F32)).astype(BF16)
    for block in range(8):
        part = slice(32 * block, 32 * block + 32)
        expand = (expand_ref[part, :] + expand_in_ref[part, :].astype(F32)).astype(BF16)
        stacked = jnp.concatenate([expand[:, 256 * j : 256 * j + 256] for j in range(8)], axis=0)
        sorted_rows = dot(order, stacked).astype(BF16)
        for i in range(8):
            chip = 8 * block + i
            place = chip % 2 * 32 + chip // 8 % 2 * 16 + chip // 16 * 4 + chip // 2 % 4
            out_ref[place, :16, :] = project[16 * chip : 16 * chip + 16, :]
            out_ref[place, 16:, :] = sorted_rows[32 * i : 32 * i + 32, :]


def pack(project, project_in, expand, expand_in):
    return pl.pallas_call(
        pack_kernel,
        out_shape=shape(64, 48, 256),
        compiler_params=params(),
        cost_estimate=cost(2 * 256 * 256 * 256 * 8, 6 * MIB),
        name="pack_gradients",
    )(project, project_in, expand, expand_in)


def finish_kernel(parts_ref, expand_ref, project_ref):
    total = jnp.sum(parts_ref[...].astype(F32), axis=0)
    project_ref[...] = total[:16, :]
    for j in range(8):
        expand_ref[:, 256 * j : 256 * j + 256] = total[16 + 4 * j : 20 + 4 * j, :]


def finish(parts):
    return pl.pallas_call(
        finish_kernel,
        out_shape=(shape(4, 2048, dtype=F32), shape(16, 256, dtype=F32)),
        compiler_params=params(),
        cost_estimate=cost(64 * 48 * 256, 2 * MIB),
        name="sum_gradients",
    )(parts)


def gate_kernel(value_ref, after_ref, out_ref):
    del value_ref, after_ref, out_ref


def gate(value, after):
    return pl.pallas_call(
        gate_kernel,
        in_specs=[pl.BlockSpec(memory_space=pl.ANY)] * 2,
        out_specs=pl.BlockSpec(memory_space=pl.ANY),
        out_shape=jax.ShapeDtypeStruct(value.shape, value.dtype),
        input_output_aliases={0: 0},
        compiler_params=params(1),
        cost_estimate=cost(10, 10),
        name="gate",
    )(value, after)


def swap(value, axis):
    return lax.ppermute(value, axis, [(0, 1), (1, 0)])


def per_device(
    tokens, w_query, w_key, w_value, w_out, w_neck, owner_table, student_in, w_expand, w_project
):
    core = lax.axis_index("c").astype(jnp.int32).reshape(1)
    normed, kv_first = first_project(in_hbm(tokens), in_hbm(w_key), in_hbm(w_value))
    far_first = swap(kv_first, "yh")
    near_first = swap(kv_first, "c")
    kv_second, query_first, query_second, kv_send = second_project(
        normed, in_hbm(w_key), in_hbm(w_value), in_hbm(w_query)
    )
    far_second = swap(kv_send, "yh")
    near_second = swap(kv_second, "c")
    pred, slope, act_t, rows_t, token = student_forward(
        core, in_hbm(student_in), in_hbm(w_expand), in_hbm(w_project)
    )
    far_first = gate(far_first, token)
    near, stats, pick, token = near_attention(
        query_second, (kv_second, near_second), owner_table
    )
    att_first, token = attention(
        query_first, (kv_first, near_first, far_first, swap(far_first, "c")), token
    )
    far_second = gate(far_second, token)
    last_second = swap(far_second, "c")
    near, stats = far_attention(query_second, far_second, near, stats, False)
    att_second = far_attention(query_second, last_second, near, stats, True)
    target = make_target(pick, tokens, att_first, att_second, w_out, w_neck)
    moved = lax.all_to_all(target, BY_CORE, split_axis=0, concat_axis=0, tiled=True)
    error, d_pred, d_pre, project_out, expand_out = student_backward(
        pred, moved, slope, w_project, act_t, rows_t
    )
    project_in = swap(project_out, "c")
    expand_in = swap(expand_out, "c")
    project, expand = own_half(d_pred, d_pre, act_t, rows_t)
    packed = pack(project, project_in, expand, expand_in)
    parts = lax.all_to_all(packed, CHIPS, split_axis=0, concat_axis=0, tiled=True)
    grad_expand, grad_project = finish(parts)
    return (error, grad_expand, grad_project)


def solution(mesh):
    fine = Mesh(mesh.devices.reshape(4, 2, 4, 2, 2), AXES)
    rows = P(AXES, None)
    return jax.shard_map(
        per_device,
        mesh=fine,
        in_specs=(rows, P(), P(), P(), P(), P(), rows, rows, P(), P()),
        out_specs=(rows, rows, rows),
        check_vma=False,
    )
```

```python
import functools

import jax
import jax.numpy as jnp
from jax import lax
from jax.experimental import pallas as pl
from jax.experimental.pallas import tpu as pltpu
from jax.sharding import Mesh
from jax.sharding import PartitionSpec as P

HEAD = 80
HALF = 320
SCALE = HEAD**-0.5 * 1.4426950408889634
AXES = ("x", "yl", "z", "yh", "c")
CHIPS = ("yh", "yl", "x", "z")
BY_CORE = ("c", "x", "yl", "z", "yh")
GELU_A = 0.7978845608028654
GELU_B = 0.044715
F32 = jnp.float32
TOKEN = jax.ShapeDtypeStruct((8, 128), jnp.float32)
BF16 = jnp.bfloat16
MIB = 2**20


def dot(a, b):
    return jnp.dot(a, b, preferred_element_type=F32)


def dot_t(a, b):
    return lax.dot_general(a, b, (((1,), (1,)), ((), ())), preferred_element_type=F32)


def layer_norm(value):
    centred = value - jnp.mean(value, axis=-1, keepdims=True)
    spread = jnp.mean(centred * centred, axis=-1, keepdims=True)
    return centred * lax.rsqrt(spread + 1e-06)


def lanes(width, low, high):
    index = lax.broadcasted_iota(jnp.int32, (1, width), 1)
    return (index >= low) & (index < high)


def shape(*dims, dtype=BF16):
    return jax.ShapeDtypeStruct(dims, dtype)


def kept(*dims, dtype=BF16):
    return pltpu.VMEM(dims, dtype)


def in_hbm(value):
    return pltpu.with_memory_space_constraint(value, pltpu.HBM)


def params(mib=16):
    return pltpu.CompilerParams(vmem_limit_bytes=mib * MIB)


def cost(flops, moved, exps=0):
    return pl.CostEstimate(flops=flops, bytes_accessed=moved, transcendentals=exps)


def first_kernel(
    tokens_hbm,
    w_key_hbm,
    w_value_hbm,
    normed_ref,
    send_ref,
    tokens_ref,
    w_key_ref,
    w_value_ref,
    kv_ref,
    sems,
):
    copies = []
    for i in range(4):
        rows = pl.ds(128 * i, 128)
        copies.append((tokens_hbm.at[rows], tokens_ref.at[rows]))
    for source, target in ((w_key_hbm, w_key_ref), (w_value_hbm, w_value_ref)):
        for i in range(2):
            rows = pl.ds(640 * i, 640)
            copies.append((source.at[rows, pl.ds(0, 384)], target.at[rows]))
    copies = [
        pltpu.make_async_copy(source, target, sems.at[i])
        for i, (source, target) in enumerate(copies)
    ]
    for copy in copies:
        copy.start()
    for i in range(4):
        copies[i].wait()
        rows = pl.ds(128 * i, 128)
        normed_ref[rows, :] = layer_norm(tokens_ref[rows, :].astype(F32)).astype(BF16)
    for copy in copies[4:]:
        copy.wait()
    sends = []
    for i in range(2):
        rows = pl.ds(256 * i, 256)
        normed = normed_ref[rows, :]
        keys = dot(normed, w_key_ref[...])
        values = dot(normed, w_value_ref[...])
        kv = jnp.concatenate([keys[:, :HALF], values[:, :HALF]], axis=1).astype(BF16)
        kv_ref[rows, :] = kv
        sends.append(pltpu.make_async_copy(kv_ref.at[rows], send_ref.at[rows], sems.at[8 + i]))
        sends[-1].start()
    for send in sends:
        send.wait()


def first_project(tokens, w_key, w_value):
    return pl.pallas_call(
        first_kernel,
        in_specs=[pl.BlockSpec(memory_space=pltpu.HBM)] * 3,
        out_specs=[pl.BlockSpec(memory_space=pltpu.VMEM), pl.BlockSpec(memory_space=pl.ANY)],
        out_shape=(kept(512, 1280), shape(512, 640)),
        scratch_shapes=[
            pltpu.VMEM((512, 1280), BF16),
            pltpu.VMEM((1280, 384), BF16),
            pltpu.VMEM((1280, 384), BF16),
            pltpu.VMEM((512, 640), BF16),
            pltpu.SemaphoreType.DMA((10,)),
        ],
        compiler_params=params(),
        cost_estimate=cost(2 * 512 * 1280 * 768, 6 * MIB),
        name="norm_kv_first",
    )(tokens, w_key, w_value)


def second_kernel(
    normed_ref, w_key_ref, w_value_ref, w_query_ref, kv_ref, q0_ref, q1_ref, send_ref, sems
):
    normed = normed_ref[...]
    keys = dot(normed, w_key_ref[:, 256:])
    values = dot(normed, w_value_ref[:, 256:])
    kv_ref[...] = jnp.concatenate([keys[:, 64:], values[:, 64:]], axis=1).astype(BF16)
    sends = (
        pltpu.make_async_copy(kv_ref, send_ref.at[pl.ds(0, 512)], sems.at[0]),
        pltpu.make_async_copy(kv_ref.at[pl.ds(0, 16)], send_ref.at[pl.ds(512, 16)], sems.at[1]),
    )
    for send in sends:
        send.start()
    query = dot(normed, w_query_ref[...])
    blank = jnp.zeros((512, 64), F32)
    q0_ref[...] = jnp.concatenate([query[:, :HALF], blank], axis=1).astype(BF16)
    q1_ref[...] = jnp.concatenate([query[:, HALF:], blank], axis=1).astype(BF16)
    for send in sends:
        send.wait()


def second_project(normed, w_key, w_value, w_query):
    return pl.pallas_call(
        second_kernel,
        out_specs=[pl.BlockSpec(memory_space=pltpu.VMEM)] * 3 + [pl.BlockSpec(memory_space=pl.ANY)],
        out_shape=(kept(512, 640), kept(512, 384), kept(512, 384), shape(528, 640)),
        scratch_shapes=[pltpu.SemaphoreType.DMA((2,))],
        compiler_params=params(),
        cost_estimate=cost(1000, 1000),
        name="kv_second_query",
    )(normed, w_key, w_value, w_query)


def masked_query(q_ref, head):
    key_at = 0 if head < 3 else 128
    low = HEAD * head - key_at
    return q_ref[:, key_at : key_at + 256] * lanes(256, low, low + HEAD).astype(F32).astype(BF16)


def wide(value, times):
    return jnp.concatenate([value] * times, axis=1)


def attend(q_ref, sources, head, floor=None):
    key_at = 0 if head < 3 else 128
    value_at = 256 if head < 2 else 384
    query = masked_query(q_ref, head)
    scores = [dot_t(query, kv[:512, key_at : key_at + 256]) for kv in sources]
    top = jnp.max(functools.reduce(jnp.maximum, scores), axis=1, keepdims=True)
    if floor is not None:
        top = jnp.maximum(jnp.broadcast_to(top, floor.shape), floor)
    shift = top if floor is None else wide(top, 4)
    probs = [jnp.exp2((part - shift) * SCALE) for part in scores]
    total = jnp.sum(functools.reduce(jnp.add, probs), axis=1, keepdims=True)
    weighed = sum(
        dot(part.astype(BF16), kv[:512, value_at : value_at + 256])
        for part, kv in zip(probs, sources)
    )
    return top, total, weighed


def side_by_side(mixed):
    low = jnp.where(
        lanes(256, 144, 256), mixed[1], jnp.where(lanes(256, 64, 144), mixed[0], 0.0)
    )
    high = jnp.where(lanes(256, 176, 256), mixed[3], mixed[2])
    middle = jnp.where(lanes(128, 0, 96), low[:, 128:], high[:, :128])
    return jnp.concatenate([low[:, :128], middle, high[:, 128:]], axis=1)


def attention_kernel(q_ref, kv0_ref, kv1_ref, kv2_ref, kv3_ref, after_ref, out_ref, token_ref):
    token_ref[...] = after_ref[...]
    sources = (kv0_ref, kv1_ref, kv2_ref, kv3_ref)
    mixed = []
    for head in range(4):
        _, total, weighed = attend(q_ref, sources, head)
        mixed.append(weighed / total)
    out_ref[...] = side_by_side(mixed).astype(BF16)


def attention(query, sources, after):
    return pl.pallas_call(
        attention_kernel,
        in_specs=[pl.BlockSpec(memory_space=pltpu.VMEM)] * 6,
        out_shape=(kept(512, 384), TOKEN),
        compiler_params=params(),
        cost_estimate=cost(1000, 1000),
        name="attention_four_heads",
    )(query, *sources, after)


def near_kernel(q_ref, kv0_ref, kv1_ref, owner_ref, mixed_ref, stats_ref, pick_ref, token_ref):
    token_ref[...] = jnp.zeros((8, 128), F32)
    block = lax.broadcasted_iota(jnp.int32, (128, 512), 0)
    source = lax.broadcasted_iota(jnp.int32, (128, 512), 1)
    spread = (source // 4 == block).astype(F32).astype(BF16)
    owner = jnp.broadcast_to(owner_ref[...].astype(F32), (8, 128)).astype(BF16)
    owner = dot(owner, spread)[:1, :].astype(jnp.int32)
    row = lax.broadcasted_iota(jnp.int32, (512, 512), 0)
    place = (owner % 2 * 64 + owner // 2) * 4 + lax.broadcasted_iota(jnp.int32, (1, 512), 1) % 4
    pick_ref[...] = (row == place).astype(F32).astype(BF16)
    mixed = []
    for head in range(4):
        top, total, weighed = attend(q_ref, (kv0_ref, kv1_ref), head)
        mixed.append(weighed)
        stats_ref[head] = jnp.broadcast_to(top, (512, 128))
        stats_ref[4 + head] = jnp.broadcast_to(total, (512, 128))
    mixed_ref[...] = side_by_side(mixed)


def near_attention(query, sources, owner_table):
    return pl.pallas_call(
        near_kernel,
        out_shape=(
            kept(512, 384, dtype=F32),
            kept(8, 512, 128, dtype=F32),
            kept(512, 512),
            TOKEN,
        ),
        compiler_params=params(),
        cost_estimate=cost(1000, 1000),
        name="attention_near_keys",
    )(query, *sources, owner_table)


def far_kernel(last, q_ref, kv_ref, near_ref, stats_ref, out_ref, *rest):
    mixed = []
    for head in range(4):
        at = 0 if head < 2 else 128
        before = stats_ref[head]
        top, total, weighed = attend(q_ref, (kv_ref,), head, before)
        factor = jnp.exp2((before - top) * SCALE)
        total = total + factor * stats_ref[4 + head]
        if last:
            share = 1.0 / total
            weighed = wide(share, 2) * weighed
            factor = factor * share
        else:
            rest[0][head] = top
            rest[0][4 + head] = total
        mixed.append(weighed + wide(factor, 2) * near_ref[:, at : at + 256])
    out_ref[...] = side_by_side(mixed).astype(out_ref.dtype)


def far_attention(query, source, near, stats, last):
    mixed = (kept(512, 384, dtype=F32), kept(8, 512, 128, dtype=F32))
    return pl.pallas_call(
        functools.partial(far_kernel, last),
        out_shape=kept(512, 384) if last else mixed,
        compiler_params=params(),
        cost_estimate=cost(2 * 512 * 512 * 512 * 4, 2 * MIB, 4 * 512 * 512),
        name="attention_last_keys" if last else "attention_far_keys",
    )(query, source, near, stats)


def first_out_kernel(tokens_ref, att_ref, w_out_ref, after_ref, out_ref, token_ref):
    token_ref[...] = after_ref[...]
    top = jnp.concatenate([jnp.zeros((64, 1280), BF16), w_out_ref[:64, :]], axis=0)
    added = dot(att_ref[:, 128:], w_out_ref[64:HALF, :]) + dot(att_ref[:, :128], top)
    out_ref[...] = tokens_ref[...].astype(F32) + added


def first_out(tokens, att, w_out, after):
    return pl.pallas_call(
        first_out_kernel,
        out_shape=(kept(512, 1280, dtype=F32), TOKEN),
        compiler_params=params(),
        cost_estimate=cost(1000, 1000),
        name="first_heads_out",
    )(tokens, att, w_out, after)


def target_kernel(pick_ref, base_ref, att_ref, w_out_ref, w_neck_ref, out_ref):
    block_out = (base_ref[...] + dot(att_ref[...], w_out_ref[256:, :])).astype(BF16)
    target = layer_norm(dot(block_out, w_neck_ref[...])).astype(BF16)
    out_ref[...] = dot(pick_ref[...], target).reshape(128, 4, 256).astype(BF16)


def make_target(pick, base, att, w_out, w_neck):
    return pl.pallas_call(
        target_kernel,
        out_shape=shape(128, 4, 256),
        compiler_params=params(),
        cost_estimate=cost(2 * 512 * 1280 * 1024, 6 * MIB),
        name="out_neck_target",
    )(pick, base, att, w_out, w_neck)


def forward_kernel(
    core_ref, rows_ref, w_expand_ref, w_project_ref, pred_ref, slope_ref, act_t_ref, rows_t_ref, token_ref
):
    token_ref[...] = jnp.zeros((8, 128), F32)
    step = pl.program_id(0)
    core = core_ref[0]
    rows = rows_ref[...]

    @pl.when(step == 0)
    def _():
        out_row = lax.broadcasted_iota(jnp.int32, (512, 512), 0)
        column = lax.broadcasted_iota(jnp.int32, (512, 512), 1)
        member = jnp.where(out_row < 256, core, 1 - core)
        wanted = (out_row % 256) // 4 * 8 + member * 4 + out_row % 4
        pick = (column == wanted).astype(F32).astype(BF16)
        rows_t_ref[...] = dot_t(pick, rows).astype(BF16)

    pre = dot(rows, w_expand_ref[...])
    square = pre * pre
    bend = jnp.tanh(GELU_A * pre * (1.0 + GELU_B * square))
    gate = 0.5 * (1.0 + bend)
    act = (pre * gate).astype(BF16)
    slope_ref[...] = gate + (0.5 * GELU_A) * pre * (1.0 - bend * bend) * (
        1.0 + (3.0 * GELU_B) * square
    )
    act_t = act.T
    for group in range(32):
        half = jnp.where(core == group % 2, 0, 1024)
        start = pl.multiple_of(half + (step * 16 + group // 2) * 16, 16)
        act_t_ref[pl.ds(start, 16), :] = act_t[group * 16 : group * 16 + 16, :]
    part = dot(act, w_project_ref[...])

    @pl.when(step == 0)
    def _():
        pred_ref[...] = part

    @pl.when(step > 0)
    def _():
        pred_ref[...] += part


def student_forward(core, rows, w_expand, w_project):
    whole = lambda i: (0, 0)
    return pl.pallas_call(
        forward_kernel,
        grid=(4,),
        in_specs=[
            pl.BlockSpec(memory_space=pltpu.SMEM),
            pl.BlockSpec((512, 512), whole),
            pl.BlockSpec((512, 512), lambda i: (0, i)),
            pl.BlockSpec((512, 256), lambda i: (i, 0)),
        ],
        out_specs=[
            pl.BlockSpec((512, 256), whole),
            pl.BlockSpec((512, 512), lambda i: (0, i)),
            pl.BlockSpec((2048, 512), whole),
            pl.BlockSpec((512, 512), whole),
            pl.BlockSpec((8, 128), whole),
        ],
        out_shape=(
            kept(512, 256, dtype=F32),
            kept(512, 2048, dtype=F32),
            kept(2048, 512),
            kept(512, 512),
            TOKEN,
        ),
        compiler_params=params(),
        cost_estimate=cost(1000, 1000),
        name="student_forward",
    )(core, rows, w_expand, w_project)


def error_kernel(pred_ref, moved_ref, act_t_ref, error_ref, d_pred_ref, project_ref):
    moved = moved_ref[...].astype(F32)
    moved = jnp.concatenate([moved[:64], moved[64:]], axis=1).reshape(512, 256)
    error = pred_ref[...] - moved
    error_ref[...] = error.astype(BF16)
    d_pred = (error * (1.0 / 512.0)).astype(BF16)
    d_pred_ref[...] = d_pred
    project_ref[...] = dot(act_t_ref[1024:, :], d_pred).astype(BF16)


def student_error(pred, moved, act_t):
    return pl.pallas_call(
        error_kernel,
        out_shape=(shape(512, 256), kept(512, 256), shape(1024, 256)),
        compiler_params=params(),
        cost_estimate=cost(1000, 1000),
        name="student_error",
    )(pred, moved, act_t)


def backward_kernel(side, d_pred_ref, slope_ref, w_project_ref, rows_t_ref, d_pre_ref, expand_ref):
    for i in range(2):
        part = slice(1024 * side + 512 * i, 1024 * side + 512 * i + 512)
        out = slice(512 * i, 512 * i + 512)
        d_act = dot_t(d_pred_ref[...], w_project_ref[part, :])
        d_pre = (slope_ref[:, part] * d_act).astype(BF16)
        d_pre_ref[:, out] = d_pre
        expand_ref[:, out] = dot(rows_t_ref[256:, :], d_pre).astype(BF16)


def student_backward(side, d_pred, slope, w_project, rows_t):
    return pl.pallas_call(
        functools.partial(backward_kernel, side),
        out_shape=(kept(512, 1024), shape(256, 1024)),
        compiler_params=params(),
        cost_estimate=cost(1000, 1000),
        name="student_backward",
    )(d_pred, slope, w_project, rows_t)


def own_kernel(
    d_pred_ref,
    d_pre0_ref,
    d_pre1_ref,
    act_t_ref,
    rows_t_ref,
    project_in_ref,
    expand0_in_ref,
    project_ref,
    expand_ref,
):
    project = dot(act_t_ref[:1024, :], d_pred_ref[...])
    project_ref[...] = (project + project_in_ref[...].astype(F32)).astype(BF16)
    for side, d_pre_ref in enumerate((d_pre0_ref, d_pre1_ref)):
        for i in range(2):
            part = slice(512 * i, 512 * i + 512)
            expand = dot(rows_t_ref[:256, :], d_pre_ref[:, part])
            if side == 0:
                expand = expand + expand0_in_ref[:, part].astype(F32)
            expand_ref[:, 1024 * side + 512 * i : 1024 * side + 512 * i + 512] = expand


def own_half(d_pred, d_pre0, d_pre1, act_t, rows_t, project_in, expand0_in):
    return pl.pallas_call(
        own_kernel,
        out_shape=(kept(1024, 256), kept(256, 2048, dtype=F32)),
        compiler_params=params(),
        cost_estimate=cost(10**11, 6 * MIB),
        name="own_half_gradients",
    )(d_pred, d_pre0, d_pre1, act_t, rows_t, project_in, expand0_in)


def pack_kernel(project_ref, expand_ref, expand1_in_ref, out_ref):
    row = lax.broadcasted_iota(jnp.int32, (256, 256), 0)
    column = lax.broadcasted_iota(jnp.int32, (256, 256), 1)
    wanted = row % 32 // 4 * 32 + row // 32 * 4 + row % 4
    order = (column == wanted).astype(F32).astype(BF16)
    for block in range(8):
        part = slice(32 * block, 32 * block + 32)
        columns = []
        for j in range(8):
            expand = expand_ref[part, 256 * j : 256 * j + 256]
            if j >= 4:
                arrived = expand1_in_ref[part, 256 * (j - 4) : 256 * (j - 4) + 256]
                expand = expand + arrived.astype(F32)
            columns.append(expand.astype(BF16))
        sorted_rows = dot(order, jnp.concatenate(columns, axis=0)).astype(BF16)
        for i in range(8):
            chip = 8 * block + i
            place = chip % 2 * 32 + chip // 8 % 2 * 16 + chip // 16 * 4 + chip // 2 % 4
            out_ref[place, :16, :] = project_ref[16 * chip : 16 * chip + 16, :]
            out_ref[place, 16:, :] = sorted_rows[32 * i : 32 * i + 32, :]


def pack(project, expand, expand1_in):
    return pl.pallas_call(
        pack_kernel,
        out_shape=shape(64, 48, 256),
        compiler_params=params(),
        cost_estimate=cost(2 * 256 * 256 * 256 * 8, 6 * MIB),
        name="pack_gradients",
    )(project, expand, expand1_in)


def finish_kernel(parts_ref, expand_ref, project_ref):
    total = jnp.sum(parts_ref[...].astype(F32), axis=0)
    project_ref[...] = total[:16, :]
    for j in range(8):
        expand_ref[:, 256 * j : 256 * j + 256] = total[16 + 4 * j : 20 + 4 * j, :]


def finish(parts):
    return pl.pallas_call(
        finish_kernel,
        out_shape=(shape(4, 2048, dtype=F32), shape(16, 256, dtype=F32)),
        compiler_params=params(),
        cost_estimate=cost(64 * 48 * 256, 2 * MIB),
        name="sum_gradients",
    )(parts)


def gate_kernel(value_ref, after_ref, out_ref):
    del value_ref, after_ref, out_ref


def gate(value, after):
    return pl.pallas_call(
        gate_kernel,
        in_specs=[pl.BlockSpec(memory_space=pl.ANY)] * 2,
        out_specs=pl.BlockSpec(memory_space=pl.ANY),
        out_shape=jax.ShapeDtypeStruct(value.shape, value.dtype),
        input_output_aliases={0: 0},
        compiler_params=params(1),
        cost_estimate=cost(10, 10),
        name="gate",
    )(value, after)


def swap(value, axis):
    return lax.ppermute(value, axis, [(0, 1), (1, 0)])


def per_device(
    tokens, w_query, w_key, w_value, w_out, w_neck, owner_table, student_in, w_expand, w_project
):
    core = lax.axis_index("c").astype(jnp.int32).reshape(1)
    normed, kv_first = first_project(in_hbm(tokens), in_hbm(w_key), in_hbm(w_value))
    far_first = swap(kv_first, "yh")
    near_first = swap(kv_first, "c")
    kv_second, query_first, query_second, kv_send = second_project(
        normed, in_hbm(w_key), in_hbm(w_value), in_hbm(w_query)
    )
    far_second = swap(kv_send, "yh")
    near_second = swap(kv_second, "c")
    pred, slope, act_t, rows_t, token = student_forward(
        core, in_hbm(student_in), in_hbm(w_expand), in_hbm(w_project)
    )
    far_first = gate(far_first, token)
    near, stats, pick, token = near_attention(
        query_second, (kv_second, near_second), owner_table
    )
    att_first, token = attention(
        query_first, (kv_first, near_first, far_first, swap(far_first, "c")), token
    )
    base, token = first_out(tokens, att_first, w_out, token)
    far_second = gate(far_second, token)
    last_second = swap(far_second, "c")
    near, stats = far_attention(query_second, far_second, near, stats, False)
    att_second = far_attention(query_second, last_second, near, stats, True)
    target = make_target(pick, base, att_second, w_out, w_neck)
    moved = lax.all_to_all(target, BY_CORE, split_axis=0, concat_axis=0, tiled=True)
    error, d_pred, project_out = student_error(pred, moved, act_t)
    project_in = swap(project_out, "c")
    d_pre0, expand0_out = student_backward(0, d_pred, slope, w_project, rows_t)
    expand0_in = swap(expand0_out, "c")
    d_pre1, expand1_out = student_backward(1, d_pred, slope, w_project, rows_t)
    expand1_in = swap(expand1_out, "c")
    project, expand = own_half(
        d_pred, d_pre0, d_pre1, act_t, rows_t, project_in, expand0_in
    )
    packed = pack(project, expand, expand1_in)
    parts = lax.all_to_all(packed, CHIPS, split_axis=0, concat_axis=0, tiled=True)
    grad_expand, grad_project = finish(parts)
    return (error, grad_expand, grad_project)


def solution(mesh):
    fine = Mesh(mesh.devices.reshape(4, 2, 4, 2, 2), AXES)
    rows = P(AXES, None)
    return jax.shard_map(
        per_device,
        mesh=fine,
        in_specs=(rows, P(), P(), P(), P(), P(), rows, rows, P(), P()),
        out_specs=(rows, rows, rows),
        check_vma=False,
    )
```

```python
import functools

import jax
import jax.numpy as jnp
from jax import lax
from jax.experimental import pallas as pl
from jax.experimental.pallas import tpu as pltpu
from jax.sharding import Mesh
from jax.sharding import PartitionSpec as P

HEAD = 80
HALF = 320
SCALE = HEAD**-0.5 * 1.4426950408889634
AXES = ("x", "yl", "z", "yh", "c")
CHIPS = ("yh", "yl", "x", "z")
BY_CORE = ("c", "x", "yl", "z", "yh")
GELU_A = 0.7978845608028654
GELU_B = 0.044715
F32 = jnp.float32
TOKEN = jax.ShapeDtypeStruct((8, 128), jnp.float32)
BF16 = jnp.bfloat16
MIB = 2**20


def dot(a, b):
    return jnp.dot(a, b, preferred_element_type=F32)


def dot_t(a, b):
    return lax.dot_general(a, b, (((1,), (1,)), ((), ())), preferred_element_type=F32)


def layer_norm(value):
    centred = value - jnp.mean(value, axis=-1, keepdims=True)
    spread = jnp.mean(centred * centred, axis=-1, keepdims=True)
    return centred * lax.rsqrt(spread + 1e-06)


def lanes(width, low, high):
    index = lax.broadcasted_iota(jnp.int32, (1, width), 1)
    return (index >= low) & (index < high)


def shape(*dims, dtype=BF16):
    return jax.ShapeDtypeStruct(dims, dtype)


def kept(*dims, dtype=BF16):
    return pltpu.VMEM(dims, dtype)


def in_hbm(value):
    return pltpu.with_memory_space_constraint(value, pltpu.HBM)


def params(mib=16):
    return pltpu.CompilerParams(vmem_limit_bytes=mib * MIB)


def cost(flops, moved, exps=0):
    return pl.CostEstimate(flops=flops, bytes_accessed=moved, transcendentals=exps)


def first_kernel(
    tokens_hbm,
    w_key_hbm,
    w_value_hbm,
    normed_ref,
    send_ref,
    tokens_ref,
    weights_ref,
    kv_ref,
    sems,
):
    copies = []
    for i in range(4):
        rows = pl.ds(128 * i, 128)
        copies.append((tokens_hbm.at[rows], tokens_ref.at[rows]))
    for side, source in enumerate((w_key_hbm, w_value_hbm)):
        for i in range(2):
            rows = pl.ds(640 * i, 640)
            target = weights_ref.at[rows, pl.ds(384 * side, 384)]
            copies.append((source.at[rows, pl.ds(0, 384)], target))
    copies = [
        pltpu.make_async_copy(source, target, sems.at[i])
        for i, (source, target) in enumerate(copies)
    ]
    for copy in copies:
        copy.start()
    for i in range(4):
        copies[i].wait()
        rows = pl.ds(128 * i, 128)
        normed_ref[rows, :] = layer_norm(tokens_ref[rows, :].astype(F32)).astype(BF16)
    for copy in copies[4:]:
        copy.wait()
    sends = []
    for i in range(2):
        rows = pl.ds(256 * i, 256)
        both = dot(normed_ref[rows, :], weights_ref[...])
        kv = jnp.concatenate([both[:, :HALF], both[:, 384 : 384 + HALF]], axis=1).astype(BF16)
        kv_ref[rows, :] = kv
        sends.append(pltpu.make_async_copy(kv_ref.at[rows], send_ref.at[rows], sems.at[8 + i]))
        sends[-1].start()
    for send in sends:
        send.wait()


def first_project(tokens, w_key, w_value):
    return pl.pallas_call(
        first_kernel,
        in_specs=[pl.BlockSpec(memory_space=pltpu.HBM)] * 3,
        out_specs=[pl.BlockSpec(memory_space=pltpu.VMEM), pl.BlockSpec(memory_space=pl.ANY)],
        out_shape=(kept(512, 1280), shape(512, 640)),
        scratch_shapes=[
            pltpu.VMEM((512, 1280), BF16),
            pltpu.VMEM((1280, 768), BF16),
            pltpu.VMEM((512, 640), BF16),
            pltpu.SemaphoreType.DMA((10,)),
        ],
        compiler_params=params(),
        cost_estimate=cost(2 * 512 * 1280 * 768, 6 * MIB),
        name="norm_kv_first",
    )(tokens, w_key, w_value)


def second_kernel(
    normed_ref, w_key_ref, w_value_ref, w_query_ref, kv_ref, q0_ref, q1_ref, send_ref, sems
):
    normed = normed_ref[...]
    keys = dot(normed, w_key_ref[:, 256:])
    values = dot(normed, w_value_ref[:, 256:])
    kv_ref[...] = jnp.concatenate([keys[:, 64:], values[:, 64:]], axis=1).astype(BF16)
    sends = (
        pltpu.make_async_copy(kv_ref, send_ref.at[pl.ds(0, 512)], sems.at[0]),
        pltpu.make_async_copy(kv_ref.at[pl.ds(0, 16)], send_ref.at[pl.ds(512, 16)], sems.at[1]),
    )
    for send in sends:
        send.start()
    query = dot(normed, w_query_ref[...])
    blank = jnp.zeros((512, 64), F32)
    q0_ref[...] = jnp.concatenate([query[:, :HALF], blank], axis=1).astype(BF16)
    q1_ref[...] = jnp.concatenate([query[:, HALF:], blank], axis=1).astype(BF16)
    for send in sends:
        send.wait()


def second_project(normed, w_key, w_value, w_query):
    return pl.pallas_call(
        second_kernel,
        out_specs=[pl.BlockSpec(memory_space=pltpu.VMEM)] * 3 + [pl.BlockSpec(memory_space=pl.ANY)],
        out_shape=(kept(512, 640), kept(512, 384), kept(512, 384), shape(528, 640)),
        scratch_shapes=[pltpu.SemaphoreType.DMA((2,))],
        compiler_params=params(),
        cost_estimate=cost(1000, 1000),
        name="kv_second_query",
    )(normed, w_key, w_value, w_query)


def masked_query(q_ref, head):
    key_at = 0 if head < 3 else 128
    low = HEAD * head - key_at
    return q_ref[:, key_at : key_at + 256] * lanes(256, low, low + HEAD).astype(F32).astype(BF16)


def wide(value, times):
    return jnp.concatenate([value] * times, axis=1)


def attend(q_ref, sources, head, floor=None):
    key_at = 0 if head < 3 else 128
    value_at = 256 if head < 2 else 384
    query = masked_query(q_ref, head)
    scores = [dot_t(query, kv[:512, key_at : key_at + 256]) for kv in sources]
    top = jnp.max(functools.reduce(jnp.maximum, scores), axis=1, keepdims=True)
    if floor is not None:
        top = jnp.maximum(jnp.broadcast_to(top, floor.shape), floor)
    shift = top if floor is None else wide(top, 4)
    probs = [jnp.exp2((part - shift) * SCALE) for part in scores]
    total = jnp.sum(functools.reduce(jnp.add, probs), axis=1, keepdims=True)
    weighed = sum(
        dot(part.astype(BF16), kv[:512, value_at : value_at + 256])
        for part, kv in zip(probs, sources)
    )
    return top, total, weighed


def side_by_side(mixed):
    low = jnp.where(
        lanes(256, 144, 256), mixed[1], jnp.where(lanes(256, 64, 144), mixed[0], 0.0)
    )
    high = jnp.where(lanes(256, 176, 256), mixed[3], mixed[2])
    middle = jnp.where(lanes(128, 0, 96), low[:, 128:], high[:, :128])
    return jnp.concatenate([low[:, :128], middle, high[:, 128:]], axis=1)


def attention_kernel(q_ref, kv0_ref, kv1_ref, kv2_ref, kv3_ref, after_ref, out_ref, token_ref):
    token_ref[...] = after_ref[...]
    sources = (kv0_ref, kv1_ref, kv2_ref, kv3_ref)
    mixed = []
    for head in range(4):
        _, total, weighed = attend(q_ref, sources, head)
        mixed.append(weighed / total)
    out_ref[...] = side_by_side(mixed).astype(BF16)


def attention(query, sources, after):
    return pl.pallas_call(
        attention_kernel,
        in_specs=[pl.BlockSpec(memory_space=pltpu.VMEM)] * 6,
        out_shape=(kept(512, 384), TOKEN),
        compiler_params=params(),
        cost_estimate=cost(1000, 1000),
        name="attention_four_heads",
    )(query, *sources, after)


def near_kernel(q_ref, kv0_ref, kv1_ref, owner_ref, mixed_ref, stats_ref, pick_ref, token_ref):
    token_ref[...] = jnp.zeros((8, 128), F32)
    block = lax.broadcasted_iota(jnp.int32, (128, 512), 0)
    source = lax.broadcasted_iota(jnp.int32, (128, 512), 1)
    spread = (source // 4 == block).astype(F32).astype(BF16)
    owner = jnp.broadcast_to(owner_ref[...].astype(F32), (8, 128)).astype(BF16)
    owner = dot(owner, spread)[:1, :].astype(jnp.int32)
    row = lax.broadcasted_iota(jnp.int32, (512, 512), 0)
    place = (owner % 2 * 64 + owner // 2) * 4 + lax.broadcasted_iota(jnp.int32, (1, 512), 1) % 4
    pick_ref[...] = (row == place).astype(F32).astype(BF16)
    mixed = []
    for head in range(4):
        top, total, weighed = attend(q_ref, (kv0_ref, kv1_ref), head)
        mixed.append(weighed)
        stats_ref[head] = jnp.broadcast_to(top, (512, 128))
        stats_ref[4 + head] = jnp.broadcast_to(total, (512, 128))
    mixed_ref[...] = side_by_side(mixed)


def near_attention(query, sources, owner_table):
    return pl.pallas_call(
        near_kernel,
        out_shape=(
            kept(512, 384, dtype=F32),
            kept(8, 512, 128, dtype=F32),
            kept(512, 512),
            TOKEN,
        ),
        compiler_params=params(),
        cost_estimate=cost(1000, 1000),
        name="attention_near_keys",
    )(query, *sources, owner_table)


def far_step(q_ref, kv_ref, near_ref, stats_ref, head, last):
    at = 0 if head < 2 else 128
    before = stats_ref[head]
    top, total, weighed = attend(q_ref, (kv_ref,), head, before)
    factor = jnp.exp2((before - top) * SCALE)
    total = total + factor * stats_ref[4 + head]
    if last:
        share = 1.0 / total
        weighed = wide(share, 2) * weighed
        factor = factor * share
    return top, total, weighed + wide(factor, 2) * near_ref[:, at : at + 256]


def far_kernel(q_ref, kv_ref, near_ref, stats_ref, out_ref, new_stats_ref):
    mixed = []
    for head in range(4):
        top, total, weighed = far_step(q_ref, kv_ref, near_ref, stats_ref, head, False)
        new_stats_ref[head] = top
        new_stats_ref[4 + head] = total
        mixed.append(weighed)
    out_ref[...] = side_by_side(mixed)


def far_attention(query, source, near, stats):
    return pl.pallas_call(
        far_kernel,
        out_shape=(kept(512, 384, dtype=F32), kept(8, 512, 128, dtype=F32)),
        compiler_params=params(),
        cost_estimate=cost(2 * 512 * 512 * 512 * 4, 2 * MIB, 4 * 512 * 512),
        name="attention_far_keys",
    )(query, source, near, stats)


def first_out_kernel(tokens_ref, att_ref, w_out_ref, after_ref, out_ref, token_ref):
    token_ref[...] = after_ref[...]
    top = jnp.concatenate([jnp.zeros((64, 1280), BF16), w_out_ref[:64, :]], axis=0)
    added = dot(att_ref[:, 128:], w_out_ref[64:HALF, :]) + dot(att_ref[:, :128], top)
    out_ref[...] = tokens_ref[...].astype(F32) + added


def first_out(tokens, att, w_out, after):
    return pl.pallas_call(
        first_out_kernel,
        out_shape=(kept(512, 1280, dtype=F32), TOKEN),
        compiler_params=params(),
        cost_estimate=cost(1000, 1000),
        name="first_heads_out",
    )(tokens, att, w_out, after)


def target_kernel(
    q_ref, kv_ref, near_ref, stats_ref, pick_ref, base_ref, w_out_ref, w_neck_ref, out_ref
):
    mixed = [far_step(q_ref, kv_ref, near_ref, stats_ref, head, True)[2] for head in range(4)]
    attended = side_by_side(mixed).astype(BF16)
    block_out = (base_ref[...] + dot(attended, w_out_ref[256:, :])).astype(BF16)
    target = layer_norm(dot(block_out, w_neck_ref[...])).astype(BF16)
    out_ref[...] = dot(pick_ref[...], target).reshape(128, 4, 256).astype(BF16)


def make_target(query, source, near, stats, pick, base, w_out, w_neck):
    return pl.pallas_call(
        target_kernel,
        out_shape=shape(128, 4, 256),
        compiler_params=params(),
        cost_estimate=cost(2 * 512 * 1280 * 1024, 6 * MIB),
        name="last_keys_target",
    )(query, source, near, stats, pick, base, w_out, w_neck)


def forward_kernel(
    core_ref, rows_ref, w_expand_ref, w_project_ref, pred_ref, slope_ref, act_t_ref, rows_t_ref, token_ref
):
    token_ref[...] = jnp.zeros((8, 128), F32)
    step = pl.program_id(0)
    core = core_ref[0]
    rows = rows_ref[...]

    @pl.when(step == 0)
    def _():
        out_row = lax.broadcasted_iota(jnp.int32, (512, 512), 0)
        column = lax.broadcasted_iota(jnp.int32, (512, 512), 1)
        member = jnp.where(out_row < 256, core, 1 - core)
        wanted = (out_row % 256) // 4 * 8 + member * 4 + out_row % 4
        pick = (column == wanted).astype(F32).astype(BF16)
        rows_t_ref[...] = dot_t(pick, rows).astype(BF16)

    pre = dot(rows, w_expand_ref[...])
    square = pre * pre
    bend = jnp.tanh(GELU_A * pre * (1.0 + GELU_B * square))
    gate = 0.5 * (1.0 + bend)
    act = (pre * gate).astype(BF16)
    slope_ref[...] = gate + (0.5 * GELU_A) * pre * (1.0 - bend * bend) * (
        1.0 + (3.0 * GELU_B) * square
    )
    act_t = act.T
    for group in range(32):
        half = jnp.where(core == group % 2, 0, 1024)
        start = pl.multiple_of(half + (step * 16 + group // 2) * 16, 16)
        act_t_ref[pl.ds(start, 16), :] = act_t[group * 16 : group * 16 + 16, :]
    part = dot(act, w_project_ref[...])

    @pl.when(step == 0)
    def _():
        pred_ref[...] = part

    @pl.when(step > 0)
    def _():
        pred_ref[...] += part


def student_forward(core, rows, w_expand, w_project):
    whole = lambda i: (0, 0)
    return pl.pallas_call(
        forward_kernel,
        grid=(4,),
        in_specs=[
            pl.BlockSpec(memory_space=pltpu.SMEM),
            pl.BlockSpec((512, 512), whole),
            pl.BlockSpec((512, 512), lambda i: (0, i)),
            pl.BlockSpec((512, 256), lambda i: (i, 0)),
        ],
        out_specs=[
            pl.BlockSpec((512, 256), whole),
            pl.BlockSpec((512, 512), lambda i: (0, i)),
            pl.BlockSpec((2048, 512), whole),
            pl.BlockSpec((512, 512), whole),
            pl.BlockSpec((8, 128), whole),
        ],
        out_shape=(
            kept(512, 256, dtype=F32),
            kept(512, 2048, dtype=F32),
            kept(2048, 512),
            kept(512, 512),
            TOKEN,
        ),
        compiler_params=params(),
        cost_estimate=cost(1000, 1000),
        name="student_forward",
    )(core, rows, w_expand, w_project)


def error_kernel(pred_ref, moved_ref, act_t_ref, error_ref, d_pred_ref, project_ref):
    moved = moved_ref[...].astype(F32)
    moved = jnp.concatenate([moved[:64], moved[64:]], axis=1).reshape(512, 256)
    error = pred_ref[...] - moved
    error_ref[...] = error.astype(BF16)
    d_pred = (error * (1.0 / 512.0)).astype(BF16)
    d_pred_ref[...] = d_pred
    project_ref[...] = dot(act_t_ref[1024:, :], d_pred).astype(BF16)


def student_error(pred, moved, act_t):
    return pl.pallas_call(
        error_kernel,
        out_shape=(shape(512, 256), kept(512, 256), shape(1024, 256)),
        compiler_params=params(),
        cost_estimate=cost(1000, 1000),
        name="student_error",
    )(pred, moved, act_t)


def backward_kernel(side, d_pred_ref, slope_ref, w_project_ref, rows_t_ref, d_pre_ref, expand_ref):
    for i in range(2):
        part = slice(1024 * side + 512 * i, 1024 * side + 512 * i + 512)
        out = slice(512 * i, 512 * i + 512)
        d_act = dot_t(d_pred_ref[...], w_project_ref[part, :])
        d_pre = (slope_ref[:, part] * d_act).astype(BF16)
        d_pre_ref[:, out] = d_pre
        expand_ref[:, out] = dot(rows_t_ref[256:, :], d_pre).astype(BF16)


def student_backward(side, d_pred, slope, w_project, rows_t):
    return pl.pallas_call(
        functools.partial(backward_kernel, side),
        out_shape=(kept(512, 1024), shape(256, 1024)),
        compiler_params=params(),
        cost_estimate=cost(1000, 1000),
        name="student_backward",
    )(d_pred, slope, w_project, rows_t)


def own_kernel(
    d_pred_ref,
    d_pre0_ref,
    d_pre1_ref,
    act_t_ref,
    rows_t_ref,
    project_in_ref,
    expand0_in_ref,
    project_ref,
    expand_ref,
):
    project = dot(act_t_ref[:1024, :], d_pred_ref[...])
    project_ref[...] = (project + project_in_ref[...].astype(F32)).astype(BF16)
    for side, d_pre_ref in enumerate((d_pre0_ref, d_pre1_ref)):
        for i in range(2):
            part = slice(512 * i, 512 * i + 512)
            expand = dot(rows_t_ref[:256, :], d_pre_ref[:, part])
            if side == 0:
                expand = expand + expand0_in_ref[:, part].astype(F32)
            expand_ref[:, 1024 * side + 512 * i : 1024 * side + 512 * i + 512] = expand


def own_half(d_pred, d_pre0, d_pre1, act_t, rows_t, project_in, expand0_in):
    return pl.pallas_call(
        own_kernel,
        out_shape=(kept(1024, 256), kept(256, 2048, dtype=F32)),
        compiler_params=params(),
        cost_estimate=cost(10**11, 6 * MIB),
        name="own_half_gradients",
    )(d_pred, d_pre0, d_pre1, act_t, rows_t, project_in, expand0_in)


def pack_kernel(project_ref, expand_ref, expand1_in_ref, out_ref):
    row = lax.broadcasted_iota(jnp.int32, (256, 256), 0)
    column = lax.broadcasted_iota(jnp.int32, (256, 256), 1)
    wanted = row % 32 // 4 * 32 + row // 32 * 4 + row % 4
    order = (column == wanted).astype(F32).astype(BF16)
    for block in range(8):
        part = slice(32 * block, 32 * block + 32)
        columns = []
        for j in range(8):
            expand = expand_ref[part, 256 * j : 256 * j + 256]
            if j >= 4:
                arrived = expand1_in_ref[part, 256 * (j - 4) : 256 * (j - 4) + 256]
                expand = expand + arrived.astype(F32)
            columns.append(expand.astype(BF16))
        sorted_rows = dot(order, jnp.concatenate(columns, axis=0)).astype(BF16)
        for i in range(8):
            chip = 8 * block + i
            place = chip % 2 * 32 + chip // 8 % 2 * 16 + chip // 16 * 4 + chip // 2 % 4
            out_ref[place, :16, :] = project_ref[16 * chip : 16 * chip + 16, :]
            out_ref[place, 16:, :] = sorted_rows[32 * i : 32 * i + 32, :]


def pack(project, expand, expand1_in):
    return pl.pallas_call(
        pack_kernel,
        out_shape=shape(64, 48, 256),
        compiler_params=params(),
        cost_estimate=cost(2 * 256 * 256 * 256 * 8, 6 * MIB),
        name="pack_gradients",
    )(project, expand, expand1_in)


def finish_kernel(parts_ref, expand_ref, project_ref):
    total = jnp.sum(parts_ref[...].astype(F32), axis=0)
    project_ref[...] = total[:16, :]
    for j in range(8):
        expand_ref[:, 256 * j : 256 * j + 256] = total[16 + 4 * j : 20 + 4 * j, :]


def finish(parts):
    return pl.pallas_call(
        finish_kernel,
        out_shape=(shape(4, 2048, dtype=F32), shape(16, 256, dtype=F32)),
        compiler_params=params(),
        cost_estimate=cost(64 * 48 * 256, 2 * MIB),
        name="sum_gradients",
    )(parts)


def gate_kernel(value_ref, after_ref, out_ref):
    del value_ref, after_ref, out_ref


def gate(value, after):
    return pl.pallas_call(
        gate_kernel,
        in_specs=[pl.BlockSpec(memory_space=pl.ANY)] * 2,
        out_specs=pl.BlockSpec(memory_space=pl.ANY),
        out_shape=jax.ShapeDtypeStruct(value.shape, value.dtype),
        input_output_aliases={0: 0},
        compiler_params=params(1),
        cost_estimate=cost(10, 10),
        name="gate",
    )(value, after)


def swap(value, axis):
    return lax.ppermute(value, axis, [(0, 1), (1, 0)])


def per_device(
    tokens, w_query, w_key, w_value, w_out, w_neck, owner_table, student_in, w_expand, w_project
):
    core = lax.axis_index("c").astype(jnp.int32).reshape(1)
    normed, kv_first = first_project(in_hbm(tokens), in_hbm(w_key), in_hbm(w_value))
    far_first = swap(kv_first, "yh")
    near_first = swap(kv_first, "c")
    kv_second, query_first, query_second, kv_send = second_project(
        normed, in_hbm(w_key), in_hbm(w_value), in_hbm(w_query)
    )
    far_second = swap(kv_send, "yh")
    near_second = swap(kv_second, "c")
    pred, slope, act_t, rows_t, token = student_forward(
        core, in_hbm(student_in), in_hbm(w_expand), in_hbm(w_project)
    )
    far_first = gate(far_first, token)
    near, stats, pick, token = near_attention(
        query_second, (kv_second, near_second), owner_table
    )
    att_first, token = attention(
        query_first, (kv_first, near_first, far_first, swap(far_first, "c")), token
    )
    base, token = first_out(tokens, att_first, w_out, token)
    far_second = gate(far_second, token)
    last_second = swap(far_second, "c")
    near, stats = far_attention(query_second, far_second, near, stats)
    target = make_target(query_second, last_second, near, stats, pick, base, w_out, w_neck)
    moved = lax.all_to_all(target, BY_CORE, split_axis=0, concat_axis=0, tiled=True)
    error, d_pred, project_out = student_error(pred, moved, act_t)
    project_in = swap(project_out, "c")
    d_pre0, expand0_out = student_backward(0, d_pred, slope, w_project, rows_t)
    expand0_in = swap(expand0_out, "c")
    d_pre1, expand1_out = student_backward(1, d_pred, slope, w_project, rows_t)
    expand1_in = swap(expand1_out, "c")
    project, expand = own_half(
        d_pred, d_pre0, d_pre1, act_t, rows_t, project_in, expand0_in
    )
    packed = pack(project, expand, expand1_in)
    parts = lax.all_to_all(packed, CHIPS, split_axis=0, concat_axis=0, tiled=True)
    grad_expand, grad_project = finish(parts)
    return (error, grad_expand, grad_project)


def solution(mesh):
    fine = Mesh(mesh.devices.reshape(4, 2, 4, 2, 2), AXES)
    rows = P(AXES, None)
    return jax.shard_map(
        per_device,
        mesh=fine,
        in_specs=(rows, P(), P(), P(), P(), P(), rows, rows, P(), P()),
        out_specs=(rows, rows, rows),
        check_vma=False,
    )
```

```python
import functools

import jax
import jax.numpy as jnp
from jax import lax
from jax.experimental import pallas as pl
from jax.experimental.pallas import tpu as pltpu
from jax.sharding import Mesh
from jax.sharding import PartitionSpec as P

HEAD = 80
HALF = 320
SCALE = HEAD**-0.5 * 1.4426950408889634
AXES = ("x", "yl", "z", "yh", "c")
CHIPS = ("yh", "yl", "x", "z")
BY_CORE = ("c", "x", "yl", "z", "yh")
GELU_A = 0.7978845608028654
GELU_B = 0.044715
F32 = jnp.float32
TOKEN = jax.ShapeDtypeStruct((8, 128), jnp.float32)
BF16 = jnp.bfloat16
MIB = 2**20


def dot(a, b):
    return jnp.dot(a, b, preferred_element_type=F32)


def dot_t(a, b):
    return lax.dot_general(a, b, (((1,), (1,)), ((), ())), preferred_element_type=F32)


def layer_norm(value):
    centred = value - jnp.mean(value, axis=-1, keepdims=True)
    spread = jnp.mean(centred * centred, axis=-1, keepdims=True)
    return centred * lax.rsqrt(spread + 1e-06)


def lanes(width, low, high):
    index = lax.broadcasted_iota(jnp.int32, (1, width), 1)
    return (index >= low) & (index < high)


def shape(*dims, dtype=BF16):
    return jax.ShapeDtypeStruct(dims, dtype)


def kept(*dims, dtype=BF16):
    return pltpu.VMEM(dims, dtype)


def in_hbm(value):
    return pltpu.with_memory_space_constraint(value, pltpu.HBM)


def params(mib=16):
    return pltpu.CompilerParams(vmem_limit_bytes=mib * MIB)


def cost(flops, moved, exps=0):
    return pl.CostEstimate(flops=flops, bytes_accessed=moved, transcendentals=exps)


def first_kernel(
    tokens_hbm,
    w_key_hbm,
    w_value_hbm,
    normed_ref,
    send_ref,
    tokens_ref,
    weights_ref,
    kv_ref,
    sems,
):
    copies = []
    for i in range(4):
        rows = pl.ds(128 * i, 128)
        copies.append((tokens_hbm.at[rows], tokens_ref.at[rows]))
    for side, source in enumerate((w_key_hbm, w_value_hbm)):
        for i in range(2):
            rows = pl.ds(640 * i, 640)
            target = weights_ref.at[rows, pl.ds(384 * side, 384)]
            copies.append((source.at[rows, pl.ds(0, 384)], target))
    copies = [
        pltpu.make_async_copy(source, target, sems.at[i])
        for i, (source, target) in enumerate(copies)
    ]
    for copy in copies:
        copy.start()
    for i in range(4):
        copies[i].wait()
        rows = pl.ds(128 * i, 128)
        normed_ref[rows, :] = layer_norm(tokens_ref[rows, :].astype(F32)).astype(BF16)
    for copy in copies[4:]:
        copy.wait()
    sends = []
    for i in range(4):
        rows = pl.ds(128 * i, 128)
        both = dot(normed_ref[rows, :], weights_ref[...])
        kv = jnp.concatenate([both[:, :HALF], both[:, 384 : 384 + HALF]], axis=1).astype(BF16)
        kv_ref[rows, :] = kv
        sends.append(pltpu.make_async_copy(kv_ref.at[rows], send_ref.at[rows], sems.at[8 + i]))
        sends[-1].start()
    for send in sends:
        send.wait()


def first_project(tokens, w_key, w_value):
    return pl.pallas_call(
        first_kernel,
        in_specs=[pl.BlockSpec(memory_space=pltpu.HBM)] * 3,
        out_specs=[pl.BlockSpec(memory_space=pltpu.VMEM), pl.BlockSpec(memory_space=pl.ANY)],
        out_shape=(kept(512, 1280), shape(512, 640)),
        scratch_shapes=[
            pltpu.VMEM((512, 1280), BF16),
            pltpu.VMEM((1280, 768), BF16),
            pltpu.VMEM((512, 640), BF16),
            pltpu.SemaphoreType.DMA((12,)),
        ],
        compiler_params=params(),
        cost_estimate=cost(2 * 512 * 1280 * 768, 6 * MIB),
        name="norm_kv_first",
    )(tokens, w_key, w_value)


def second_kernel(
    normed_ref, w_key_ref, w_value_ref, w_query_ref, kv_ref, q0_ref, q1_ref, send_ref, sems
):
    normed = normed_ref[...]
    keys = dot(normed, w_key_ref[:, 256:])
    values = dot(normed, w_value_ref[:, 256:])
    kv_ref[...] = jnp.concatenate([keys[:, 64:], values[:, 64:]], axis=1).astype(BF16)
    sends = (
        pltpu.make_async_copy(kv_ref, send_ref.at[pl.ds(0, 512)], sems.at[0]),
        pltpu.make_async_copy(kv_ref.at[pl.ds(0, 16)], send_ref.at[pl.ds(512, 16)], sems.at[1]),
    )
    for send in sends:
        send.start()
    query = dot(normed, w_query_ref[...])
    blank = jnp.zeros((512, 64), F32)
    q0_ref[...] = jnp.concatenate([query[:, :HALF], blank], axis=1).astype(BF16)
    q1_ref[...] = jnp.concatenate([query[:, HALF:], blank], axis=1).astype(BF16)
    for send in sends:
        send.wait()


def second_project(normed, w_key, w_value, w_query):
    return pl.pallas_call(
        second_kernel,
        out_specs=[pl.BlockSpec(memory_space=pltpu.VMEM)] * 3 + [pl.BlockSpec(memory_space=pl.ANY)],
        out_shape=(kept(512, 640), kept(512, 384), kept(512, 384), shape(528, 640)),
        scratch_shapes=[pltpu.SemaphoreType.DMA((2,))],
        compiler_params=params(),
        cost_estimate=cost(1000, 1000),
        name="kv_second_query",
    )(normed, w_key, w_value, w_query)


def masked_query(q_ref, head):
    key_at = 0 if head < 3 else 128
    low = HEAD * head - key_at
    return q_ref[:, key_at : key_at + 256] * lanes(256, low, low + HEAD).astype(F32).astype(BF16)


def wide(value, times):
    return jnp.concatenate([value] * times, axis=1)


def attend(q_ref, sources, head, floor=None):
    key_at = 0 if head < 3 else 128
    value_at = 256 if head < 2 else 384
    query = masked_query(q_ref, head)
    scores = [dot_t(query, kv[:512, key_at : key_at + 256]) for kv in sources]
    top = jnp.max(functools.reduce(jnp.maximum, scores), axis=1, keepdims=True)
    if floor is not None:
        top = jnp.maximum(jnp.broadcast_to(top, floor.shape), floor)
    shift = top if floor is None else wide(top, 4)
    probs = [jnp.exp2((part - shift) * SCALE) for part in scores]
    total = jnp.sum(functools.reduce(jnp.add, probs), axis=1, keepdims=True)
    weighed = sum(
        dot(part.astype(BF16), kv[:512, value_at : value_at + 256])
        for part, kv in zip(probs, sources)
    )
    return top, total, weighed


def side_by_side(mixed):
    low = jnp.where(
        lanes(256, 144, 256), mixed[1], jnp.where(lanes(256, 64, 144), mixed[0], 0.0)
    )
    high = jnp.where(lanes(256, 176, 256), mixed[3], mixed[2])
    middle = jnp.where(lanes(128, 0, 96), low[:, 128:], high[:, :128])
    return jnp.concatenate([low[:, :128], middle, high[:, 128:]], axis=1)


def attention_kernel(q_ref, kv0_ref, kv1_ref, kv2_ref, kv3_ref, after_ref, out_ref, token_ref):
    token_ref[...] = after_ref[...]
    sources = (kv0_ref, kv1_ref, kv2_ref, kv3_ref)
    mixed = []
    for head in range(4):
        _, total, weighed = attend(q_ref, sources, head)
        mixed.append(weighed / total)
    out_ref[...] = side_by_side(mixed).astype(BF16)


def attention(query, sources, after):
    return pl.pallas_call(
        attention_kernel,
        in_specs=[pl.BlockSpec(memory_space=pltpu.VMEM)] * 6,
        out_shape=(kept(512, 384), TOKEN),
        compiler_params=params(),
        cost_estimate=cost(1000, 1000),
        name="attention_four_heads",
    )(query, *sources, after)


def near_kernel(q_ref, kv0_ref, kv1_ref, owner_ref, mixed_ref, stats_ref, pick_ref, token_ref):
    token_ref[...] = jnp.zeros((8, 128), F32)
    block = lax.broadcasted_iota(jnp.int32, (128, 512), 0)
    source = lax.broadcasted_iota(jnp.int32, (128, 512), 1)
    spread = (source // 4 == block).astype(F32).astype(BF16)
    owner = jnp.broadcast_to(owner_ref[...].astype(F32), (8, 128)).astype(BF16)
    owner = dot(owner, spread)[:1, :].astype(jnp.int32)
    row = lax.broadcasted_iota(jnp.int32, (512, 512), 0)
    place = (owner % 2 * 64 + owner // 2) * 4 + lax.broadcasted_iota(jnp.int32, (1, 512), 1) % 4
    pick_ref[...] = (row == place).astype(F32).astype(BF16)
    mixed = []
    for head in range(4):
        top, total, weighed = attend(q_ref, (kv0_ref, kv1_ref), head)
        mixed.append(weighed)
        stats_ref[head] = jnp.broadcast_to(top, (512, 128))
        stats_ref[4 + head] = jnp.broadcast_to(total, (512, 128))
    mixed_ref[...] = side_by_side(mixed)


def near_attention(query, sources, owner_table):
    return pl.pallas_call(
        near_kernel,
        out_shape=(
            kept(512, 384, dtype=F32),
            kept(8, 512, 128, dtype=F32),
            kept(512, 512),
            TOKEN,
        ),
        compiler_params=params(),
        cost_estimate=cost(1000, 1000),
        name="attention_near_keys",
    )(query, *sources, owner_table)


def far_step(q_ref, kv_ref, near_ref, stats_ref, head, last):
    at = 0 if head < 2 else 128
    before = stats_ref[head]
    top, total, weighed = attend(q_ref, (kv_ref,), head, before)
    factor = jnp.exp2((before - top) * SCALE)
    total = total + factor * stats_ref[4 + head]
    if last:
        share = 1.0 / total
        weighed = wide(share, 2) * weighed
        factor = factor * share
    return top, total, weighed + wide(factor, 2) * near_ref[:, at : at + 256]


def far_kernel(q_ref, kv_ref, near_ref, stats_ref, out_ref, new_stats_ref):
    mixed = []
    for head in range(4):
        top, total, weighed = far_step(q_ref, kv_ref, near_ref, stats_ref, head, False)
        new_stats_ref[head] = top
        new_stats_ref[4 + head] = total
        mixed.append(weighed)
    out_ref[...] = side_by_side(mixed)


def far_attention(query, source, near, stats):
    return pl.pallas_call(
        far_kernel,
        out_shape=(kept(512, 384, dtype=F32), kept(8, 512, 128, dtype=F32)),
        compiler_params=params(),
        cost_estimate=cost(2 * 512 * 512 * 512 * 4, 2 * MIB, 4 * 512 * 512),
        name="attention_far_keys",
    )(query, source, near, stats)


def first_out_kernel(tokens_ref, att_ref, w_out_ref, after_ref, out_ref, token_ref):
    token_ref[...] = after_ref[...]
    top = jnp.concatenate([jnp.zeros((64, 1280), BF16), w_out_ref[:64, :]], axis=0)
    added = dot(att_ref[:, 128:], w_out_ref[64:HALF, :]) + dot(att_ref[:, :128], top)
    out_ref[...] = tokens_ref[...].astype(F32) + added


def first_out(tokens, att, w_out, after):
    return pl.pallas_call(
        first_out_kernel,
        out_shape=(kept(512, 1280, dtype=F32), TOKEN),
        compiler_params=params(),
        cost_estimate=cost(1000, 1000),
        name="first_heads_out",
    )(tokens, att, w_out, after)


def target_kernel(
    q_ref, kv_ref, near_ref, stats_ref, pick_ref, base_ref, w_out_ref, w_neck_ref, out_ref
):
    mixed = [far_step(q_ref, kv_ref, near_ref, stats_ref, head, True)[2] for head in range(4)]
    attended = side_by_side(mixed).astype(BF16)
    block_out = (base_ref[...] + dot(attended, w_out_ref[256:, :])).astype(BF16)
    target = layer_norm(dot(block_out, w_neck_ref[...])).astype(BF16)
    out_ref[...] = dot(pick_ref[...], target).reshape(128, 4, 256).astype(BF16)


def make_target(query, source, near, stats, pick, base, w_out, w_neck):
    return pl.pallas_call(
        target_kernel,
        out_shape=shape(128, 4, 256),
        compiler_params=params(),
        cost_estimate=cost(2 * 512 * 1280 * 1024, 6 * MIB),
        name="last_keys_target",
    )(query, source, near, stats, pick, base, w_out, w_neck)


def forward_kernel(
    core_ref, rows_ref, w_expand_ref, w_project_ref, pred_ref, slope_ref, act_t_ref, rows_t_ref, token_ref
):
    token_ref[...] = jnp.zeros((8, 128), F32)
    step = pl.program_id(0)
    core = core_ref[0]
    rows = rows_ref[...]

    @pl.when(step == 0)
    def _():
        out_row = lax.broadcasted_iota(jnp.int32, (512, 512), 0)
        column = lax.broadcasted_iota(jnp.int32, (512, 512), 1)
        member = jnp.where(out_row < 256, core, 1 - core)
        wanted = (out_row % 256) // 4 * 8 + member * 4 + out_row % 4
        pick = (column == wanted).astype(F32).astype(BF16)
        rows_t_ref[...] = dot_t(pick, rows).astype(BF16)

    pre = dot(rows, w_expand_ref[...])
    square = pre * pre
    bend = jnp.tanh(GELU_A * pre * (1.0 + GELU_B * square))
    gate = 0.5 * (1.0 + bend)
    act = (pre * gate).astype(BF16)
    slope_ref[...] = gate + (0.5 * GELU_A) * pre * (1.0 - bend * bend) * (
        1.0 + (3.0 * GELU_B) * square
    )
    act_t = act.T
    for group in range(32):
        half = jnp.where(core == group % 2, 0, 1024)
        start = pl.multiple_of(half + (step * 16 + group // 2) * 16, 16)
        act_t_ref[pl.ds(start, 16), :] = act_t[group * 16 : group * 16 + 16, :]
    part = dot(act, w_project_ref[...])

    @pl.when(step == 0)
    def _():
        pred_ref[...] = part

    @pl.when(step > 0)
    def _():
        pred_ref[...] += part


def student_forward(core, rows, w_expand, w_project):
    whole = lambda i: (0, 0)
    return pl.pallas_call(
        forward_kernel,
        grid=(4,),
        in_specs=[
            pl.BlockSpec(memory_space=pltpu.SMEM),
            pl.BlockSpec((512, 512), whole),
            pl.BlockSpec((512, 512), lambda i: (0, i)),
            pl.BlockSpec((512, 256), lambda i: (i, 0)),
        ],
        out_specs=[
            pl.BlockSpec((512, 256), whole),
            pl.BlockSpec((512, 512), lambda i: (0, i)),
            pl.BlockSpec((2048, 512), whole),
            pl.BlockSpec((512, 512), whole),
            pl.BlockSpec((8, 128), whole),
        ],
        out_shape=(
            kept(512, 256, dtype=F32),
            kept(512, 2048, dtype=F32),
            kept(2048, 512),
            kept(512, 512),
            TOKEN,
        ),
        compiler_params=params(),
        cost_estimate=cost(1000, 1000),
        name="student_forward",
    )(core, rows, w_expand, w_project)


def error_kernel(pred_ref, moved_ref, act_t_ref, error_ref, d_pred_ref, project_ref):
    moved = moved_ref[...].astype(F32)
    moved = jnp.concatenate([moved[:64], moved[64:]], axis=1).reshape(512, 256)
    error = pred_ref[...] - moved
    error_ref[...] = error.astype(BF16)
    d_pred = (error * (1.0 / 512.0)).astype(BF16)
    d_pred_ref[...] = d_pred
    project_ref[...] = dot(act_t_ref[1024:, :], d_pred).astype(BF16)


def student_error(pred, moved, act_t):
    return pl.pallas_call(
        error_kernel,
        out_shape=(shape(512, 256), kept(512, 256), shape(1024, 256)),
        compiler_params=params(),
        cost_estimate=cost(1000, 1000),
        name="student_error",
    )(pred, moved, act_t)


def backward_kernel(side, d_pred_ref, slope_ref, w_project_ref, rows_t_ref, d_pre_ref, expand_ref):
    for i in range(2):
        part = slice(1024 * side + 512 * i, 1024 * side + 512 * i + 512)
        out = slice(512 * i, 512 * i + 512)
        d_act = dot_t(d_pred_ref[...], w_project_ref[part, :])
        d_pre = (slope_ref[:, part] * d_act).astype(BF16)
        d_pre_ref[:, out] = d_pre
        expand_ref[:, out] = dot(rows_t_ref[256:, :], d_pre).astype(BF16)


def student_backward(side, d_pred, slope, w_project, rows_t):
    return pl.pallas_call(
        functools.partial(backward_kernel, side),
        out_shape=(kept(512, 1024), shape(256, 1024)),
        compiler_params=params(),
        cost_estimate=cost(1000, 1000),
        name="student_backward",
    )(d_pred, slope, w_project, rows_t)


def own_kernel(
    d_pred_ref,
    d_pre0_ref,
    d_pre1_ref,
    act_t_ref,
    rows_t_ref,
    project_in_ref,
    expand0_in_ref,
    project_ref,
    expand_ref,
):
    project = dot(act_t_ref[:1024, :], d_pred_ref[...])
    project_ref[...] = (project + project_in_ref[...].astype(F32)).astype(BF16)
    for side, d_pre_ref in enumerate((d_pre0_ref, d_pre1_ref)):
        for i in range(2):
            part = slice(512 * i, 512 * i + 512)
            expand = dot(rows_t_ref[:256, :], d_pre_ref[:, part])
            if side == 0:
                expand = expand + expand0_in_ref[:, part].astype(F32)
            expand_ref[:, 1024 * side + 512 * i : 1024 * side + 512 * i + 512] = expand


def own_half(d_pred, d_pre0, d_pre1, act_t, rows_t, project_in, expand0_in):
    return pl.pallas_call(
        own_kernel,
        out_shape=(kept(1024, 256), kept(256, 2048, dtype=F32)),
        compiler_params=params(),
        cost_estimate=cost(10**11, 6 * MIB),
        name="own_half_gradients",
    )(d_pred, d_pre0, d_pre1, act_t, rows_t, project_in, expand0_in)


def pack_kernel(project_ref, expand_ref, expand1_in_ref, out_ref):
    row = lax.broadcasted_iota(jnp.int32, (256, 256), 0)
    column = lax.broadcasted_iota(jnp.int32, (256, 256), 1)
    wanted = row % 32 // 4 * 32 + row // 32 * 4 + row % 4
    order = (column == wanted).astype(F32).astype(BF16)
    for block in range(8):
        part = slice(32 * block, 32 * block + 32)
        columns = []
        for j in range(8):
            expand = expand_ref[part, 256 * j : 256 * j + 256]
            if j >= 4:
                arrived = expand1_in_ref[part, 256 * (j - 4) : 256 * (j - 4) + 256]
                expand = expand + arrived.astype(F32)
            columns.append(expand.astype(BF16))
        sorted_rows = dot(order, jnp.concatenate(columns, axis=0)).astype(BF16)
        for i in range(8):
            chip = 8 * block + i
            place = chip % 2 * 32 + chip // 8 % 2 * 16 + chip // 16 * 4 + chip // 2 % 4
            out_ref[place, :16, :] = project_ref[16 * chip : 16 * chip + 16, :]
            out_ref[place, 16:, :] = sorted_rows[32 * i : 32 * i + 32, :]


def pack(project, expand, expand1_in):
    return pl.pallas_call(
        pack_kernel,
        out_shape=shape(64, 48, 256),
        compiler_params=params(),
        cost_estimate=cost(2 * 256 * 256 * 256 * 8, 6 * MIB),
        name="pack_gradients",
    )(project, expand, expand1_in)


def finish_kernel(parts_ref, expand_ref, project_ref):
    total = jnp.sum(parts_ref[...].astype(F32), axis=0)
    project_ref[...] = total[:16, :]
    for j in range(8):
        expand_ref[:, 256 * j : 256 * j + 256] = total[16 + 4 * j : 20 + 4 * j, :]


def finish(parts):
    return pl.pallas_call(
        finish_kernel,
        out_shape=(shape(4, 2048, dtype=F32), shape(16, 256, dtype=F32)),
        compiler_params=params(),
        cost_estimate=cost(64 * 48 * 256, 2 * MIB),
        name="sum_gradients",
    )(parts)


def gate_kernel(value_ref, after_ref, out_ref):
    del value_ref, after_ref, out_ref


def gate(value, after):
    return pl.pallas_call(
        gate_kernel,
        in_specs=[pl.BlockSpec(memory_space=pl.ANY)] * 2,
        out_specs=pl.BlockSpec(memory_space=pl.ANY),
        out_shape=jax.ShapeDtypeStruct(value.shape, value.dtype),
        input_output_aliases={0: 0},
        compiler_params=params(1),
        cost_estimate=cost(10, 10),
        name="gate",
    )(value, after)


def swap(value, axis):
    return lax.ppermute(value, axis, [(0, 1), (1, 0)])


def per_device(
    tokens, w_query, w_key, w_value, w_out, w_neck, owner_table, student_in, w_expand, w_project
):
    core = lax.axis_index("c").astype(jnp.int32).reshape(1)
    normed, kv_first = first_project(in_hbm(tokens), in_hbm(w_key), in_hbm(w_value))
    far_first = swap(kv_first, "yh")
    near_first = swap(kv_first, "c")
    kv_second, query_first, query_second, kv_send = second_project(
        normed, in_hbm(w_key), in_hbm(w_value), in_hbm(w_query)
    )
    far_second = swap(kv_send, "yh")
    near_second = swap(kv_second, "c")
    pred, slope, act_t, rows_t, token = student_forward(
        core, in_hbm(student_in), in_hbm(w_expand), in_hbm(w_project)
    )
    far_first = gate(far_first, token)
    near, stats, pick, token = near_attention(
        query_second, (kv_second, near_second), owner_table
    )
    att_first, token = attention(
        query_first, (kv_first, near_first, far_first, swap(far_first, "c")), token
    )
    base, token = first_out(tokens, att_first, w_out, token)
    far_second = gate(far_second, token)
    last_second = swap(far_second, "c")
    near, stats = far_attention(query_second, far_second, near, stats)
    target = make_target(query_second, last_second, near, stats, pick, base, w_out, w_neck)
    moved = lax.all_to_all(target, BY_CORE, split_axis=0, concat_axis=0, tiled=True)
    error, d_pred, project_out = student_error(pred, moved, act_t)
    project_in = swap(project_out, "c")
    d_pre0, expand0_out = student_backward(0, d_pred, slope, w_project, rows_t)
    expand0_in = swap(expand0_out, "c")
    d_pre1, expand1_out = student_backward(1, d_pred, slope, w_project, rows_t)
    expand1_in = swap(expand1_out, "c")
    project, expand = own_half(
        d_pred, d_pre0, d_pre1, act_t, rows_t, project_in, expand0_in
    )
    packed = pack(project, expand, expand1_in)
    parts = lax.all_to_all(packed, CHIPS, split_axis=0, concat_axis=0, tiled=True)
    grad_expand, grad_project = finish(parts)
    return (error, grad_expand, grad_project)


def solution(mesh):
    fine = Mesh(mesh.devices.reshape(4, 2, 4, 2, 2), AXES)
    rows = P(AXES, None)
    return jax.shard_map(
        per_device,
        mesh=fine,
        in_specs=(rows, P(), P(), P(), P(), P(), rows, rows, P(), P()),
        out_specs=(rows, rows, rows),
        check_vma=False,
    )
```

```python
import functools

import jax
import jax.numpy as jnp
from jax import lax
from jax.experimental import pallas as pl
from jax.experimental.pallas import tpu as pltpu
from jax.sharding import Mesh
from jax.sharding import PartitionSpec as P

HEAD = 80
HALF = 320
SCALE = HEAD**-0.5 * 1.4426950408889634
AXES = ("x", "yl", "z", "yh", "c")
CHIPS = ("yh", "yl", "x", "z")
BY_CORE = ("c", "x", "yl", "z", "yh")
GELU_A = 0.7978845608028654
GELU_B = 0.044715
F32 = jnp.float32
TOKEN = jax.ShapeDtypeStruct((8, 128), jnp.float32)
BF16 = jnp.bfloat16
MIB = 2**20


def dot(a, b):
    return jnp.dot(a, b, preferred_element_type=F32)


def dot_t(a, b):
    return lax.dot_general(a, b, (((1,), (1,)), ((), ())), preferred_element_type=F32)


def layer_norm(value):
    centred = value - jnp.mean(value, axis=-1, keepdims=True)
    spread = jnp.mean(centred * centred, axis=-1, keepdims=True)
    return centred * lax.rsqrt(spread + 1e-06)


def lanes(width, low, high):
    index = lax.broadcasted_iota(jnp.int32, (1, width), 1)
    return (index >= low) & (index < high)


def shape(*dims, dtype=BF16):
    return jax.ShapeDtypeStruct(dims, dtype)


def kept(*dims, dtype=BF16):
    return pltpu.VMEM(dims, dtype)


def in_hbm(value):
    return pltpu.with_memory_space_constraint(value, pltpu.HBM)


def params(mib=16):
    return pltpu.CompilerParams(vmem_limit_bytes=mib * MIB)


def cost(flops, moved, exps=0):
    return pl.CostEstimate(flops=flops, bytes_accessed=moved, transcendentals=exps)


def first_kernel(
    tokens_hbm,
    w_key_hbm,
    w_value_hbm,
    normed_ref,
    send_ref,
    tokens_ref,
    weights_ref,
    kv_ref,
    sems,
):
    copies = []
    for i in range(4):
        rows = pl.ds(128 * i, 128)
        copies.append((tokens_hbm.at[rows], tokens_ref.at[rows]))
    for side, source in enumerate((w_key_hbm, w_value_hbm)):
        for i in range(2):
            rows = pl.ds(640 * i, 640)
            target = weights_ref.at[rows, pl.ds(384 * side, 384)]
            copies.append((source.at[rows, pl.ds(0, 384)], target))
    copies = [
        pltpu.make_async_copy(source, target, sems.at[i])
        for i, (source, target) in enumerate(copies)
    ]
    for copy in copies:
        copy.start()
    for i in range(4):
        copies[i].wait()
        rows = pl.ds(128 * i, 128)
        normed_ref[rows, :] = layer_norm(tokens_ref[rows, :].astype(F32)).astype(BF16)
    for copy in copies[4:]:
        copy.wait()
    sends = []
    for i in range(4):
        rows = pl.ds(128 * i, 128)
        both = dot(normed_ref[rows, :], weights_ref[...])
        kv = jnp.concatenate([both[:, :HALF], both[:, 384 : 384 + HALF]], axis=1).astype(BF16)
        kv_ref[rows, :] = kv
        sends.append(pltpu.make_async_copy(kv_ref.at[rows], send_ref.at[rows], sems.at[8 + i]))
        sends[-1].start()
    for send in sends:
        send.wait()


def first_project(tokens, w_key, w_value):
    return pl.pallas_call(
        first_kernel,
        in_specs=[pl.BlockSpec(memory_space=pltpu.HBM)] * 3,
        out_specs=[pl.BlockSpec(memory_space=pltpu.VMEM), pl.BlockSpec(memory_space=pl.ANY)],
        out_shape=(kept(512, 1280), shape(512, 640)),
        scratch_shapes=[
            pltpu.VMEM((512, 1280), BF16),
            pltpu.VMEM((1280, 768), BF16),
            pltpu.VMEM((512, 640), BF16),
            pltpu.SemaphoreType.DMA((12,)),
        ],
        compiler_params=params(),
        cost_estimate=cost(2 * 512 * 1280 * 768, 6 * MIB),
        name="norm_kv_first",
    )(tokens, w_key, w_value)


def second_kernel(
    normed_ref, w_key_ref, w_value_ref, w_query_ref, kv_ref, q0_ref, q1_ref, send_ref, sems
):
    normed = normed_ref[...]
    keys = dot(normed, w_key_ref[:, 256:])
    values = dot(normed, w_value_ref[:, 256:])
    kv_ref[...] = jnp.concatenate([keys[:, 64:], values[:, 64:]], axis=1).astype(BF16)
    sends = (
        pltpu.make_async_copy(kv_ref, send_ref.at[pl.ds(0, 512)], sems.at[0]),
        pltpu.make_async_copy(kv_ref.at[pl.ds(0, 16)], send_ref.at[pl.ds(512, 16)], sems.at[1]),
    )
    for send in sends:
        send.start()
    query = dot(normed, w_query_ref[...])
    blank = jnp.zeros((512, 64), F32)
    q0_ref[...] = jnp.concatenate([query[:, :HALF], blank], axis=1).astype(BF16)
    q1_ref[...] = jnp.concatenate([query[:, HALF:], blank], axis=1).astype(BF16)
    for send in sends:
        send.wait()


def second_project(normed, w_key, w_value, w_query):
    return pl.pallas_call(
        second_kernel,
        out_specs=[pl.BlockSpec(memory_space=pltpu.VMEM)] * 3 + [pl.BlockSpec(memory_space=pl.ANY)],
        out_shape=(kept(512, 640), kept(512, 384), kept(512, 384), shape(528, 640)),
        scratch_shapes=[pltpu.SemaphoreType.DMA((2,))],
        compiler_params=params(),
        cost_estimate=cost(1000, 1000),
        name="kv_second_query",
    )(normed, w_key, w_value, w_query)


def masked_query(q_ref, head):
    key_at = 0 if head < 3 else 128
    low = HEAD * head - key_at
    return q_ref[:, key_at : key_at + 256] * lanes(256, low, low + HEAD).astype(F32).astype(BF16)


def wide(value, times):
    return jnp.concatenate([value] * times, axis=1)


def attend(q_ref, sources, head, floor=None):
    key_at = 0 if head < 3 else 128
    value_at = 256 if head < 2 else 384
    query = masked_query(q_ref, head)
    scores = [dot_t(query, kv[:512, key_at : key_at + 256]) for kv in sources]
    top = jnp.max(functools.reduce(jnp.maximum, scores), axis=1, keepdims=True)
    if floor is not None:
        top = jnp.maximum(jnp.broadcast_to(top, floor.shape), floor)
    shift = top if floor is None else wide(top, 4)
    probs = [jnp.exp2((part - shift) * SCALE) for part in scores]
    total = jnp.sum(functools.reduce(jnp.add, probs), axis=1, keepdims=True)
    weighed = sum(
        dot(part.astype(BF16), kv[:512, value_at : value_at + 256])
        for part, kv in zip(probs, sources)
    )
    return top, total, weighed


def side_by_side(mixed):
    low = jnp.where(
        lanes(256, 144, 256), mixed[1], jnp.where(lanes(256, 64, 144), mixed[0], 0.0)
    )
    high = jnp.where(lanes(256, 176, 256), mixed[3], mixed[2])
    middle = jnp.where(lanes(128, 0, 96), low[:, 128:], high[:, :128])
    return jnp.concatenate([low[:, :128], middle, high[:, 128:]], axis=1)


def attention_kernel(q_ref, kv0_ref, kv1_ref, kv2_ref, kv3_ref, after_ref, out_ref, token_ref):
    token_ref[...] = after_ref[...]
    sources = (kv0_ref, kv1_ref, kv2_ref, kv3_ref)
    mixed = []
    for head in range(4):
        _, total, weighed = attend(q_ref, sources, head)
        mixed.append(weighed / total)
    out_ref[...] = side_by_side(mixed).astype(BF16)


def attention(query, sources, after):
    return pl.pallas_call(
        attention_kernel,
        in_specs=[pl.BlockSpec(memory_space=pltpu.VMEM)] * 6,
        out_shape=(kept(512, 384), TOKEN),
        compiler_params=params(),
        cost_estimate=cost(1000, 1000),
        name="attention_four_heads",
    )(query, *sources, after)


def near_kernel(q_ref, kv0_ref, kv1_ref, owner_ref, mixed_ref, stats_ref, pick_ref, token_ref):
    token_ref[...] = jnp.zeros((8, 128), F32)
    block = lax.broadcasted_iota(jnp.int32, (128, 512), 0)
    source = lax.broadcasted_iota(jnp.int32, (128, 512), 1)
    spread = (source // 4 == block).astype(F32).astype(BF16)
    owner = jnp.broadcast_to(owner_ref[...].astype(F32), (8, 128)).astype(BF16)
    owner = dot(owner, spread)[:1, :].astype(jnp.int32)
    row = lax.broadcasted_iota(jnp.int32, (512, 512), 0)
    place = (owner % 2 * 64 + owner // 2) * 4 + lax.broadcasted_iota(jnp.int32, (1, 512), 1) % 4
    pick_ref[...] = (row == place).astype(F32).astype(BF16)
    mixed = []
    for head in range(4):
        top, total, weighed = attend(q_ref, (kv0_ref, kv1_ref), head)
        mixed.append(weighed)
        stats_ref[head] = jnp.broadcast_to(top, (512, 128))
        stats_ref[4 + head] = jnp.broadcast_to(total, (512, 128))
    mixed_ref[...] = side_by_side(mixed)


def near_attention(query, sources, owner_table):
    return pl.pallas_call(
        near_kernel,
        out_shape=(
            kept(512, 384, dtype=F32),
            kept(8, 512, 128, dtype=F32),
            kept(512, 512),
            TOKEN,
        ),
        compiler_params=params(),
        cost_estimate=cost(1000, 1000),
        name="attention_near_keys",
    )(query, *sources, owner_table)


def far_step(q_ref, kv_ref, near_ref, stats_ref, head, last):
    at = 0 if head < 2 else 128
    before = stats_ref[head]
    top, total, weighed = attend(q_ref, (kv_ref,), head, before)
    factor = jnp.exp2((before - top) * SCALE)
    total = total + factor * stats_ref[4 + head]
    if last:
        share = 1.0 / total
        weighed = wide(share, 2) * weighed
        factor = factor * share
    return top, total, weighed + wide(factor, 2) * near_ref[:, at : at + 256]


def far_kernel(q_ref, kv_ref, near_ref, stats_ref, out_ref, new_stats_ref):
    mixed = []
    for head in range(4):
        top, total, weighed = far_step(q_ref, kv_ref, near_ref, stats_ref, head, False)
        new_stats_ref[head] = top
        new_stats_ref[4 + head] = total
        mixed.append(weighed)
    out_ref[...] = side_by_side(mixed)


def far_attention(query, source, near, stats):
    return pl.pallas_call(
        far_kernel,
        out_shape=(kept(512, 384, dtype=F32), kept(8, 512, 128, dtype=F32)),
        compiler_params=params(),
        cost_estimate=cost(2 * 512 * 512 * 512 * 4, 2 * MIB, 4 * 512 * 512),
        name="attention_far_keys",
    )(query, source, near, stats)


def first_out_kernel(tokens_ref, att_ref, w_out_ref, after_ref, out_ref, token_ref):
    token_ref[...] = after_ref[...]
    top = jnp.concatenate([jnp.zeros((64, 1280), BF16), w_out_ref[:64, :]], axis=0)
    added = dot(att_ref[:, 128:], w_out_ref[64:HALF, :]) + dot(att_ref[:, :128], top)
    out_ref[...] = tokens_ref[...].astype(F32) + added


def first_out(tokens, att, w_out, after):
    return pl.pallas_call(
        first_out_kernel,
        out_shape=(kept(512, 1280, dtype=F32), TOKEN),
        compiler_params=params(),
        cost_estimate=cost(1000, 1000),
        name="first_heads_out",
    )(tokens, att, w_out, after)


def target_kernel(
    q_ref, kv_ref, near_ref, stats_ref, pick_ref, base_ref, w_out_ref, w_neck_ref, out_ref
):
    mixed = [far_step(q_ref, kv_ref, near_ref, stats_ref, head, True)[2] for head in range(4)]
    attended = side_by_side(mixed).astype(BF16)
    block_out = (base_ref[...] + dot(attended, w_out_ref[256:, :])).astype(BF16)
    target = layer_norm(dot(block_out, w_neck_ref[...])).astype(BF16)
    out_ref[...] = dot(pick_ref[...], target).reshape(128, 4, 256).astype(BF16)


def make_target(query, source, near, stats, pick, base, w_out, w_neck):
    return pl.pallas_call(
        target_kernel,
        out_shape=shape(128, 4, 256),
        compiler_params=params(),
        cost_estimate=cost(2 * 512 * 1280 * 1024, 6 * MIB),
        name="last_keys_target",
    )(query, source, near, stats, pick, base, w_out, w_neck)


def forward_kernel(
    core_ref, rows_ref, w_expand_ref, w_project_ref, pred_ref, slope_ref, act_t_ref, rows_t_ref, token_ref
):
    token_ref[...] = jnp.zeros((8, 128), F32)
    step = pl.program_id(0)
    core = core_ref[0]
    rows = rows_ref[...]

    @pl.when(step == 0)
    def _():
        out_row = lax.broadcasted_iota(jnp.int32, (512, 512), 0)
        column = lax.broadcasted_iota(jnp.int32, (512, 512), 1)
        member = jnp.where(out_row < 256, core, 1 - core)
        wanted = (out_row % 256) // 4 * 8 + member * 4 + out_row % 4
        pick = (column == wanted).astype(F32).astype(BF16)
        rows_t_ref[...] = dot_t(pick, rows).astype(BF16)

    pre = dot(rows, w_expand_ref[...])
    square = pre * pre
    bend = jnp.tanh(GELU_A * pre * (1.0 + GELU_B * square))
    gate = 0.5 * (1.0 + bend)
    act = (pre * gate).astype(BF16)
    slope_ref[...] = gate + (0.5 * GELU_A) * pre * (1.0 - bend * bend) * (
        1.0 + (3.0 * GELU_B) * square
    )
    act_t = act.T
    for group in range(32):
        half = jnp.where(core == group % 2, 0, 1024)
        start = pl.multiple_of(half + (step * 16 + group // 2) * 16, 16)
        act_t_ref[pl.ds(start, 16), :] = act_t[group * 16 : group * 16 + 16, :]
    part = dot(act, w_project_ref[...])

    @pl.when(step == 0)
    def _():
        pred_ref[...] = part

    @pl.when(step > 0)
    def _():
        pred_ref[...] += part


def student_forward(core, rows, w_expand, w_project):
    whole = lambda i: (0, 0)
    return pl.pallas_call(
        forward_kernel,
        grid=(4,),
        in_specs=[
            pl.BlockSpec(memory_space=pltpu.SMEM),
            pl.BlockSpec((512, 512), whole),
            pl.BlockSpec((512, 512), lambda i: (0, i)),
            pl.BlockSpec((512, 256), lambda i: (i, 0)),
        ],
        out_specs=[
            pl.BlockSpec((512, 256), whole),
            pl.BlockSpec((512, 512), lambda i: (0, i)),
            pl.BlockSpec((2048, 512), whole),
            pl.BlockSpec((512, 512), whole),
            pl.BlockSpec((8, 128), whole),
        ],
        out_shape=(
            kept(512, 256, dtype=F32),
            kept(512, 2048, dtype=F32),
            kept(2048, 512),
            kept(512, 512),
            TOKEN,
        ),
        compiler_params=params(),
        cost_estimate=cost(1000, 1000),
        name="student_forward",
    )(core, rows, w_expand, w_project)


def error_kernel(pred_ref, moved_ref, act_t_ref, error_ref, d_pred_ref, project_ref):
    moved = moved_ref[...].astype(F32)
    moved = jnp.concatenate([moved[:64], moved[64:]], axis=1).reshape(512, 256)
    error = pred_ref[...] - moved
    error_ref[...] = error.astype(BF16)
    d_pred = (error * (1.0 / 512.0)).astype(BF16)
    d_pred_ref[...] = d_pred
    project_ref[...] = dot(act_t_ref[1024:, :], d_pred).astype(BF16)


def student_error(pred, moved, act_t):
    return pl.pallas_call(
        error_kernel,
        out_shape=(shape(512, 256), kept(512, 256), shape(1024, 256)),
        compiler_params=params(),
        cost_estimate=cost(1000, 1000),
        name="student_error",
    )(pred, moved, act_t)


def backward_kernel(side, d_pred_ref, slope_ref, w_project_ref, rows_t_ref, d_pre_ref, expand_ref):
    for i in range(2):
        part = slice(1024 * side + 512 * i, 1024 * side + 512 * i + 512)
        out = slice(512 * i, 512 * i + 512)
        d_act = dot_t(d_pred_ref[...], w_project_ref[part, :])
        d_pre = (slope_ref[:, part] * d_act).astype(BF16)
        d_pre_ref[:, out] = d_pre
        expand_ref[:, out] = dot(rows_t_ref[256:, :], d_pre).astype(BF16)


def student_backward(side, d_pred, slope, w_project, rows_t):
    return pl.pallas_call(
        functools.partial(backward_kernel, side),
        out_shape=(kept(512, 1024), shape(256, 1024)),
        compiler_params=params(),
        cost_estimate=cost(1000, 1000),
        name="student_backward",
    )(d_pred, slope, w_project, rows_t)


def own_kernel(
    d_pred_ref,
    d_pre0_ref,
    d_pre1_ref,
    act_t_ref,
    rows_t_ref,
    project_in_ref,
    expand0_in_ref,
    project_ref,
    expand_ref,
):
    project = dot(act_t_ref[:1024, :], d_pred_ref[...])
    project_ref[...] = (project + project_in_ref[...].astype(F32)).astype(BF16)
    for side, d_pre_ref in enumerate((d_pre0_ref, d_pre1_ref)):
        for i in range(2):
            part = slice(512 * i, 512 * i + 512)
            expand = dot(rows_t_ref[:256, :], d_pre_ref[:, part])
            if side == 0:
                expand = expand + expand0_in_ref[:, part].astype(F32)
            expand_ref[:, 1024 * side + 512 * i : 1024 * side + 512 * i + 512] = expand


def own_half(d_pred, d_pre0, d_pre1, act_t, rows_t, project_in, expand0_in):
    return pl.pallas_call(
        own_kernel,
        out_shape=(kept(1024, 256), kept(256, 2048, dtype=F32)),
        compiler_params=params(),
        cost_estimate=cost(10**11, 6 * MIB),
        name="own_half_gradients",
    )(d_pred, d_pre0, d_pre1, act_t, rows_t, project_in, expand0_in)


def pack_kernel(project_ref, expand_ref, expand1_in_ref, out_ref):
    row = lax.broadcasted_iota(jnp.int32, (256, 256), 0)
    column = lax.broadcasted_iota(jnp.int32, (256, 256), 1)
    wanted = row % 32 // 4 * 32 + row // 32 * 4 + row % 4
    order = (column == wanted).astype(F32).astype(BF16)
    for block in range(8):
        part = slice(32 * block, 32 * block + 32)
        columns = []
        for j in range(8):
            expand = expand_ref[part, 256 * j : 256 * j + 256]
            if j >= 4:
                arrived = expand1_in_ref[part, 256 * (j - 4) : 256 * (j - 4) + 256]
                expand = expand + arrived.astype(F32)
            columns.append(expand.astype(BF16))
        sorted_rows = dot(order, jnp.concatenate(columns, axis=0)).astype(BF16)
        for i in range(8):
            chip = 8 * block + i
            place = chip % 2 * 32 + chip // 8 % 2 * 16 + chip // 16 * 4 + chip // 2 % 4
            out_ref[place, :16, :] = project_ref[16 * chip : 16 * chip + 16, :]
            out_ref[place, 16:, :] = sorted_rows[32 * i : 32 * i + 32, :]


def pack(project, expand, expand1_in):
    return pl.pallas_call(
        pack_kernel,
        out_shape=shape(64, 48, 256),
        compiler_params=params(),
        cost_estimate=cost(2 * 256 * 256 * 256 * 8, 6 * MIB),
        name="pack_gradients",
    )(project, expand, expand1_in)


def finish_kernel(parts_ref, expand_ref, project_ref):
    sums = [jnp.sum(parts_ref[16 * i : 16 * i + 16].astype(F32), axis=0) for i in range(4)]
    total = (sums[0] + sums[1]) + (sums[2] + sums[3])
    project_ref[...] = total[:16, :]
    for j in range(8):
        expand_ref[:, 256 * j : 256 * j + 256] = total[16 + 4 * j : 20 + 4 * j, :]


def finish(parts):
    return pl.pallas_call(
        finish_kernel,
        out_shape=(shape(4, 2048, dtype=F32), shape(16, 256, dtype=F32)),
        compiler_params=params(),
        cost_estimate=cost(64 * 48 * 256, 2 * MIB),
        name="sum_gradients",
    )(parts)


def gate_kernel(value_ref, after_ref, out_ref):
    del value_ref, after_ref, out_ref


def gate(value, after):
    return pl.pallas_call(
        gate_kernel,
        in_specs=[pl.BlockSpec(memory_space=pl.ANY)] * 2,
        out_specs=pl.BlockSpec(memory_space=pl.ANY),
        out_shape=jax.ShapeDtypeStruct(value.shape, value.dtype),
        input_output_aliases={0: 0},
        compiler_params=params(1),
        cost_estimate=cost(10, 10),
        name="gate",
    )(value, after)


def swap(value, axis):
    return lax.ppermute(value, axis, [(0, 1), (1, 0)])


def per_device(
    tokens, w_query, w_key, w_value, w_out, w_neck, owner_table, student_in, w_expand, w_project
):
    core = lax.axis_index("c").astype(jnp.int32).reshape(1)
    normed, kv_first = first_project(in_hbm(tokens), in_hbm(w_key), in_hbm(w_value))
    far_first = swap(kv_first, "yh")
    near_first = swap(kv_first, "c")
    kv_second, query_first, query_second, kv_send = second_project(
        normed, in_hbm(w_key), in_hbm(w_value), in_hbm(w_query)
    )
    far_second = swap(kv_send, "yh")
    near_second = swap(kv_second, "c")
    pred, slope, act_t, rows_t, token = student_forward(
        core, in_hbm(student_in), in_hbm(w_expand), in_hbm(w_project)
    )
    far_first = gate(far_first, token)
    near, stats, pick, token = near_attention(
        query_second, (kv_second, near_second), owner_table
    )
    att_first, token = attention(
        query_first, (kv_first, near_first, far_first, swap(far_first, "c")), token
    )
    base, token = first_out(tokens, att_first, w_out, token)
    far_second = gate(far_second, token)
    last_second = swap(far_second, "c")
    near, stats = far_attention(query_second, far_second, near, stats)
    target = make_target(query_second, last_second, near, stats, pick, base, w_out, w_neck)
    moved = lax.all_to_all(target, BY_CORE, split_axis=0, concat_axis=0, tiled=True)
    error, d_pred, project_out = student_error(pred, moved, act_t)
    project_in = swap(project_out, "c")
    d_pre0, expand0_out = student_backward(0, d_pred, slope, w_project, rows_t)
    expand0_in = swap(expand0_out, "c")
    d_pre1, expand1_out = student_backward(1, d_pred, slope, w_project, rows_t)
    expand1_in = swap(expand1_out, "c")
    project, expand = own_half(
        d_pred, d_pre0, d_pre1, act_t, rows_t, project_in, expand0_in
    )
    packed = pack(project, expand, expand1_in)
    parts = lax.all_to_all(packed, CHIPS, split_axis=0, concat_axis=0, tiled=True)
    grad_expand, grad_project = finish(parts)
    return (error, grad_expand, grad_project)


def solution(mesh):
    fine = Mesh(mesh.devices.reshape(4, 2, 4, 2, 2), AXES)
    rows = P(AXES, None)
    return jax.shard_map(
        per_device,
        mesh=fine,
        in_specs=(rows, P(), P(), P(), P(), P(), rows, rows, P(), P()),
        out_specs=(rows, rows, rows),
        check_vma=False,
    )
```
